32 devices in a mesh: dp: 2 (over y), seq: 16 (over z, x, core).
Axes of the slice: x: 2, y: 2, z: 4, core: 2. Of those that a mesh axis runs over, the one named last changes fastest.
Arguments:
- tokens: bfloat16 [4096, 2048], P(('dp', 'seq')), may hold values from -6 to 6
- gain_attn: bfloat16 [2048], P(('dp', 'seq')), may hold values from 0.5 to 1.5
- w_query: bfloat16 [2048, 2048], P(('dp', 'seq')), may hold values from -0.125 to 0.125
- w_key: bfloat16 [2048, 256], P(('dp', 'seq')), may hold values from -0.125 to 0.125
- w_value: bfloat16 [2048, 256], P(('dp', 'seq')), may hold values from -0.125 to 0.125
- w_out: bfloat16 [2048, 2048], P(('dp', 'seq')), may hold values from -1 to 1
- gain_mlp: bfloat16 [2048], P(('dp', 'seq')), may hold values from 0.5 to 1.5
- w_gate: bfloat16 [2048, 5632], P(None, ('dp', 'seq')), may hold values from -0.125 to 0.125
- w_up: bfloat16 [2048, 5632], P(None, ('dp', 'seq')), may hold values from -0.125 to 0.125
- w_down: bfloat16 [5632, 2048], P(('dp', 'seq')), may hold values from -0.078125 to 0.078125
- doc_ids: int32 [2, 2048], P('dp'), may hold values from 0 to 2, never falling along the last dimension, each value on 1 to 2000 neighbouring positions
- cotangent: bfloat16 [4096, 2048], P(('dp', 'seq')), may hold values from -6 to 6
Outputs:
- block_out: bfloat16 [4096, 2048], P(('dp', 'seq'))
- input_grad: float32 [4096, 2048], P(('dp', 'seq'))
- grad_gain_attn: float32 [2048], P(('dp', 'seq'))
- grad_w_query: float32 [2048, 2048], P(('dp', 'seq'))
- grad_w_key: float32 [2048, 256], P(('dp', 'seq'))
- grad_w_value: float32 [2048, 256], P(('dp', 'seq'))
- grad_w_out: float32 [2048, 2048], P(('dp', 'seq'))
- grad_gain_mlp: float32 [2048], P(('dp', 'seq'))
- grad_w_gate: float32 [2048, 5632], P(None, ('dp', 'seq'))
- grad_w_up: float32 [2048, 5632], P(None, ('dp', 'seq'))
- grad_w_down: float32 [5632, 2048], P(('dp', 'seq'))
The draws below stay inside these ranges and needn't reach their ends.
Inputs may be any that keep to these rules, and one draw needn't show every extreme that they name: `doc_ids`: within each sequence the ids never fall, every id covers at most 2000 consecutive tokens, and some document has exactly 2000 tokens.
All inputs are finite; a program needn't handle non-finite values.
Results may differ from the reference program's by a relative error of at most 0.019.
Values may be sent and summed in bfloat16 or wider, within the bound.
A program may use at most 384 MiB of HBM per device.

```python
import math
import jax
import jax.numpy as jnp
import numpy as np
from jax import lax

D = 2048
FF = 5632
HEADS = 32
KV_HEADS = 4
HEAD_DIM = 64
DOC_MOST = 2000
SEQLEN = 2048
SEQS = 2
TOKENS = 4096
DOCS = 3


def block_scale(stream_key, shape, pieces, least, largest):
    factor_of = 1.0
    for dim, shards_of in pieces:
        heights = jax.random.uniform(jax.random.fold_in(jax.random.fold_in(stream_key, 6), dim), (shards_of,), jnp.float32, least / len(pieces), largest / len(pieces))
        factor_of = factor_of * jnp.repeat(jnp.exp(heights), shape[dim] // shards_of).reshape((-1,) + (1,) * (len(shape) - 1 - dim))
    return factor_of


def length_profile(number_of, total, bound, lean):
    portions = [(1 << 20) // math.isqrt(grade ** lean) + 1 for grade in range(2, number_of + 1)]
    rest, given = total - bound - (number_of - 1), [1] * (number_of - 1)
    while rest > 0:
        free = [i for i in range(number_of - 1) if given[i] < bound]
        pool, remaining = sum([portions[i] for i in free]), rest
        for i in free:
            addition = min(bound - given[i], max(1, remaining * portions[i] // pool), rest)
            given[i] = given[i] + addition
            rest = rest - addition
    return np.array([bound] + given)


def uneven(own_key, count, total, reach, skew):
    if count == 2:
        one = jax.random.randint(own_key, (), max(1, total - reach), min(reach, total - 1) + 1)
        return jnp.stack([one, total - one])
    lengths = jnp.asarray(length_profile(count, total, reach, skew), jnp.int32)
    twos = (count - 1) // 2
    donor, sink = lengths[1:1 + 2 * twos:2], lengths[2:2 + 2 * twos:2]
    slack = jnp.minimum(donor - 1, reach - sink)
    moved = jax.random.randint(jax.random.fold_in(own_key, 1), (twos,), 0, 1 << 20) % (slack + 1)
    lengths = lengths.at[1:1 + 2 * twos:2].set(donor - moved).at[2:2 + 2 * twos:2].set(sink + moved)
    return lengths[jax.random.permutation(jax.random.fold_in(own_key, 2), count)]


def gaussian(stream_key, dims, spread, most, shards=(), held_as=jnp.bfloat16):
    loudness = block_scale(stream_key, dims, shards, -0.22, 0.18) if shards else 1.0
    entries = jax.random.normal(stream_key, dims, jnp.float32) * spread * loudness
    return jnp.minimum(jnp.maximum(entries, -most), most).astype(held_as)


def setup_inputs(seed: int = 0) -> dict:
    streams_of = jax.random.split(jax.random.key(seed), 13)
    return {
        "tokens": gaussian(streams_of[0], (TOKENS, D), 1.0, 6.0, ((0, 32),)),
        "gain_attn": jnp.clip(1.0 + 0.1 * jax.random.normal(streams_of[1], (D,), jnp.float32), 0.5, 1.5).astype(jnp.bfloat16),
        "w_query": gaussian(streams_of[2], (D, HEADS * HEAD_DIM), D ** -0.5, 0.125, ((0, 32),)),
        "w_key": gaussian(streams_of[3], (D, KV_HEADS * HEAD_DIM), D ** -0.5, 0.125, ((0, 32),)),
        "w_value": gaussian(streams_of[4], (D, KV_HEADS * HEAD_DIM), D ** -0.5, 0.125, ((0, 32),)),
        "w_out": gaussian(streams_of[5], (HEADS * HEAD_DIM, D), (max(HEADS * HEAD_DIM // 64, 1)) ** -0.5, 1.0, ((0, 32),)),
        "gain_mlp": jnp.clip(1.0 + 0.1 * jax.random.normal(streams_of[6], (D,), jnp.float32), 0.5, 1.5).astype(jnp.bfloat16),
        "w_gate": gaussian(streams_of[7], (D, FF), D ** -0.5, 0.125, ((1, 32),)),
        "w_up": gaussian(streams_of[8], (D, FF), D ** -0.5, 0.125, ((1, 32),)),
        "w_down": gaussian(streams_of[9], (FF, D), FF ** -0.5, 0.078125, ((0, 32),)),
        "doc_ids": jax.vmap(lambda own: jnp.searchsorted(jnp.cumsum(uneven(own, DOCS, SEQLEN, DOC_MOST, 2)), jnp.arange(SEQLEN), side="right"))(jax.random.split(streams_of[10], SEQS)).reshape((SEQS, SEQLEN)).astype(jnp.int32),
        "cotangent": gaussian(streams_of[11], (TOKENS, D), 1.0, 6.0, ((0, 32),)),
    }


NORM_EPS = 1e-05
MASKED = -1e+30

@jax.custom_vjp
def low(v):
    return lax.optimization_barrier(v.astype(jnp.bfloat16)).astype(jnp.float32)

@jax.custom_vjp
def low_back(v):
    return v

def low_keep(v):
    return (low(v), None)

def low_pass(kept, grad):
    return (grad,)

def back_keep(v):
    return (v, None)

def back_low(kept, grad):
    return (low(grad),)
low.defvjp(low_keep, low_pass)
low_back.defvjp(back_keep, back_low)

def exact_dot(left, right):
    return jnp.dot(left, right, precision=lax.Precision.HIGHEST)

def angles(positions):
    half_dim = HEAD_DIM // 2
    frequency = 10000.0 ** (-jnp.arange(half_dim, dtype=jnp.float32) / half_dim)
    phases = positions.astype(jnp.float32)[:, None] * frequency[None, :]
    return (jnp.cos(phases), jnp.sin(phases))

def rotate(field, cosines, sine_vals):
    half_dim = field.shape[-1] // 2
    front_half = field[..., :half_dim]
    back_half = field[..., half_dim:]
    return jnp.concatenate([front_half * cosines - back_half * sine_vals, back_half * cosines + front_half * sine_vals], axis=-1)

def rms_norm(field, gain_vec):
    inv_rms = lax.rsqrt(lax.optimization_barrier(jnp.mean(field * field, axis=-1, keepdims=True)) + NORM_EPS)
    return field * inv_rms * gain_vec

def sequence(inputs, seq_ids, params):
    gain_attn, w_query, w_key, w_value, w_out, gain_mlp, w_gate, w_up, w_down = params
    length = inputs.shape[0]
    group_size = HEADS // KV_HEADS
    score_scale = HEAD_DIM ** (-0.5)
    token_index = jnp.arange(length, dtype=jnp.int32)
    doc_starts = lax.optimization_barrier(jnp.sum((seq_ids[None, :] < seq_ids[:, None]).astype(jnp.int32), axis=1))
    cosines, sine_vals = angles(token_index - doc_starts)
    cos_heads = cosines[:, None, :]
    sin_heads = sine_vals[:, None, :]
    normed = low(rms_norm(inputs, gain_attn))
    query_raw = low_back(exact_dot(normed, w_query)).reshape(length, HEADS, HEAD_DIM)
    key_raw = low_back(exact_dot(normed, w_key)).reshape(length, KV_HEADS, HEAD_DIM)
    values = low(low_back(exact_dot(normed, w_value))).reshape(length, KV_HEADS, HEAD_DIM)
    queries = low(rotate(query_raw, cos_heads, sin_heads)).reshape(length, KV_HEADS, group_size, HEAD_DIM)
    key_rot = low(rotate(key_raw, cos_heads, sin_heads))
    block_rows = min(512, length)
    blocks = length // block_rows

    def attend(block_items):
        query_block, block_ids, block_start = block_items
        query_pos = block_start + jnp.arange(block_rows, dtype=jnp.int32)
        allowed = (seq_ids[None, :] == block_ids[:, None]) & (token_index[None, :] <= query_pos[:, None])
        raw_scores = jnp.einsum('tkgd,skd->tkgs', query_block, key_rot, precision=lax.Precision.HIGHEST) * score_scale
        scores = jnp.where(allowed[:, None, None, :], low_back(raw_scores), MASKED)
        prob_rows = jax.nn.softmax(scores, axis=-1)
        return jnp.einsum('tkgs,skd->tkgd', low(prob_rows), values, precision=lax.Precision.HIGHEST)
    block_starts = jnp.arange(blocks, dtype=jnp.int32) * block_rows
    head_outs = lax.map(jax.checkpoint(attend), (queries.reshape(blocks, block_rows, KV_HEADS, group_size, HEAD_DIM), seq_ids.reshape(blocks, block_rows), block_starts))
    attn_in = low(low_back(head_outs.reshape(length, HEADS * HEAD_DIM)))
    attn_out = low_back(exact_dot(attn_in, w_out))
    middle = inputs + attn_out
    normed_mlp = low(rms_norm(middle, gain_mlp))
    gate_pre = low_back(exact_dot(normed_mlp, w_gate))
    up_pre = low_back(exact_dot(normed_mlp, w_up))
    hidden = low(jax.nn.silu(gate_pre) * up_pre)
    return middle + low_back(exact_dot(hidden, w_down))

def reference(tokens, gain_attn, w_query, w_key, w_value, w_out, gain_mlp, w_gate, w_up, w_down, doc_ids, cotangent):
    params = tuple((weight.astype(jnp.float32) for weight in (gain_attn, w_query, w_key, w_value, w_out, gain_mlp, w_gate, w_up, w_down)))
    inputs = tokens.astype(jnp.float32).reshape(SEQS, SEQLEN, D)

    def forward(layer_in, layer_params):
        return lax.map(lambda seq_item: sequence(seq_item[0], seq_item[1], layer_params), (layer_in, doc_ids))
    result, pullback = jax.vjp(forward, inputs, params)
    input_grad, weight_grads = pullback(cotangent.astype(jnp.float32).reshape(SEQS, SEQLEN, D))
    block_out = result.reshape(TOKENS, D).astype(jnp.bfloat16)
    return (block_out, input_grad.reshape(TOKENS, D), weight_grads[0], weight_grads[1], weight_grads[2], weight_grads[3], weight_grads[4], weight_grads[5], weight_grads[6], weight_grads[7], weight_grads[8])
```

```python
import jax
import jax.numpy as jnp
from jax import lax
from jax.experimental import pallas as pl
from jax.experimental.pallas import tpu as pltpu
from jax.sharding import Mesh, PartitionSpec as P

HEADS = 32
KV_HEADS = 4
HEAD_DIM = 64
GROUP = HEADS // KV_HEADS
NORM_EPS = 1e-05
MASKED = -1e30
AXES = ("dh", "dl", "zh", "zl", "x", "c")
T = ("x", "c")
Z = ("zh", "zl")
DP = ("dh", "dl")
CUBE = ("dl", "zl", "x", "c")
REST = ("dh", "zh")
BF = jnp.bfloat16
F32 = jnp.float32


def nn(a, b):
    return jnp.dot(a, b, preferred_element_type=F32)


def nt(a, b):
    return lax.dot_general(a, b, (((1,), (1,)), ((), ())), preferred_element_type=F32)


def tn(a, b):
    return lax.dot_general(a, b, (((0,), (0,)), ((), ())), preferred_element_type=F32)


def rotate(v, cos, sin, sign):
    h = v.shape[-1] // 2
    a, b = v[..., :h], v[..., h:]
    s = sin * sign
    return jnp.concatenate([a * cos - b * s, b * cos + a * s], axis=-1)


PARTS = ((0, 768), (768, 640), (1408, 640))
MESH = pl.DeviceIdType.MESH


def place():
    return {a: lax.axis_index(a) for a in AXES}


def other(at, *flip):
    return tuple(1 - at[a] if a in flip else at[a] for a in AXES)


def greet(at, partners):
    barrier = pltpu.get_barrier_semaphore()
    for flip in partners:
        pl.semaphore_signal(barrier, inc=1, device_id=other(at, *flip), device_id_type=MESH)
    pl.semaphore_wait(barrier, len(partners))


CDIMS = ("x", "zl", "dl")
MASKS = ((), ("x",), ("zl",), ("dl",), ("x", "zl"), ("zl", "dl"), ("dl", "x"), ("x", "zl", "dl"))


def cube_index(at, mask):
    return tuple(1 - at[a] if a in mask else at[a] for a in ("dl", "zl", "x"))


def order_of(p):
    return tuple(CDIMS[(p + s) % 3] for s in range(3))


class Gather:
    def __init__(self, at, buf, ssem, rsem, csend, crecv):
        self.at, self.buf, self.ssem, self.rsem, self.csend, self.crecv = at, buf, ssem, rsem, csend, crecv
        self.rows = buf.shape[3] // 2
        self.open = []

    def block(self, mask, core, p=None):
        i = cube_index(self.at, mask)
        r = pl.ds(pl.multiple_of(core * self.rows, self.rows), self.rows)
        if p is None:
            return self.buf.at[i[0], i[1], i[2], r, :]
        lo, w = PARTS[p]
        return self.buf.at[i[0], i[1], i[2], r, lo:lo + w]

    def send(self, p, mask, dim):
        ref = self.block(mask, self.at["c"], p)
        k = MASKS.index(tuple(a for a in mask_sorted(mask + (dim,))))
        cp = pltpu.make_async_remote_copy(ref, ref, self.ssem.at[p, k], self.rsem.at[p, k],
                                          device_id=other(self.at, dim), device_id_type=MESH)
        cp.start()
        self.open.append(cp)

    def arrived(self, p, mask):
        k = MASKS.index(mask)
        ref = self.block(mask, self.at["c"], p)
        pltpu.make_async_remote_copy(ref, ref, self.ssem.at[p, k], self.rsem.at[p, k],
                                     device_id=other(self.at, "x"), device_id_type=MESH).wait_recv()

    def pass_on(self, mask):
        k = MASKS.index(mask)
        ref = self.block(mask, self.at["c"])
        cp = pltpu.make_async_remote_copy(ref, ref, self.csend.at[k], self.crecv.at[k],
                                          device_id=other(self.at, "c"), device_id_type=MESH)
        cp.start()
        self.open.append(cp)

    def sibling_arrived(self, mask):
        k = MASKS.index(mask)
        ref = self.block(mask, 1 - self.at["c"])
        pltpu.make_async_remote_copy(ref, ref, self.csend.at[k], self.crecv.at[k],
                                     device_id=other(self.at, "c"), device_id_type=MESH).wait_recv()

    def first(self):
        for p in range(3):
            self.send(p, (), order_of(p)[0])
        self.pass_on(())

    def second(self):
        for p in range(3):
            a, b, _ = order_of(p)
            self.send(p, (), b)
        for p in range(3):
            a, b, _ = order_of(p)
            self.arrived(p, (a,))
            self.send(p, (a,), b)

    def third(self):
        for p in range(3):
            a, b, c = order_of(p)
            self.send(p, (), c)
        for p in range(3):
            a, b, c = order_of(p)
            self.send(p, (a,), c)
        for p in range(3):
            a, b, c = order_of(p)
            self.arrived(p, (b,))
            self.send(p, (b,), c)
        for p in range(3):
            a, b, c = order_of(p)
            self.arrived(p, mask_sorted((a, b)))
            self.send(p, mask_sorted((a, b)), c)

    def complete(self, mask):
        for p in range(3):
            if order_of(p)[2] in mask:
                self.arrived(p, mask)

    def close(self):
        for cp in self.open:
            cp.wait_send()


def mask_sorted(mask):
    for m in MASKS:
        if set(m) == set(mask):
            return m
    raise ValueError(mask)


class Scatter:
    def __init__(self, at, full, core_in, r0, r1, r2, ssem, rsem):
        self.at, self.full, self.core_in, self.r = at, full, core_in, (r0, r1, r2)
        self.ssem, self.rsem = ssem, rsem
        self.rows = full.shape[3] // 2
        self.open = []

    def own(self, core):
        return pl.ds(pl.multiple_of(core * self.rows, self.rows), self.rows)

    def core_copy(self, p):
        lo, w = PARTS[p]
        return pltpu.make_async_remote_copy(
            self.full.at[:, :, :, self.own(1 - self.at["c"]), lo:lo + w], self.core_in.at[:, :, :, :, lo:lo + w],
            self.ssem.at[p, 3], self.rsem.at[p, 3], device_id=other(self.at, "c"), device_id_type=MESH)

    def stage_copy(self, p, s):
        lo, w = PARTS[p]
        dims = order_of(p)
        ix = []
        for a in ("dl", "zl", "x"):
            if a == dims[s]:
                ix.append(1 - self.at[a])
            elif a in dims[:s]:
                ix.append(self.at[a])
            else:
                ix.append(slice(None))
        dst = self.r[s]
        dst = dst.at[(slice(None),) * (len(dst.shape) - 1) + (slice(lo, lo + w),)]
        return pltpu.make_async_remote_copy(
            self.full.at[ix[0], ix[1], ix[2], self.own(self.at["c"]), lo:lo + w], dst,
            self.ssem.at[p, s], self.rsem.at[p, s], device_id=other(self.at, dims[s]), device_id_type=MESH)

    def start(self, cp):
        cp.start()
        self.open.append(cp)

    def blocks(self, p, s):
        dims = order_of(p)
        rest = dims[s:]
        out = []
        for m in MASKS:
            if set(m) <= set(rest):
                out.append(m)
        if rest:
            out.sort(key=lambda m: 0 if rest[0] in m else 1)
        return out

    def add_core(self, p):
        lo, w = PARTS[p]
        cp = self.core_copy(p)
        cp.wait_recv()
        self.add_loop(p, 0, None)
        self.start(self.stage_copy(p, 0))
        self.add_loop(p, 0, None, tail=True)

    def add_loop(self, p, s, src, tail=False):
        lo, w = PARTS[p]
        dims = order_of(p)
        for m in self.blocks(p, s):
            first = s < 3 and dims[s] in m
            if first == tail:
                continue
            i = cube_index(self.at, m)
            ref = self.full.at[i[0], i[1], i[2], self.own(self.at["c"]), lo:lo + w]
            if src is None:
                val = self.core_in[i[0], i[1], i[2], :, lo:lo + w]
            else:
                ix = [j for a, j in zip(("dl", "zl", "x"), i) if a in dims[s:]]
                val = src[tuple(ix) + (slice(None), slice(lo, lo + w))]
            ref[...] = (ref[...].astype(F32) + val.astype(F32)).astype(BF)

    def step(self, p, s):
        self.stage_copy(p, s).wait_recv()
        self.add_loop(p, s + 1, self.r[s])
        if s < 2:
            self.start(self.stage_copy(p, s + 1))
            self.add_loop(p, s + 1, self.r[s], tail=True)

    def finish(self, p, out):
        lo, w = PARTS[p]
        self.stage_copy(p, 2).wait_recv()
        i = cube_index(self.at, ())
        ref = self.full.at[i[0], i[1], i[2], self.own(self.at["c"]), lo:lo + w]
        out[:, lo:lo + w] = (ref[...].astype(F32) + self.r[2][:, lo:lo + w].astype(F32)).astype(out.dtype)

    def close(self):
        for cp in self.open:
            cp.wait_send()


def mlp_kernel(n2_ref, cot_ref, wg_ref, wu_ref, wd_ref, down_out, dn2_out, gwd_out, gwg_out, gwu_out,
               rows, wgu, zb, dgu, fa, fb, core_in, a0, a1, a2, b0, b1, b2,
               lsem, gs, gr, gcs, gcr, sas, sar, sbs, sbr, credit):
    at = place()
    units = wd_ref.shape[0]
    brows = n2_ref.shape[0]
    copies = [pltpu.make_async_copy(wg_ref, wgu.at[:units, :], lsem.at[0]),
              pltpu.make_async_copy(wu_ref, wgu.at[units:, :], lsem.at[1])]
    for cp in copies:
        cp.start()
    greet(at, (("c",), ("x",), ("zl",), ("dl",)))
    g = Gather(at, rows, gs, gr, gcs, gcr)
    own = pl.ds(pl.multiple_of(at["c"] * brows, brows), brows)
    rows[at["dl"], at["zl"], at["x"], own, :] = n2_ref[...]
    g.first()
    for cp in copies:
        cp.wait()

    def units_of(mask):
        i = cube_index(at, mask)
        r = rows[i[0], i[1], i[2]]
        gu = nt(wgu[...], r)
        dz = nt(wd_ref[...], cot_ref[i[0], i[1], i[2]])
        gate, up = gu[:units], gu[units:]
        sg = jax.nn.sigmoid(gate)
        sl = gate * sg
        zb[i[0], i[1], i[2]] = (sl * up).astype(BF)
        dgu[i[0], i[1], i[2], :units, :] = (dz * up * (sg * (1.0 + gate * (1.0 - sg)))).astype(BF)
        dgu[i[0], i[1], i[2], units:, :] = (dz * sl).astype(BF)

    g.second()
    g.sibling_arrived(())
    units_of(())
    g.third()
    last = None
    for m in MASKS[1:]:
        g.complete(m)
        g.pass_on(m)
        if last is not None:
            g.sibling_arrived(last)
            units_of(last)
        last = m
    g.sibling_arrived(last)
    units_of(last)

    def partial(dst, lhs, rhs, p):
        lo, w = PARTS[p]

        @pl.loop(0, 8)
        def _(q):
            a, b, c = q // 4, (q // 2) % 2, q % 2
            dst[a, b, c, :, lo:lo + w] = tn(lhs[a, b, c], rhs[:, lo:lo + w]).astype(BF)

    sa = Scatter(at, fa, core_in, a0, a1, a2, sas, sar)
    sb = Scatter(at, fb, core_in, b0, b1, b2, sbs, sbr)
    for p in range(3):
        partial(fa, dgu, wgu, p)
        sa.start(sa.core_copy(p))
        if p:
            sa.add_core(p - 1)
    sa.add_core(2)
    pl.semaphore_signal(credit, inc=1, device_id=other(at, "c"), device_id_type=MESH)
    for p in range(3):
        partial(fb, zb, wd_ref, p)
    for p in range(3):
        sa.step(p, 0)
    pl.semaphore_wait(credit, 1)
    for p in range(3):
        sb.start(sb.core_copy(p))
    cw = 512

    def grads(lhs_list):
        @pl.loop(0, rows.shape[4] // cw)
        def _(n):
            s = pl.ds(pl.multiple_of(n * cw, cw), cw)
            for lhs, rhs, outs in lhs_list:
                acc = None
                for q in range(8):
                    a, b, c = q // 4, (q // 2) % 2, q % 2
                    v = nn(lhs[a, b, c], rhs[a, b, c, :, s])
                    acc = v if acc is None else acc + v
                for k, o in enumerate(outs):
                    o[:, s] = acc[k * units:(k + 1) * units].astype(BF)

    for p in range(3):
        sb.add_core(p)
    for p in range(3):
        sa.step(p, 1)
    grads([(zb, cot_ref, (gwd_out,))])
    for p in range(3):
        sa.finish(p, dn2_out)
    grads([(dgu, rows, (gwg_out, gwu_out))])
    for p in range(3):
        sb.step(p, 0)
    for p in range(3):
        sb.step(p, 1)
    for p in range(3):
        sb.finish(p, down_out)
    g.close()
    sa.close()
    sb.close()


def mlp(n2, cot_all, wg, wu, wd):
    rows, d = n2.shape
    units = wd.shape[0]
    vm = pl.BlockSpec(memory_space=pltpu.VMEM)
    hbm = pl.BlockSpec(memory_space=pl.ANY)
    cube = (2, 2, 2)
    dma = pltpu.SemaphoreType.DMA
    return pl.pallas_call(
        mlp_kernel,
        out_shape=(jax.ShapeDtypeStruct((rows, d), BF), jax.ShapeDtypeStruct((rows, d), F32))
        + (jax.ShapeDtypeStruct((units, d), BF),) * 3,
        in_specs=[vm, vm, hbm, hbm, vm],
        out_specs=(vm,) * 5,
        scratch_shapes=[
            pltpu.VMEM(cube + (2 * rows, d), BF),
            pltpu.VMEM((2 * units, d), BF),
            pltpu.VMEM(cube + (units, 2 * rows), BF),
            pltpu.VMEM(cube + (2 * units, 2 * rows), BF),
            pltpu.VMEM(cube + (2 * rows, d), BF),
            pltpu.VMEM(cube + (2 * rows, d), BF),
            pltpu.VMEM(cube + (rows, d), BF),
            pltpu.VMEM((2, 2, rows, d), BF), pltpu.VMEM((2, rows, d), BF), pltpu.VMEM((rows, d), BF),
            pltpu.VMEM((2, 2, rows, d), BF), pltpu.VMEM((2, rows, d), BF), pltpu.VMEM((rows, d), BF),
            dma((2,)), dma((3, 8)), dma((3, 8)), dma((8,)), dma((8,)),
            dma((3, 4)), dma((3, 4)), dma((3, 4)), dma((3, 4)), pltpu.SemaphoreType.REGULAR,
        ],
        compiler_params=pltpu.CompilerParams(collective_id=1, has_side_effects=True, vmem_limit_bytes=63 * 2**20),
        cost_estimate=pl.CostEstimate(flops=18 * 16 * rows * d * units, bytes_accessed=40 * 2**20, transcendentals=16 * rows * units),
        name="mlp",
    )(n2, cot_all.reshape(cube + (2 * rows, d)), wg, wu, wd)


def local(tokens, gain_attn, w_query, w_key, w_value, w_out, gain_mlp, w_gate_t, w_up_t, w_down, doc_ids, cotangent):
    rows, d = tokens.shape
    wrows = w_query.shape[0]
    grows = rows * 4
    seq_ids = doc_ids[0]
    length = seq_ids.shape[0]
    t = lax.axis_index(T)
    zi = lax.axis_index(Z)
    hd = HEAD_DIM
    qc = GROUP * hd
    gains = lax.all_gather(jnp.stack([gain_attn, gain_mlp]), AXES, axis=1, tiled=True).astype(F32)
    ga, gm = gains[0], gains[1]
    wall = jnp.concatenate([w_query.reshape(wrows, 4, qc), w_key.reshape(wrows, 4, hd), w_value.reshape(wrows, 4, hd)], axis=2).transpose(1, 0, 2)
    wsl = lax.all_to_all(wall, T, 0, 0, tiled=True)
    wqkv = lax.all_gather(wsl.reshape(4 * wrows, qc + 2 * hd), DP + Z, axis=0, tiled=True)
    wo = lax.dynamic_slice_in_dim(lax.all_gather(w_out, AXES, axis=0, tiled=True), t * qc, qc, 0)
    first = zi * grows
    own_ids = lax.dynamic_slice_in_dim(seq_ids, first, grows, 0)
    qpos = first + jnp.arange(grows, dtype=jnp.int32)
    kpos = jnp.arange(length, dtype=jnp.int32)
    starts = jnp.sum((seq_ids[None, :] < own_ids[:, None]).astype(jnp.int32), axis=1)
    freq = 10000.0 ** (-jnp.arange(hd // 2, dtype=F32) / (hd // 2))
    ph = (qpos - starts).astype(F32)[:, None] * freq[None, :]
    cos, sin = jnp.cos(ph), jnp.sin(ph)
    allowed = (seq_ids[None, :] == own_ids[:, None]) & (kpos[None, :] <= qpos[:, None])
    x = tokens.astype(F32)
    inv1 = lax.rsqrt(jnp.mean(x * x, axis=-1, keepdims=True) + NORM_EPS)
    n1 = (x * inv1 * ga).astype(BF)
    n1g = lax.all_gather(n1, T, axis=0, tiled=True)
    qkv = nn(n1g, wqkv)
    q = rotate(qkv[:, :qc].reshape(grows, GROUP, hd), cos[:, None], sin[:, None], 1.0).astype(BF)
    k = rotate(qkv[:, qc:qc + hd], cos, sin, 1.0).astype(BF)
    v = qkv[:, qc + hd:].astype(BF)
    kv = lax.all_gather(jnp.concatenate([k, v], axis=1), Z, axis=0, tiled=True)
    ka, va = kv[:, :hd], kv[:, hd:]
    scale = hd ** -0.5
    qh = q.transpose(1, 0, 2)

    def fwd(qq):
        s = jnp.where(allowed, nt(qq, ka) * scale, MASKED)
        mx = jnp.max(s, axis=1, keepdims=True)
        e = jnp.exp(s - mx)
        tot = jnp.sum(e, axis=1, keepdims=True)
        return nn((e / tot).astype(BF), va), mx + jnp.log(tot)

    o, lse = lax.map(fwd, qh)
    o = o.transpose(1, 0, 2).reshape(grows, qc).astype(BF)
    part = nn(o, wo).astype(BF)
    m = x + lax.psum_scatter(part, T, scatter_dimension=0, tiled=True).astype(F32)
    inv2 = lax.rsqrt(jnp.mean(m * m, axis=-1, keepdims=True) + NORM_EPS)
    n2 = (m * inv2 * gm).astype(BF)
    wgt = lax.all_gather(w_gate_t, REST, axis=0, tiled=True)
    wut = lax.all_gather(w_up_t, REST, axis=0, tiled=True)
    wdn = lax.all_gather(w_down, REST, axis=0, tiled=True)
    cot_all = lax.all_gather(cotangent, CUBE, axis=0, tiled=True)
    down, dn2, gwd, gwg, gwu = mlp(n2, cot_all, wgt, wut, wdn)
    rs = lambda a: lax.psum_scatter(a, REST, scatter_dimension=0, tiled=True).astype(F32)
    gwd, gwg, gwu = rs(gwd), rs(gwg), rs(gwu)
    block_out = (m + down.astype(F32)).astype(BF)
    ggm = jnp.sum(dn2 * m * inv2, axis=0)
    dy = dn2 * gm
    dm = cotangent.astype(F32) + inv2 * (dy - m * (inv2 * inv2) * jnp.mean(dy * m, axis=-1, keepdims=True))
    da = lax.all_gather(dm.astype(BF), T, axis=0, tiled=True)
    do = nt(da, wo).astype(BF)
    gwo = tn(o, da)
    doh = do.reshape(grows, GROUP, hd).transpose(1, 0, 2)

    def bwd(a):
        qq, dd, ls = a
        s = jnp.where(allowed, nt(qq, ka) * scale, MASKED)
        p = jnp.exp(s - ls)
        dp = nt(dd, va)
        ds = (p * (dp - jnp.sum(p * dp, axis=1, keepdims=True))).astype(BF)
        return nn(ds, ka) * scale, tn(ds, qq) * scale, tn(p.astype(BF), dd)

    dq, dk, dv = lax.map(bwd, (qh, doh, lse))
    dkv = jnp.concatenate([jnp.sum(dk, 0), jnp.sum(dv, 0)], axis=1).astype(BF)
    dkv = lax.psum_scatter(dkv, Z, scatter_dimension=0, tiled=True).astype(F32)
    dqr = rotate(dq.transpose(1, 0, 2), cos[:, None], sin[:, None], -1.0).reshape(grows, qc).astype(BF)
    dkr = rotate(dkv[:, :hd], cos, sin, -1.0).astype(BF)
    dqkv = jnp.concatenate([dqr, dkr, dkv[:, hd:].astype(BF)], axis=1)
    gw = lax.psum_scatter(tn(n1g, dqkv).astype(BF), DP + Z, scatter_dimension=0, tiled=True)
    gw = lax.all_to_all(gw.reshape(4, wrows, qc + 2 * hd), T, 0, 0, tiled=True).transpose(1, 0, 2).astype(F32)
    gwq = gw[:, :, :qc].reshape(wrows, 4 * qc)
    gwk = gw[:, :, qc:qc + hd].reshape(wrows, 4 * hd)
    gwv = gw[:, :, qc + hd:].reshape(wrows, 4 * hd)
    full = lax.dynamic_update_slice(jnp.zeros((4 * qc, d), BF), gwo.astype(BF), (t * qc, 0))
    gwo = lax.psum_scatter(full, AXES, scatter_dimension=0, tiled=True).astype(F32)
    dn1 = lax.psum_scatter(nt(dqkv, wqkv).astype(BF), T, scatter_dimension=0, tiled=True).astype(F32)
    gga = jnp.sum(dn1 * x * inv1, axis=0)
    dy1 = dn1 * ga
    dx1 = inv1 * (dy1 - x * (inv1 * inv1) * jnp.mean(dy1 * x, axis=-1, keepdims=True))
    gg = lax.psum_scatter(jnp.stack([gga, ggm]), AXES, scatter_dimension=1, tiled=True)
    return block_out, dm + dx1, gg[0], gwq, gwk, gwv, gwo, gg[1], gwg, gwu, gwd


def solution(mesh):
    dp, seq = mesh.shape["dp"], mesh.shape["seq"]
    m6 = Mesh(mesh.devices.reshape(dp // 2, 2, seq // 8, 2, 2, 2), AXES)
    row = P(AXES, None)
    vec = P(AXES)
    col = P(None, AXES)
    inner = jax.shard_map(
        local, mesh=m6,
        in_specs=(row, vec, row, row, row, row, vec, row, row, row, P(DP, None), row),
        out_specs=(row, row, vec, row, row, row, row, vec, row, row, row),
        check_vma=False,
    )

    def run(tokens, gain_attn, w_query, w_key, w_value, w_out, gain_mlp, w_gate, w_up, w_down, doc_ids, cotangent):
        outs = inner(tokens, gain_attn, w_query, w_key, w_value, w_out, gain_mlp, w_gate.T, w_up.T, w_down, doc_ids, cotangent)
        return outs[:8] + (outs[8].T, outs[9].T, outs[10])

    return run
```

```python
import functools

import jax
import jax.numpy as jnp
from jax import lax
from jax.experimental import pallas as pl
from jax.experimental.pallas import tpu as pltpu
from jax.sharding import Mesh, PartitionSpec as P

HEADS = 32
KV_HEADS = 4
HEAD_DIM = 64
GROUP = HEADS // KV_HEADS
NORM_EPS = 1e-05
MASKED = -1e30
AXES = ("dh", "dl", "zh", "zl", "x", "c")
T = ("x", "c")
Z = ("zh", "zl")
DP = ("dh", "dl")
CUBE = ("dl", "zl", "x", "c")
REST = ("dh", "zh")
BF = jnp.bfloat16
F32 = jnp.float32


def nn(a, b):
    return jnp.dot(a, b, preferred_element_type=F32)


def nt(a, b):
    return lax.dot_general(a, b, (((1,), (1,)), ((), ())), preferred_element_type=F32)


def tn(a, b):
    return lax.dot_general(a, b, (((0,), (0,)), ((), ())), preferred_element_type=F32)


def rotate(v, cos, sin, sign):
    h = v.shape[-1] // 2
    a, b = v[..., :h], v[..., h:]
    s = sin * sign
    return jnp.concatenate([a * cos - b * s, b * cos + a * s], axis=-1)


PARTS = ((0, 768), (768, 640), (1408, 640))
MESH = pl.DeviceIdType.MESH


def place():
    return {a: lax.axis_index(a) for a in AXES}


def other(at, *flip):
    return tuple(1 - at[a] if a in flip else at[a] for a in AXES)


def greet(at, partners):
    barrier = pltpu.get_barrier_semaphore()
    for flip in partners:
        pl.semaphore_signal(barrier, inc=1, device_id=other(at, *flip), device_id_type=MESH)
    pl.semaphore_wait(barrier, len(partners))


CDIMS = ("x", "zl", "dl")
MASKS = ((), ("x",), ("zl",), ("dl",), ("x", "zl"), ("zl", "dl"), ("dl", "x"), ("x", "zl", "dl"))


def cube_index(at, mask):
    return tuple(1 - at[a] if a in mask else at[a] for a in ("dl", "zl", "x"))


def order_of(p):
    return tuple(CDIMS[(p + s) % 3] for s in range(3))


class Log:
    def __init__(self):
        self.open = []

    def push(self, src, dst, ssem, rsem, device):
        cp = pltpu.make_async_remote_copy(src, dst, ssem, rsem, device_id=device, device_id_type=MESH)
        cp.start()
        self.open.append(cp)

    def close(self):
        for cp in self.open:
            cp.wait_send()


def landed(dst, sem, device):
    pltpu.make_async_remote_copy(dst, dst, sem, sem, device_id=device, device_id_type=MESH).wait_recv()


def at_z(at, o, n):
    i = lax.rem(at["zh"] * 2 + at["zl"] + o, n)
    return tuple(i // 2 if a == "zh" else lax.rem(i, 2) if a == "zl" else at[a] for a in AXES), i


def at_dp(at, o, n):
    i = lax.rem(at["dh"] * 2 + at["dl"] + o, n)
    return tuple(i // 2 if a == "dh" else lax.rem(i, 2) if a == "dl" else at[a] for a in AXES), i


def at_rest(at, o, n):
    i = lax.rem(at["dh"] * 2 + at["zh"] + o, n)
    return tuple(i // 2 if a == "dh" else lax.rem(i, 2) if a == "zh" else at[a] for a in AXES), i


def signal(device):
    pl.semaphore_signal(pltpu.get_barrier_semaphore(), inc=1, device_id=device, device_id_type=MESH)


def device_of(i, nz):
    t, j = lax.rem(i, 4), i // 4
    z, p = lax.rem(j, nz), j // nz
    return (p // 2, lax.rem(p, 2), z // 2, lax.rem(z, 2), t // 2, lax.rem(t, 2))


class Quad:
    def __init__(self, at, log, buf, ssem, rsem):
        self.at, self.log, self.buf, self.ssem, self.rsem = at, log, buf, ssem, rsem

    def start(self):
        at = self.at
        own = self.buf.at[at["x"], at["c"]]
        self.log.push(own, own, self.ssem.at[0], self.rsem.at[0], other(at, "x"))
        self.log.push(own, own, self.ssem.at[1], self.rsem.at[1], other(at, "c"))

    def forward(self):
        at = self.at
        far = self.buf.at[1 - at["x"], at["c"]]
        landed(far, self.rsem.at[0], other(at, "x"))
        self.log.push(far, far, self.ssem.at[2], self.rsem.at[2], other(at, "c"))

    def finish(self):
        at = self.at
        landed(self.buf.at[at["x"], 1 - at["c"]], self.rsem.at[1], other(at, "c"))
        landed(self.buf.at[1 - at["x"], 1 - at["c"]], self.rsem.at[2], other(at, "c"))


class QuadSum:
    def __init__(self, at, log, part, cin, xin, total, ssem, rsem, width):
        self.at, self.log, self.part, self.cin, self.xin, self.total = at, log, part, cin, xin, total
        self.ssem, self.rsem, self.width = ssem, rsem, width

    def cols(self, n):
        return slice(n * self.width, (n + 1) * self.width)

    def start(self, n):
        at, s = self.at, self.cols(n)
        self.log.push(self.part.at[:, 1 - at["c"], :, s], self.cin.at[:, :, s], self.ssem.at[0, n], self.rsem.at[0, n], other(at, "c"))

    def middle(self, n):
        at, s = self.at, self.cols(n)
        landed(self.cin.at[:, :, s], self.rsem.at[0, n], other(at, "c"))
        far = self.part.at[1 - at["x"], at["c"], :, s]
        far[...] = (far[...].astype(F32) + self.cin[1 - at["x"], :, s].astype(F32)).astype(BF)
        self.log.push(far, self.xin.at[:, s], self.ssem.at[1, n], self.rsem.at[1, n], other(at, "x"))
        near = self.part[at["x"], at["c"], :, s].astype(F32) + self.cin[at["x"], :, s].astype(F32)
        self.total[:, s] = self.total[:, s] + near

    def finish(self, n):
        s = self.cols(n)
        landed(self.xin.at[:, s], self.rsem.at[1, n], other(self.at, "x"))
        self.total[:, s] = self.total[:, s] + self.xin[:, s].astype(F32)


class Spread:
    def __init__(self, at, log, buf, nrest, parts, sems):
        self.at, self.log, self.buf, self.n, self.parts = at, log, buf, nrest, parts
        self.s0, self.r0, self.s1, self.r1 = sems

    def block(self, o, flip=(), part=None):
        at = self.at
        r = lax.rem(at["dh"] * (self.n_zh()) + at["zh"] + o, self.n)
        dh, zh = r // self.n_zh(), lax.rem(r, self.n_zh())
        dl = 1 - at["dl"] if "dl" in flip else at["dl"]
        zl = 1 - at["zl"] if "zl" in flip else at["zl"]
        ref = self.buf.at[dh * 2 + dl, zh * 2 + zl]
        if part is None:
            return ref
        lo, w = self.parts[part][:2]
        return ref.at[(slice(None),) * (len(ref.shape) - 1) + (slice(lo, lo + w),)]

    def n_zh(self):
        return self.buf.shape[1] // 2

    def start(self):
        for o in range(1, self.n):
            ref = self.block(0)
            self.log.push(ref, ref, self.s0.at[o - 1], self.r0.at[o - 1], at_rest(self.at, o, self.n)[0])

    def arrive(self, o):
        if o:
            landed(self.block(self.n - o), self.r0.at[o - 1], other(self.at, "zl"))

    def send(self, o, k, flip, part, dim):
        ref = self.block((self.n - o) % self.n, flip, part)
        self.log.push(ref, ref, self.s1.at[o, k], self.r1.at[o, k], other(self.at, dim))

    def take(self, o, k, flip, part):
        landed(self.block((self.n - o) % self.n, flip, part), self.r1.at[o, k], other(self.at, "zl"))

    def stage1(self, o):
        self.arrive(o)
        for p, (_, _, a, b) in enumerate(self.parts):
            self.send(o, 3 * p, (), p, a)
        for p, (_, _, a, b) in enumerate(self.parts):
            self.send(o, 3 * p + 1, (), p, b)

    def stage2(self, o):
        for p, (_, _, a, b) in enumerate(self.parts):
            self.take(o, 3 * p, (a,), p)
            self.send(o, 3 * p + 2, (a,), p, b)

    def finish(self, o):
        for p, (_, _, a, b) in enumerate(self.parts):
            self.take(o, 3 * p + 1, (b,), p)
            self.take(o, 3 * p + 2, (a, b), p)


class Merge:
    def __init__(self, at, log, buf, in1, in2, far, nrest, parts, sems):
        self.at, self.log, self.buf, self.in1, self.in2, self.far = at, log, buf, in1, in2, far
        self.n, self.parts = nrest, parts
        self.s0, self.r0, self.s1, self.r1 = sems

    def cut(self, ref, p):
        lo, w = self.parts[p][:2]
        return ref.at[(slice(None),) * (len(ref.shape) - 1) + (slice(lo, lo + w),)]

    def block(self, o, flip, p):
        at, nzh = self.at, self.buf.shape[1] // 2
        r = lax.rem(at["dh"] * nzh + at["zh"] + o, self.n)
        dl = 1 - at["dl"] if "dl" in flip else at["dl"]
        zl = 1 - at["zl"] if "zl" in flip else at["zl"]
        return self.cut(self.buf.at[(r // nzh) * 2 + dl, lax.rem(r, nzh) * 2 + zl], p)

    def stage1(self, o):
        for p, (_, _, a, b) in enumerate(self.parts):
            for k, flip in enumerate(((a, b), (a,))):
                self.log.push(self.block(o, flip, p), self.cut(self.in1.at[o, k], p), self.s1.at[o, 3 * p + k], self.r1.at[o, 3 * p + k],
                              other(self.at, a))

    def add(self, o, flip, p, ref):
        blk = self.block(o, flip, p)
        blk[...] = (blk[...].astype(F32) + ref[...].astype(F32)).astype(BF)

    def stage2(self, o):
        for p, (_, _, a, b) in enumerate(self.parts):
            src = self.cut(self.in1.at[o, 0], p)
            landed(src, self.r1.at[o, 3 * p], other(self.at, a))
            self.add(o, (b,), p, src)
            self.log.push(self.block(o, (b,), p), self.cut(self.in2.at[o], p), self.s1.at[o, 3 * p + 2], self.r1.at[o, 3 * p + 2],
                          other(self.at, b))
        for p, (_, _, a, b) in enumerate(self.parts):
            src = self.cut(self.in1.at[o, 1], p)
            landed(src, self.r1.at[o, 3 * p + 1], other(self.at, a))
            self.add(o, (), p, src)

    def stage3(self, o):
        for p, (_, _, a, b) in enumerate(self.parts):
            src = self.cut(self.in2.at[o], p)
            landed(src, self.r1.at[o, 3 * p + 2], other(self.at, b))
            self.add(o, (), p, src)
        if o:
            nzh = self.buf.shape[1] // 2
            at = self.at
            r = lax.rem(at["dh"] * nzh + at["zh"] + o, self.n)
            ref = self.buf.at[(r // nzh) * 2 + at["dl"], lax.rem(r, nzh) * 2 + at["zl"]]
            self.log.push(ref, self.far.at[o - 1], self.s0.at[o - 1], self.r0.at[o - 1], at_rest(at, o, self.n)[0])

    def result(self):
        at = self.at
        nzh = self.buf.shape[1] // 2
        total = self.buf[at["dh"] * 2 + at["dl"], at["zh"] * 2 + at["zl"]].astype(F32)
        for o in range(1, self.n):
            landed(self.far.at[o - 1], self.r0.at[o - 1], at_rest(at, self.n - o, self.n)[0])
            total = total + self.far[o - 1].astype(F32)
        return total


class AllSum:
    DIMS = ("c", "x", "dl", "zl")

    def __init__(self, at, log, val, got, nrest, ssem, rsem):
        self.at, self.log, self.val, self.got, self.n, self.ssem, self.rsem = at, log, val, got, nrest, ssem, rsem

    def start(self, k):
        if k < 4:
            self.log.push(self.val.at[k], self.got.at[k], self.ssem.at[k], self.rsem.at[k], other(self.at, self.DIMS[k]))
        else:
            for o in range(1, self.n):
                i = 3 + o
                self.log.push(self.val.at[4], self.got.at[i], self.ssem.at[i], self.rsem.at[i], at_rest(self.at, o, self.n)[0])

    def take(self, k):
        if k < 4:
            landed(self.got.at[k], self.rsem.at[k], other(self.at, self.DIMS[k]))
            self.val[k + 1] = self.val[k] + self.got[k]
            return None
        total = self.val[4]
        for o in range(1, self.n):
            i = 3 + o
            landed(self.got.at[i], self.rsem.at[i], other(self.at, "c"))
            total = total + self.got[i]
        return total


class Gather:
    def __init__(self, at, buf, ssem, rsem, csend, crecv):
        self.at, self.buf, self.ssem, self.rsem, self.csend, self.crecv = at, buf, ssem, rsem, csend, crecv
        self.rows = buf.shape[3] // 2
        self.open = []

    def block(self, mask, core, p=None):
        i = cube_index(self.at, mask)
        r = pl.ds(pl.multiple_of(core * self.rows, self.rows), self.rows)
        if p is None:
            return self.buf.at[i[0], i[1], i[2], r, :]
        lo, w = PARTS[p]
        return self.buf.at[i[0], i[1], i[2], r, lo:lo + w]

    def send(self, p, mask, dim):
        ref = self.block(mask, self.at["c"], p)
        k = MASKS.index(tuple(a for a in mask_sorted(mask + (dim,))))
        cp = pltpu.make_async_remote_copy(ref, ref, self.ssem.at[p, k], self.rsem.at[p, k],
                                          device_id=other(self.at, dim), device_id_type=MESH)
        cp.start()
        self.open.append(cp)

    def arrived(self, p, mask):
        k = MASKS.index(mask)
        ref = self.block(mask, self.at["c"], p)
        pltpu.make_async_remote_copy(ref, ref, self.ssem.at[p, k], self.rsem.at[p, k],
                                     device_id=other(self.at, "x"), device_id_type=MESH).wait_recv()

    def pass_on(self, mask):
        k = MASKS.index(mask)
        ref = self.block(mask, self.at["c"])
        cp = pltpu.make_async_remote_copy(ref, ref, self.csend.at[k], self.crecv.at[k],
                                          device_id=other(self.at, "c"), device_id_type=MESH)
        cp.start()
        self.open.append(cp)

    def sibling_arrived(self, mask):
        k = MASKS.index(mask)
        ref = self.block(mask, 1 - self.at["c"])
        pltpu.make_async_remote_copy(ref, ref, self.csend.at[k], self.crecv.at[k],
                                     device_id=other(self.at, "c"), device_id_type=MESH).wait_recv()

    def first(self):
        for p in range(3):
            self.send(p, (), order_of(p)[0])
        self.pass_on(())

    def second(self):
        for p in range(3):
            a, b, _ = order_of(p)
            self.send(p, (), b)
        for p in range(3):
            a, b, _ = order_of(p)
            self.arrived(p, (a,))
            self.send(p, (a,), b)

    def third(self):
        for p in range(3):
            a, b, c = order_of(p)
            self.send(p, (), c)
        for p in range(3):
            a, b, c = order_of(p)
            self.send(p, (a,), c)
        for p in range(3):
            a, b, c = order_of(p)
            self.arrived(p, (b,))
            self.send(p, (b,), c)
        for p in range(3):
            a, b, c = order_of(p)
            self.arrived(p, mask_sorted((a, b)))
            self.send(p, mask_sorted((a, b)), c)

    def complete(self, mask):
        for p in range(3):
            if order_of(p)[2] in mask:
                self.arrived(p, mask)

    def close(self):
        for cp in self.open:
            cp.wait_send()


def mask_sorted(mask):
    for m in MASKS:
        if set(m) == set(mask):
            return m
    raise ValueError(mask)


class Scatter:
    def __init__(self, at, full, core_in, r0, r1, r2, ssem, rsem):
        self.at, self.full, self.core_in, self.r = at, full, core_in, (r0, r1, r2)
        self.ssem, self.rsem = ssem, rsem
        self.rows = full.shape[3] // 2
        self.open = []

    def own(self, core):
        return pl.ds(pl.multiple_of(core * self.rows, self.rows), self.rows)

    def core_copy(self, p):
        lo, w = PARTS[p]
        return pltpu.make_async_remote_copy(
            self.full.at[:, :, :, self.own(1 - self.at["c"]), lo:lo + w], self.core_in.at[:, :, :, :, lo:lo + w],
            self.ssem.at[p, 3], self.rsem.at[p, 3], device_id=other(self.at, "c"), device_id_type=MESH)

    def stage_copy(self, p, s):
        lo, w = PARTS[p]
        dims = order_of(p)
        ix = []
        for a in ("dl", "zl", "x"):
            if a == dims[s]:
                ix.append(1 - self.at[a])
            elif a in dims[:s]:
                ix.append(self.at[a])
            else:
                ix.append(slice(None))
        dst = self.r[s]
        dst = dst.at[(slice(None),) * (len(dst.shape) - 1) + (slice(lo, lo + w),)]
        return pltpu.make_async_remote_copy(
            self.full.at[ix[0], ix[1], ix[2], self.own(self.at["c"]), lo:lo + w], dst,
            self.ssem.at[p, s], self.rsem.at[p, s], device_id=other(self.at, dims[s]), device_id_type=MESH)

    def start(self, cp):
        cp.start()
        self.open.append(cp)

    def blocks(self, p, s):
        dims = order_of(p)
        rest = dims[s:]
        out = []
        for m in MASKS:
            if set(m) <= set(rest):
                out.append(m)
        if rest:
            out.sort(key=lambda m: 0 if rest[0] in m else 1)
        return out

    def add_core(self, p):
        lo, w = PARTS[p]
        cp = self.core_copy(p)
        cp.wait_recv()
        self.add_loop(p, 0, None)
        self.start(self.stage_copy(p, 0))
        self.add_loop(p, 0, None, tail=True)

    def add_loop(self, p, s, src, tail=False):
        lo, w = PARTS[p]
        dims = order_of(p)
        for m in self.blocks(p, s):
            first = s < 3 and dims[s] in m
            if first == tail:
                continue
            i = cube_index(self.at, m)
            ref = self.full.at[i[0], i[1], i[2], self.own(self.at["c"]), lo:lo + w]
            if src is None:
                val = self.core_in[i[0], i[1], i[2], :, lo:lo + w]
            else:
                ix = [j for a, j in zip(("dl", "zl", "x"), i) if a in dims[s:]]
                val = src[tuple(ix) + (slice(None), slice(lo, lo + w))]
            ref[...] = (ref[...].astype(F32) + val.astype(F32)).astype(BF)

    def step(self, p, s):
        self.stage_copy(p, s).wait_recv()
        self.add_loop(p, s + 1, self.r[s])
        if s < 2:
            self.start(self.stage_copy(p, s + 1))
            self.add_loop(p, s + 1, self.r[s], tail=True)

    def finish(self, p, out):
        lo, w = PARTS[p]
        self.stage_copy(p, 2).wait_recv()
        i = cube_index(self.at, ())
        ref = self.full.at[i[0], i[1], i[2], self.own(self.at["c"]), lo:lo + w]
        out[:, lo:lo + w] = (ref[...].astype(F32) + self.r[2][:, lo:lo + w].astype(F32)).astype(out.dtype)

    def close(self):
        for cp in self.open:
            cp.wait_send()


def mlp_kernel(m_ref, gain_ref, cot_ref, wg_own, wu_own, wd_own, wg_far, wu_far, wd_far, down_out, dn2_out, gwd_out, gwg_out, gwu_out,
               rows, wgu, wd_ref, zb, dgu, fa, fb, core_in, a0, a1, a2, b0, b1, b2,
               lsem, gs, gr, gcs, gcr, sas, sar, sbs, sbr, credit):
    at = place()
    units = wd_ref.shape[0]
    brows = m_ref.shape[0]
    part = wd_own.shape[0]
    copies = []
    for k, (own_w, far_w, dst, lo) in enumerate(((wg_own, wg_far, wgu, 0), (wu_own, wu_far, wgu, units), (wd_own, wd_far, wd_ref, 0))):
        copies.append(pltpu.make_async_copy(own_w, dst.at[lo:lo + part, :], lsem.at[2 * k]))
        copies.append(pltpu.make_async_copy(far_w, dst.at[lo + part:lo + units, :], lsem.at[2 * k + 1]))
    for cp in copies:
        cp.start()
    greet(at, (("c",), ("x",), ("zl",), ("dl",)))
    g = Gather(at, rows, gs, gr, gcs, gcr)
    own = pl.ds(pl.multiple_of(at["c"] * brows, brows), brows)
    m = m_ref[...]
    inv = lax.rsqrt(jnp.mean(m * m, axis=1, keepdims=True) + NORM_EPS)
    rows[at["dl"], at["zl"], at["x"], own, :] = (m * inv * gain_ref[...]).astype(BF)
    g.first()
    for cp in copies:
        cp.wait()

    def units_of(mask):
        i = cube_index(at, mask)
        r = rows[i[0], i[1], i[2]]
        gu = nt(wgu[...], r)
        dz = nt(wd_ref[...], cot_ref[i[0], i[1], i[2]])
        gate, up = gu[:units], gu[units:]
        sg = jax.nn.sigmoid(gate)
        sl = gate * sg
        zb[i[0], i[1], i[2]] = (sl * up).astype(BF)
        dgu[i[0], i[1], i[2], :units, :] = (dz * up * (sg * (1.0 + gate * (1.0 - sg)))).astype(BF)
        dgu[i[0], i[1], i[2], units:, :] = (dz * sl).astype(BF)

    g.second()
    g.sibling_arrived(())
    units_of(())
    g.third()
    last = None
    for m in MASKS[1:]:
        g.complete(m)
        g.pass_on(m)
        if last is not None:
            g.sibling_arrived(last)
            units_of(last)
        last = m
    g.sibling_arrived(last)
    units_of(last)

    def partial(dst, lhs, rhs, p):
        lo, w = PARTS[p]

        @pl.loop(0, 8)
        def _(q):
            a, b, c = q // 4, (q // 2) % 2, q % 2
            dst[a, b, c, :, lo:lo + w] = tn(lhs[a, b, c], rhs[:, lo:lo + w]).astype(BF)

    sa = Scatter(at, fa, core_in, a0, a1, a2, sas, sar)
    sb = Scatter(at, fb, core_in, b0, b1, b2, sbs, sbr)
    for p in range(3):
        partial(fa, dgu, wgu, p)
        sa.start(sa.core_copy(p))
        if p:
            sa.add_core(p - 1)
    sa.add_core(2)
    pl.semaphore_signal(credit, inc=1, device_id=other(at, "c"), device_id_type=MESH)
    for p in range(3):
        partial(fb, zb, wd_ref, p)
    for p in range(3):
        sa.step(p, 0)
    pl.semaphore_wait(credit, 1)
    for p in range(3):
        sb.start(sb.core_copy(p))
    cw = 512

    def grads(lhs_list):
        @pl.loop(0, rows.shape[4] // cw)
        def _(n):
            s = pl.ds(pl.multiple_of(n * cw, cw), cw)
            for lhs, rhs, outs in lhs_list:
                acc = None
                for q in range(8):
                    a, b, c = q // 4, (q // 2) % 2, q % 2
                    v = nn(lhs[a, b, c], rhs[a, b, c, :, s])
                    acc = v if acc is None else acc + v
                for k, o in enumerate(outs):
                    o[:, s] = acc[k * units:(k + 1) * units].astype(BF)

    for p in range(3):
        sb.add_core(p)
    for p in range(3):
        sa.step(p, 1)
    grads([(zb, cot_ref, (gwd_out,))])
    for p in range(3):
        sa.finish(p, dn2_out)
    grads([(dgu, rows, (gwg_out, gwu_out))])
    for p in range(3):
        sb.step(p, 0)
    for p in range(3):
        sb.step(p, 1)
    for p in range(3):
        sb.finish(p, down_out)
    g.close()
    sa.close()
    sb.close()


def mlp(m, gain, cot_all, own, far):
    rows, d = m.shape
    far = tuple(a.reshape(-1, d) for a in far)
    units = own[0].shape[0] + far[0].shape[0]
    vm = pl.BlockSpec(memory_space=pltpu.VMEM)
    hbm = pl.BlockSpec(memory_space=pl.ANY)
    cube = (2, 2, 2)
    dma = pltpu.SemaphoreType.DMA
    return pl.pallas_call(
        mlp_kernel,
        out_shape=(jax.ShapeDtypeStruct((rows, d), BF), jax.ShapeDtypeStruct((rows, d), F32))
        + (jax.ShapeDtypeStruct((units, d), BF),) * 3,
        in_specs=[vm, vm, vm] + [hbm] * 6,
        out_specs=(vm,) * 5,
        scratch_shapes=[
            pltpu.VMEM(cube + (2 * rows, d), BF),
            pltpu.VMEM((2 * units, d), BF),
            pltpu.VMEM((units, d), BF),
            pltpu.VMEM(cube + (units, 2 * rows), BF),
            pltpu.VMEM(cube + (2 * units, 2 * rows), BF),
            pltpu.VMEM(cube + (2 * rows, d), BF),
            pltpu.VMEM(cube + (2 * rows, d), BF),
            pltpu.VMEM(cube + (rows, d), BF),
            pltpu.VMEM((2, 2, rows, d), BF), pltpu.VMEM((2, rows, d), BF), pltpu.VMEM((rows, d), BF),
            pltpu.VMEM((2, 2, rows, d), BF), pltpu.VMEM((2, rows, d), BF), pltpu.VMEM((rows, d), BF),
            dma((6,)), dma((3, 8)), dma((3, 8)), dma((8,)), dma((8,)),
            dma((3, 4)), dma((3, 4)), dma((3, 4)), dma((3, 4)), pltpu.SemaphoreType.REGULAR,
        ],
        compiler_params=pltpu.CompilerParams(collective_id=1, has_side_effects=True, vmem_limit_bytes=63 * 2**20),
        cost_estimate=pl.CostEstimate(flops=18 * 16 * rows * d * units, bytes_accessed=40 * 2**20, transcendentals=16 * rows * units),
        name="mlp",
    )(m, gain, cot_all, *own, *far)


def rot_rows(v, cos, sin):
    h = v.shape[0] // 2
    a, b = v[:h], v[h:]
    return jnp.concatenate([a * cos - b * sin, b * cos + a * sin], axis=0)


def attn_kernel(nz, ndp, tok_ref, wpack, wout_ref, gpack, cos_ref, sin_ref, start_ref, cot_ref, wg_ref, wu_ref, wd_ref,
                m_out, q_out, kv_out, o_out, lse_out, xg_out, wqkv_out, wo_out, gain_out, cot_out, wg_out, wu_out, wd_out,
                xg, wbuf, wobuf, gbuf, kvbuf, qbuf, kn, vt, obuf, lbuf, bias, part, cin, xin, total,
                lsem, s_disp, r_disp, s_gd, r_gd, s_w0, r_w0, s_w1, r_w1, s_g0, r_g0, s_g1, r_g1, s_o0, r_o0, s_o1, r_o1,
                s_od, r_od, s_x, r_x, s_kv, r_kv, s_p, r_p, s_rest, r_rest, gs, gr, gcs, gcr):
    at = place()
    log = Log()
    rows, d = tok_ref.shape
    hd = HEAD_DIM
    zi = at["zh"] * 2 + at["zl"]
    di = at["dh"] * 2 + at["dl"]
    t = at["x"] * 2 + at["c"]
    nrest = nz * ndp // 4
    wr = wpack.shape[1]
    quad = (("c",), ("x",), ("x", "c"))
    npeers = nz * ndp
    lin = (di * nz + zi) * 4 + t
    target = lax.rem(lin, npeers) * 4 + lin // npeers
    source = lax.rem(lin, 4) * npeers + lin // 4
    for f in quad:
        signal(other(at, *f))
    signal(other(at, "zl"))
    signal(other(at, "dl"))
    for o in range(1, nrest):
        signal(at_rest(at, o, nrest)[0])

    @pl.when(source != lin)
    def _():
        signal(device_of(source, nz))

    pl.semaphore_wait(pltpu.get_barrier_semaphore(), 4 + nrest + (target != lin).astype(jnp.int32))
    for k, f in enumerate(quad):
        dev = other(at, *f)
        tt = dev[4] * 2 + dev[5]
        log.push(wpack.at[tt], wbuf.at[di, zi, pl.ds(pl.multiple_of(t * wr, wr), wr), :], s_disp.at[k], r_disp.at[k], dev)
        log.push(gpack, gbuf.at[di, zi, t], s_gd.at[k], r_gd.at[k], dev)
    wbuf[di, zi, pl.ds(pl.multiple_of(t * wr, wr), wr), :] = wpack[t]
    gbuf[di, zi, t] = gpack[...]
    x = tok_ref[...].astype(F32)
    inv = lax.rsqrt(jnp.mean(x * x, axis=1, keepdims=True) + NORM_EPS)
    xg[at["x"], at["c"]] = (x * inv).astype(BF)
    total[...] = x
    qx = Quad(at, log, xg, s_x, r_x)
    qx.start()
    for k, f in enumerate(quad):
        dev = other(at, *f)
        tt = dev[4] * 2 + dev[5]
        landed(wbuf.at[di, zi, pl.ds(pl.multiple_of(tt * wr, wr), wr), :], r_disp.at[k], dev)
        landed(gbuf.at[di, zi, tt], r_gd.at[k], dev)
    half = 128 * (wbuf.shape[3] // 256)
    sw = Spread(at, log, wbuf, nrest, ((0, half, "dl", "zl"), (half, wbuf.shape[3] - half, "zl", "dl")), (s_w0, r_w0, s_w1, r_w1))
    sg = Spread(at, log, gbuf, nrest, ((0, 128, "zl", "dl"),), (s_g0, r_g0, s_g1, r_g1))
    so = Spread(at, log, wobuf, nrest, ((0, d // 2, "dl", "zl"), (d // 2, d // 2, "zl", "dl")), (s_o0, r_o0, s_o1, r_o1))
    for sp in (sw, sg):
        sp.start()
        sp.stage1(0)
    qx.forward()
    @pl.when(target != lin)
    def _():
        pltpu.make_async_remote_copy(wout_ref, wobuf.at[lax.rem(lin, npeers) // nz, lax.rem(lax.rem(lin, npeers), nz)], s_od, r_od,
                                     device_id=device_of(target, nz), device_id_type=MESH).start()

    @pl.when(target == lin)
    def _():
        wobuf[di, zi] = wout_ref[...]

    qn = bias.shape[2]
    nq = bias.shape[0]
    keys = bias.shape[1]
    kpos = lax.broadcasted_iota(jnp.int32, (keys, qn), 0)
    for b in range(nq):
        qpos = zi * (4 * rows) + b * qn + lax.broadcasted_iota(jnp.int32, (1, qn), 1)
        first = start_ref[:, b * qn:(b + 1) * qn]
        bias[b] = jnp.where((kpos >= first) & (kpos <= qpos), 0.0, MASKED)
    for sp in (sw, sg):
        sp.stage2(0)
    for o in range(1, nrest):
        for sp in (sw, sg):
            sp.stage1(o)
    outs = ((wg_ref, wg_out), (wu_ref, wu_out), (wd_ref, wd_out))

    def push_rest(k):
        a, b = outs[k]
        for o in range(1, nrest):
            dev, _ = at_rest(at, o, nrest)
            log.push(a, b.at[o - 1], s_rest.at[k, o - 1], r_rest.at[k, o - 1], dev)

    push_rest(0)
    for o in range(1, nrest):
        for sp in (sw, sg):
            sp.stage2(o)
    for o in range(nrest):
        for sp in (sw, sg):
            sp.finish(o)
    qx.finish()
    xa = xg[...].reshape(4 * rows, d)
    qkv = jnp.transpose(nn(xa, wbuf[...].reshape(d, wbuf.shape[3])))
    cos, sin = cos_ref[...], sin_ref[...]
    kvbuf[zi, :hd, :] = rot_rows(qkv[GROUP * hd:(GROUP + 1) * hd], cos, sin).astype(BF)
    kvbuf[zi, hd:, :] = qkv[(GROUP + 1) * hd:].astype(BF)
    nzh = nz // 2
    for o in range(1, nzh):
        log.push(kvbuf.at[zi], kvbuf.at[zi], s_kv.at[0, o], r_kv.at[0, o], at_z(at, 2 * o, nz)[0])
    log.push(kvbuf.at[zi], kvbuf.at[zi], s_kv.at[1, 0], r_kv.at[1, 0], other(at, "zl"))
    for h in range(GROUP):
        qbuf[h] = (rot_rows(qkv[h * hd:(h + 1) * hd], cos, sin).astype(BF) * 0.125).astype(BF)

    @pl.when(source != lin)
    def _():
        pltpu.make_async_remote_copy(wobuf.at[di, zi], wobuf.at[di, zi], s_od, r_od,
                                     device_id=device_of(source, nz), device_id_type=MESH).wait_recv()

    so.start()
    so.stage1(0)
    g = Gather(at, cot_out, gs, gr, gcs, gcr)
    here = [pltpu.make_async_copy(cot_ref, g.block((), at["c"]), lsem.at[0])]
    for cp in here:
        cp.start()
    save = [pltpu.make_async_copy(xg, xg_out, lsem.at[4]), pltpu.make_async_copy(wbuf, wqkv_out, lsem.at[5]),
            pltpu.make_async_copy(gbuf, gain_out, lsem.at[6]), pltpu.make_async_copy(qbuf, q_out, lsem.at[7])]
    for cp in save:
        cp.start()
    for o in range(1, nzh):
        dev, i = at_z(at, nz - 2 * o, nz)
        landed(kvbuf.at[i], r_kv.at[0, o], dev)
        log.push(kvbuf.at[i], kvbuf.at[i], s_kv.at[1, o], r_kv.at[1, o], other(at, "zl"))
    for o in range(nzh):
        landed(kvbuf.at[zi], r_kv.at[1, o], other(at, "zl"))
    push_rest(1)
    here[0].wait()
    g.first()
    save.append(pltpu.make_async_copy(kvbuf, kv_out, lsem.at[8]))
    save[-1].start()
    tl = kvbuf.shape[2]
    for i in range(nz):
        kn[i * tl:(i + 1) * tl, :] = jnp.transpose(kvbuf[i, :hd, :].astype(F32)).astype(BF)
        vt[:hd, i * tl:(i + 1) * tl] = kvbuf[i, hd:, :]
    vt[hd:, :] = jnp.ones((vt.shape[0] - hd, keys), BF)

    def heads(b, lo, hi):
        @pl.loop(lo, hi)
        def _(h):
            s = nn(kn[...], qbuf[h, :, b * qn:(b + 1) * qn]) + bias[b]
            mx = jnp.max(s, axis=0, keepdims=True)
            e = jnp.exp(s - mx).astype(BF)
            oe = nn(vt[...], e)
            tot = oe[hd:hd + 1]
            obuf[h, :, b * qn:(b + 1) * qn] = (oe[:hd] / tot).astype(BF)
            lbuf[h, :, b * qn:(b + 1) * qn] = mx + jnp.log(tot)

    heads(0, 0, 4)
    so.stage2(0)
    for o in range(1, nrest):
        so.stage1(o)
    g.second()
    heads(0, 4, 8)
    for o in range(1, nrest):
        so.stage2(o)
    g.third()
    push_rest(2)
    heads(1, 0, 8)
    for m in MASKS[1:4]:
        g.complete(m)
        g.pass_on(m)
    for o in range(nrest):
        so.finish(o)
    save += [pltpu.make_async_copy(wobuf, wo_out, lsem.at[9]), pltpu.make_async_copy(obuf, o_out, lsem.at[10]),
             pltpu.make_async_copy(lbuf, lse_out, lsem.at[11])]
    for cp in save[-3:]:
        cp.start()
    cw = 512
    nc = d // cw
    oT = obuf[...].reshape(GROUP * hd, 4 * rows)
    red = QuadSum(at, log, part, cin, xin, total, s_p, r_p, cw)
    for n in range(nc):
        s = slice(n * cw, (n + 1) * cw)
        wo = wobuf[:, :, :, s].reshape(GROUP * hd, cw)
        part[:, :, :, s] = tn(oT, wo).astype(BF).reshape(2, 2, rows, cw)
        red.start(n)
        if n:
            red.middle(n - 1)
    red.middle(nc - 1)
    for m in MASKS[4:]:
        g.complete(m)
        g.pass_on(m)
    for n in range(nc):
        red.finish(n)
    m_out[...] = total[...]
    for m in MASKS:
        g.sibling_arrived(m)
    for k, (a, b) in enumerate(outs):
        for o in range(1, nrest):
            dev, _ = at_rest(at, nrest - o, nrest)
            landed(b.at[o - 1], r_rest.at[k, o - 1], dev)
    for cp in save:
        cp.wait()

    @pl.when(target != lin)
    def _():
        pltpu.make_async_remote_copy(wout_ref, wobuf.at[di, zi], s_od, r_od,
                                     device_id=device_of(target, nz), device_id_type=MESH).wait_send()

    g.close()
    log.close()


def attn(nz, ndp, tokens, wpack, w_out, gpack, cosT, sinT, starts, cot, wg, wu, wd):
    rows, d = tokens.shape
    wr, wc = wpack.shape[1:]
    hd = HEAD_DIM
    units = wd.shape[0]
    nrest = nz * ndp // 4
    keys = nz * 4 * rows
    qn = 2 * rows
    vm = pl.BlockSpec(memory_space=pltpu.VMEM)
    hbm = pl.BlockSpec(memory_space=pl.ANY)
    dma = pltpu.SemaphoreType.DMA
    sd = jax.ShapeDtypeStruct
    sh = dict(
        xg=(2, 2, rows, d), w=(ndp, nz, 4 * wr, wc), wo=(ndp, nz, wr, d), g=(ndp, nz, 4, 16, 128),
        kv=(nz, 2 * hd, 4 * rows), q=(GROUP, hd, 4 * rows), lse=(GROUP, 1, 4 * rows))
    outs = (sd((rows, d), F32), sd(sh["q"], BF), sd(sh["kv"], BF), sd(sh["q"], BF), sd(sh["lse"], F32), sd(sh["xg"], BF),
            sd(sh["w"], BF), sd(sh["wo"], BF), sd(sh["g"], BF), sd((2, 2, 2, 2 * rows, d), BF)) + (sd((nrest - 1, units, d), BF),) * 3
    nq = 4 * rows // qn
    zz = (max(nrest - 1, 1),)
    return pl.pallas_call(
        functools.partial(attn_kernel, nz, ndp),
        out_shape=outs,
        in_specs=[vm] * 8 + [hbm] * 3,
        out_specs=(vm,) + (hbm,) * (len(outs) - 1),
        scratch_shapes=[
            pltpu.VMEM(sh["xg"], BF), pltpu.VMEM(sh["w"], BF), pltpu.VMEM(sh["wo"], BF), pltpu.VMEM(sh["g"], BF),
            pltpu.VMEM(sh["kv"], BF), pltpu.VMEM(sh["q"], BF), pltpu.VMEM((keys, hd), BF), pltpu.VMEM((hd + 16, keys), BF),
            pltpu.VMEM(sh["q"], BF), pltpu.VMEM(sh["lse"], F32), pltpu.VMEM((nq, keys, qn), F32),
            pltpu.VMEM((2, 2, rows, d), BF), pltpu.VMEM((2, rows, d), BF), pltpu.VMEM((rows, d), BF), pltpu.VMEM((rows, d), F32),
            dma((12,)), dma((3,)), dma((3,)), dma((3,)), dma((3,))] + [dma(zz), dma(zz), dma((nrest, 6)), dma((nrest, 6))] * 3 + [
            dma, dma, dma((3,)), dma((3,)), dma((2, nz // 2)), dma((2, nz // 2)), dma((2, 4)), dma((2, 4)),
            dma((3,) + zz), dma((3,) + zz), dma((3, 8)), dma((3, 8)), dma((8,)), dma((8,)),
        ],
        compiler_params=pltpu.CompilerParams(collective_id=2, has_side_effects=True, vmem_limit_bytes=58 * 2**20),
        name="attention",
    )(tokens, wpack, w_out, gpack, cosT, sinT, starts, cot, wg, wu, wd)


def back_kernel(nz, ndp, m_ref, dn2_ref, gain_ref, cot_ref, tok_ref, cos_ref, sin_ref, start_ref,
                xg_in, wqkv_in, wo_in, q_in, kv_in, o_in, lse_in, gd_in, gg_in, gu_in,
                dx_out, gq_out, gkv_out, gwo_out, gain_out, fd_out, fg_out, fu_out,
                xg, wqkv, wo, qbuf, kvbuf, obuf, lbuf, dag, dob, delta, kn, vn, kt, bias, dkv, dqb, kvp, kvin, dqkv,
                gob, go1, go2, gof, gqb, gq1, gq2, gqf, gkb, gk1, gk2, gkf, gsend, gpart, part, cin, xin, total, ogot, val, got,
                lsem, s_x, r_x, s_o0, r_o0, s_o1, r_o1, s_q0, r_q0, s_q1, r_q1, s_k0, r_k0, s_k1, r_k1,
                s_kv, r_kv, s_p, r_p, s_rest, r_rest, s_od, r_od, s_gq, r_gq, s_gk, r_gk, s_v, r_v):
    at = place()
    log = Log()
    rows, d = m_ref.shape
    hd = HEAD_DIM
    qc = GROUP * hd
    zi = at["zh"] * 2 + at["zl"]
    di = at["dh"] * 2 + at["dl"]
    t = at["x"] * 2 + at["c"]
    nrest = nz * ndp // 4
    npeers = nz * ndp
    nzh = nz // 2
    wr = gwo_out.shape[0]
    keys = kn.shape[0]
    tl = 4 * rows
    lin = (di * nz + zi) * 4 + t
    target = lax.rem(lin, npeers) * 4 + lin // npeers
    source = lax.rem(lin, 4) * npeers + lin // 4
    loads = [pltpu.make_async_copy(a, b, lsem.at[k]) for k, (a, b) in enumerate((
        (kv_in, kvbuf), (wo_in, wo), (o_in, obuf), (q_in, qbuf), (lse_in, lbuf), (xg_in, xg), (wqkv_in, wqkv)))]
    for cp in loads:
        cp.start()
    quad = (("c",), ("x",), ("x", "c"))
    for f in quad:
        signal(other(at, *f))
    signal(other(at, "zl"))
    signal(other(at, "dl"))
    for o in range(1, nrest):
        signal(at_rest(at, o, nrest)[0])

    @pl.when(target != lin)
    def _():
        signal(device_of(target, nz))

    m = m_ref[...]
    inv2 = lax.rsqrt(jnp.mean(m * m, axis=1, keepdims=True) + NORM_EPS)
    mh = m * inv2
    dn2 = dn2_ref[...].astype(F32)
    dy = dn2 * gain_ref[...]
    dm = cot_ref[...].astype(F32) + inv2 * (dy - mh * jnp.mean(dy * mh, axis=1, keepdims=True))
    dx_out[...] = dm
    dag[at["x"], at["c"]] = dm.astype(BF)
    total[...] = jnp.zeros_like(total)
    gsum = jnp.sum(dn2 * mh, axis=0, keepdims=True)
    for i in range(d // 128):
        val[0, i:i + 1, :] = gsum[:, i * 128:(i + 1) * 128]
    pl.semaphore_wait(pltpu.get_barrier_semaphore(), 4 + nrest + (source != lin).astype(jnp.int32))
    qx = Quad(at, log, dag, s_x, r_x)
    qx.start()
    gs = AllSum(at, log, val, got, nrest, s_v, r_v)
    gs.start(0)
    fars = ((gd_in, fd_out), (gg_in, fg_out), (gu_in, fu_out))
    units = fd_out.shape[1]
    for k, (a, b) in enumerate(fars):
        for o in range(1, nrest):
            dev, _ = at_rest(at, nrest - o, nrest)
            log.push(a.at[pl.ds(o * units, units), :], b.at[o - 1], s_rest.at[k, o - 1], r_rest.at[k, o - 1], dev)
    loads[0].wait()
    for i in range(nz):
        kn[i * tl:(i + 1) * tl, :] = jnp.transpose(kvbuf[i, :hd, :].astype(F32)).astype(BF)
        vn[i * tl:(i + 1) * tl, :] = jnp.transpose(kvbuf[i, hd:, :].astype(F32)).astype(BF)
        kt[:, i * tl:(i + 1) * tl] = kvbuf[i, :hd, :]
    kpos = lax.broadcasted_iota(jnp.int32, (keys, tl), 0)
    qpos = zi * tl + lax.broadcasted_iota(jnp.int32, (1, tl), 1)
    bias[...] = jnp.where((kpos >= start_ref[...]) & (kpos <= qpos), 0.0, MASKED)
    dkv[...] = jnp.zeros_like(dkv)
    for cp in loads[1:]:
        cp.wait()
    gs.take(0)
    gs.start(1)
    qx.forward()
    qx.finish()
    da = dag[...].reshape(tl, d)
    doT = nt(wo[...].reshape(qc, d), da).astype(BF)
    dob[...] = doT.reshape(GROUP, hd, tl)
    delta[...] = jnp.sum((dob[...].astype(F32) * obuf[...].astype(F32)), axis=1, keepdims=True)
    gs.take(1)
    gs.start(2)
    cw = 512
    oT = obuf[...].reshape(qc, tl)
    for n in range(d // cw):
        s = slice(n * cw, (n + 1) * cw)
        gob[:, :, :, s] = nn(oT, dag[:, :, :, s].reshape(tl, cw)).astype(BF).reshape(ndp, nz, wr, cw)
    mo = Merge(at, log, gob, go1, go2, gof, nrest, ((0, d // 2, "dl", "zl"), (d // 2, d // 2, "zl", "dl")), (s_o0, r_o0, s_o1, r_o1))
    far_first = tuple(range(1, nrest)) + (0,)
    for o in far_first:
        mo.stage1(o)

    def heads(lo, hi):
        @pl.loop(lo, hi)
        def _(h):
            qT, dT = qbuf[h], dob[h]
            p = jnp.exp(nn(kn[...], qT) + bias[...] - lbuf[h])
            ds = (p * (nn(vn[...], dT) - delta[h])).astype(BF)
            pb = p.astype(BF)
            dkv[:hd, :] += nt(qT, ds)
            dkv[hd:, :] += nt(dT, pb)
            dqb[pl.ds(pl.multiple_of(h * hd, hd), hd), :] = rot_rows(nn(kt[...], ds) * 0.125, cos_ref[...], -sin_ref[...])

    heads(0, 3)
    gs.take(2)
    gs.start(3)
    for o in far_first:
        mo.stage2(o)
    heads(3, 6)
    gs.take(3)
    gs.start(4)
    for o in far_first:
        mo.stage3(o)
    heads(6, 8)
    for i in range(nz):
        kvp[i] = dkv[:, i * tl:(i + 1) * tl].astype(BF)
    for o in range(1, nz):
        dev, i = at_z(at, o, nz)
        log.push(kvp.at[i], kvin.at[o - 1], s_kv.at[o - 1], r_kv.at[o - 1], dev)
    dqkv[:, :qc] = jnp.transpose(dqb[...]).astype(BF)
    mq = Merge(at, log, gqb, gq1, gq2, gqf, nrest, ((0, qc // 2, "dl", "zl"), (qc // 2, qc // 2, "zl", "dl")), (s_q0, r_q0, s_q1, r_q1))
    mk = Merge(at, log, gkb, gk1, gk2, gkf, nrest, ((0, 2 * hd, "zl", "dl"),), (s_k0, r_k0, s_k1, r_k1))

    def weight_grad(dst, lo, hi):
        step = 256
        per = step // (4 * wr)
        for n in range(d // step):
            xs = xg[:, :, :, n * step:(n + 1) * step].reshape(tl, step)
            v = tn(xs, dqkv[:, lo:hi]).astype(BF)
            for b in range(per):
                f = n * per + b
                dst[f // nz, f % nz] = v[b * 4 * wr:(b + 1) * 4 * wr]

    weight_grad(gqb, 0, qc)
    for o in far_first:
        mq.stage1(o)
    acc = dkv[:, pl.ds(pl.multiple_of(zi * tl, tl), tl)]
    for o in range(1, nz):
        dev, _ = at_z(at, nz - o, nz)
        landed(kvin.at[o - 1], r_kv.at[o - 1], dev)
        acc = acc + kvin[o - 1].astype(F32)
    dk = rot_rows(acc[:hd], cos_ref[...], -sin_ref[...])
    dqkv[:, qc:] = jnp.transpose(jnp.concatenate([dk, acc[hd:]], axis=0)).astype(BF)
    weight_grad(gkb, qc, qc + 2 * hd)
    for o in far_first:
        mk.stage1(o)
    red = QuadSum(at, log, part, cin, xin, total, s_p, r_p, cw)
    w = wqkv[...].reshape(d, qc + 2 * hd)
    nc = d // cw
    for n in range(nc):
        part[:, :, :, n * cw:(n + 1) * cw] = nt(dqkv[...], w[n * cw:(n + 1) * cw]).astype(BF).reshape(2, 2, rows, cw)
        red.start(n)
        if n:
            red.middle(n - 1)
    for o in far_first:
        mq.stage2(o)
    red.middle(nc - 1)
    for o in far_first:
        mk.stage2(o)
    for o in far_first:
        mq.stage3(o)
    for o in far_first:
        mk.stage3(o)
    gsend[...] = mo.result().astype(BF)

    @pl.when(source != lin)
    def _():
        pltpu.make_async_remote_copy(gsend, ogot, s_od, r_od, device_id=device_of(source, nz), device_id_type=MESH).start()

    @pl.when(source == lin)
    def _():
        ogot[...] = gsend[...]

    for n in range(nc):
        red.finish(n)
    x = tok_ref[...].astype(F32)
    inv1 = lax.rsqrt(jnp.mean(x * x, axis=1, keepdims=True) + NORM_EPS)
    xh = x * inv1
    dy1 = total[...]
    dx_out[...] = dx_out[...] + inv1 * (dy1 - xh * jnp.mean(dy1 * xh, axis=1, keepdims=True))
    gain_out[...] = gs.take(4)
    for merge, dst, sp, ss, rs, lo, hi in ((mq, gq_out, gpart.at[:, :qc], s_gq, r_gq, 0, qc), (mk, gkv_out, gpart.at[:, qc:], s_gk, r_gk, qc, qc + 2 * hd)):
        gpart[:, lo:hi] = merge.result().astype(BF)
        dst[t] = gpart[pl.ds(pl.multiple_of(t * wr, wr), wr), lo:hi]
        for k, f in enumerate(quad):
            dev = other(at, *f)
            tt = dev[4] * 2 + dev[5]
            log.push(gpart.at[pl.ds(pl.multiple_of(tt * wr, wr), wr), lo:hi], dst.at[t], ss.at[k], rs.at[k], dev)
    @pl.when(target != lin)
    def _():
        pltpu.make_async_remote_copy(gsend, ogot, s_od, r_od, device_id=device_of(target, nz), device_id_type=MESH).wait_recv()

    gwo_out[...] = ogot[...].astype(F32)
    for dst, rs in ((gq_out, r_gq), (gkv_out, r_gk)):
        for k, f in enumerate(quad):
            dev = other(at, *f)
            tt = dev[4] * 2 + dev[5]
            landed(dst.at[tt], rs.at[k], dev)
    for k, (a, b) in enumerate(fars):
        for o in range(1, nrest):
            dev, _ = at_rest(at, o, nrest)
            landed(b.at[o - 1], r_rest.at[k, o - 1], dev)

    @pl.when(source != lin)
    def _():
        pltpu.make_async_remote_copy(gsend, ogot, s_od, r_od, device_id=device_of(source, nz), device_id_type=MESH).wait_send()

    log.close()


def back(nz, ndp, m, dn2, gain, cot, tokens, cosT, sinT, starts, xg, wqkv, wo, q, kv, o, lse, grads):
    rows, d = m.shape
    hd = HEAD_DIM
    qc = GROUP * hd
    nrest = nz * ndp // 4
    wr = wo.shape[2]
    keys = nz * 4 * rows
    tl = 4 * rows
    units = grads[0].shape[0] // nrest
    vm = pl.BlockSpec(memory_space=pltpu.VMEM)
    hbm = pl.BlockSpec(memory_space=pl.ANY)
    dma = pltpu.SemaphoreType.DMA
    sd = jax.ShapeDtypeStruct
    nf = max(nrest - 1, 1)
    outs = (sd((rows, d), F32), sd((4, wr, qc), BF), sd((4, wr, 2 * hd), BF), sd((wr, d), F32), sd((16, 128), F32)) + (
        sd((nrest - 1, units, d), BF),) * 3
    V = pltpu.VMEM

    def merge_bufs(r, c):
        return [V((ndp, nz, r, c), BF), V((nrest, 2, r, c), BF), V((nrest, r, c), BF), V((nf, r, c), BF)]

    return pl.pallas_call(
        functools.partial(back_kernel, nz, ndp),
        out_shape=outs,
        in_specs=[vm] * 8 + [hbm] * 10,
        out_specs=(vm,) * 5 + (hbm,) * 3,
        scratch_shapes=[
            V(xg.shape, BF), V(wqkv.shape, BF), V(wo.shape, BF), V(q.shape, BF), V(kv.shape, BF), V(o.shape, BF), V(lse.shape, F32),
            V((2, 2, rows, d), BF), V(q.shape, BF), V(lse.shape, F32), V((keys, hd), BF), V((keys, hd), BF), V((hd, keys), BF),
            V((keys, tl), F32), V((2 * hd, keys), F32), V((qc, tl), F32), V(kv.shape, BF), V((max(nz - 1, 1), 2 * hd, tl), BF),
            V((tl, qc + 2 * hd), BF)]
        + merge_bufs(wr, d) + merge_bufs(4 * wr, qc) + merge_bufs(4 * wr, 2 * hd) + [
            V((wr, d), BF), V((4 * wr, qc + 2 * hd), BF), V((2, 2, rows, d), BF), V((2, rows, d), BF), V((rows, d), BF), V((rows, d), F32),
            V((wr, d), BF), V((5, 16, 128), F32), V((4 + nf, 16, 128), F32),
            dma((7,)), dma((3,)), dma((3,))] + [dma((nf,)), dma((nf,)), dma((nrest, 6)), dma((nrest, 6))] * 3 + [
            dma((nz,)), dma((nz,)), dma((2, 4)), dma((2, 4)), dma((3, nf)), dma((3, nf)), dma, dma, dma((3,)), dma((3,)), dma((3,)), dma((3,)),
            dma((4 + nf,)), dma((4 + nf,))],
        compiler_params=pltpu.CompilerParams(collective_id=3, has_side_effects=True, vmem_limit_bytes=62 * 2**20),
        name="backward",
    )(m, dn2, gain, cot, tokens, cosT, sinT, starts, xg, wqkv, wo, q, kv, o, lse, *grads)


def local(tokens, gain_attn, w_query, w_key, w_value, w_out, gain_mlp, w_gate_t, w_up_t, w_down, doc_ids, cotangent, nz, ndp):
    rows, d = tokens.shape
    wr = w_query.shape[0]
    grows = rows * 4
    seq_ids = doc_ids[0]
    length = seq_ids.shape[0]
    zi = lax.axis_index(Z)
    hd = HEAD_DIM
    qc = GROUP * hd
    ga = gain_attn.astype(F32)[:, None]
    wall = jnp.concatenate([w_query.reshape(wr, 4, qc), w_key.reshape(wr, 4, hd), w_value.reshape(wr, 4, hd)], axis=2).transpose(1, 0, 2)
    wpack = (wall.astype(F32) * ga[None]).astype(BF)
    gpack = jnp.pad(gain_mlp[None], ((0, 15), (0, 128 - wr)))
    first = zi * grows
    own_ids = lax.dynamic_slice_in_dim(seq_ids, first, grows, 0)
    qpos = first + jnp.arange(grows, dtype=jnp.int32)
    starts = jnp.sum((seq_ids[:, None] < own_ids[None, :]).astype(jnp.int32), axis=0)
    freq = 10000.0 ** (-jnp.arange(hd // 2, dtype=F32) / (hd // 2))
    ph = (qpos - starts).astype(F32)[None, :] * freq[:, None]
    cosT, sinT = jnp.cos(ph), jnp.sin(ph)
    units = w_down.shape[0]
    fill = -units % 16
    if fill:
        w_gate_t, w_up_t, w_down = (jnp.pad(w, ((0, fill), (0, 0))) for w in (w_gate_t, w_up_t, w_down))
    m, q, kv, o, lse, xg, wqkv, wo, gains, cot_all, wgt, wut, wdn = attn(
        nz, ndp, tokens, wpack, w_out, gpack, cosT, sinT, starts[None], cotangent, w_gate_t, w_up_t, w_down)
    gm = gains[:, :, :, 0, :wr].reshape(1, d).astype(F32)
    down, dn2, gwd, gwg, gwu = mlp(m, gm, cot_all, (w_gate_t, w_up_t, w_down), (wgt, wut, wdn))
    dx, gq, gkv, gwo, gsum, fd, fg, fu = back(
        nz, ndp, m, dn2, gm, cotangent, tokens, cosT, sinT, starts[None], xg, wqkv, wo, q, kv, o, lse, (gwd, gwg, gwu))
    block_out = (m + down.astype(F32)).astype(BF)

    def own(a, far):
        return (a[:units + fill].astype(F32) + jnp.sum(far.astype(F32), axis=0))[:units]

    gw = jnp.concatenate([gq, gkv], axis=2).astype(F32)
    gga = jnp.sum(gw * wall.astype(F32), axis=(0, 2))
    gw = (gw * ga[None]).transpose(1, 0, 2)
    gwq = gw[:, :, :qc].reshape(wr, 4 * qc)
    gwk = gw[:, :, qc:qc + hd].reshape(wr, 4 * hd)
    gwv = gw[:, :, qc + hd:].reshape(wr, 4 * hd)
    ggm = lax.dynamic_slice_in_dim(gsum.reshape(d), lax.axis_index(AXES) * wr, wr, 0)
    return block_out, dx, gga, gwq, gwk, gwv, gwo, ggm, own(gwg, fg), own(gwu, fu), own(gwd, fd)


def solution(mesh):
    dp, seq = mesh.shape["dp"], mesh.shape["seq"]
    m6 = Mesh(mesh.devices.reshape(dp // 2, 2, seq // 8, 2, 2, 2), AXES)
    row = P(AXES, None)
    vec = P(AXES)
    col = P(None, AXES)
    inner = jax.shard_map(
        functools.partial(local, nz=seq // 4, ndp=dp), mesh=m6,
        in_specs=(row, vec, row, row, row, row, vec, row, row, row, P(DP, None), row),
        out_specs=(row, row, vec, row, row, row, row, vec, row, row, row),
        check_vma=False,
    )

    def run(tokens, gain_attn, w_query, w_key, w_value, w_out, gain_mlp, w_gate, w_up, w_down, doc_ids, cotangent):
        outs = inner(tokens, gain_attn, w_query, w_key, w_value, w_out, gain_mlp, w_gate.T, w_up.T, w_down, doc_ids, cotangent)
        return outs[:8] + (outs[8].T, outs[9].T, outs[10])

    return run
```

```python
import functools

import jax
import jax.numpy as jnp
from jax import lax
from jax.experimental import pallas as pl
from jax.experimental.pallas import tpu as pltpu
from jax.sharding import Mesh, PartitionSpec as P

HEADS = 32
KV_HEADS = 4
HEAD_DIM = 64
GROUP = HEADS // KV_HEADS
NORM_EPS = 1e-05
MASKED = -1e30
AXES = ("dh", "dl", "zh", "zl", "x", "c")
T = ("x", "c")
Z = ("zh", "zl")
DP = ("dh", "dl")
CUBE = ("dl", "zl", "x", "c")
REST = ("dh", "zh")
BF = jnp.bfloat16
F32 = jnp.float32


def nn(a, b):
    return jnp.dot(a, b, preferred_element_type=F32)


def nt(a, b):
    return lax.dot_general(a, b, (((1,), (1,)), ((), ())), preferred_element_type=F32)


def tn(a, b):
    return lax.dot_general(a, b, (((0,), (0,)), ((), ())), preferred_element_type=F32)


def rotate(v, cos, sin, sign):
    h = v.shape[-1] // 2
    a, b = v[..., :h], v[..., h:]
    s = sin * sign
    return jnp.concatenate([a * cos - b * s, b * cos + a * s], axis=-1)


PARTS = ((0, 768), (768, 640), (1408, 640))
MESH = pl.DeviceIdType.MESH


def place():
    return {a: lax.axis_index(a) for a in AXES}


def other(at, *flip):
    return tuple(1 - at[a] if a in flip else at[a] for a in AXES)


def greet(at, partners):
    barrier = pltpu.get_barrier_semaphore()
    for flip in partners:
        pl.semaphore_signal(barrier, inc=1, device_id=other(at, *flip), device_id_type=MESH)
    pl.semaphore_wait(barrier, len(partners))


CDIMS = ("x", "zl", "dl")
MASKS = ((), ("x",), ("zl",), ("dl",), ("x", "zl"), ("zl", "dl"), ("dl", "x"), ("x", "zl", "dl"))


def cube_index(at, mask):
    return tuple(1 - at[a] if a in mask else at[a] for a in ("dl", "zl", "x"))


ORDERS = tuple(tuple(CDIMS[(p + s) % 3] for s in range(3)) for p in range(3))


class Log:
    def __init__(self):
        self.open = []

    def push(self, src, dst, ssem, rsem, device):
        cp = pltpu.make_async_remote_copy(src, dst, ssem, rsem, device_id=device, device_id_type=MESH)
        cp.start()
        self.open.append(cp)

    def close(self):
        for cp in self.open:
            cp.wait_send()


def landed(dst, sem, device):
    pltpu.make_async_remote_copy(dst, dst, sem, sem, device_id=device, device_id_type=MESH).wait_recv()


def at_z(at, o, n):
    i = lax.rem(at["zh"] * 2 + at["zl"] + o, n)
    return tuple(i // 2 if a == "zh" else lax.rem(i, 2) if a == "zl" else at[a] for a in AXES), i


def at_dp(at, o, n):
    i = lax.rem(at["dh"] * 2 + at["dl"] + o, n)
    return tuple(i // 2 if a == "dh" else lax.rem(i, 2) if a == "dl" else at[a] for a in AXES), i


def at_rest(at, o, n):
    i = lax.rem(at["dh"] * 2 + at["zh"] + o, n)
    return tuple(i // 2 if a == "dh" else lax.rem(i, 2) if a == "zh" else at[a] for a in AXES), i


def signal(device):
    pl.semaphore_signal(pltpu.get_barrier_semaphore(), inc=1, device_id=device, device_id_type=MESH)


def device_of(i, nz):
    t, j = lax.rem(i, 4), i // 4
    z, p = lax.rem(j, nz), j // nz
    return (p // 2, lax.rem(p, 2), z // 2, lax.rem(z, 2), t // 2, lax.rem(t, 2))


class Quad:
    def __init__(self, at, log, buf, ssem, rsem):
        self.at, self.log, self.buf, self.ssem, self.rsem = at, log, buf, ssem, rsem

    def start(self):
        at = self.at
        own = self.buf.at[at["x"], at["c"]]
        self.log.push(own, own, self.ssem.at[0], self.rsem.at[0], other(at, "x"))
        self.log.push(own, own, self.ssem.at[1], self.rsem.at[1], other(at, "c"))

    def forward(self):
        at = self.at
        far = self.buf.at[1 - at["x"], at["c"]]
        landed(far, self.rsem.at[0], other(at, "x"))
        self.log.push(far, far, self.ssem.at[2], self.rsem.at[2], other(at, "c"))

    def finish(self):
        at = self.at
        landed(self.buf.at[at["x"], 1 - at["c"]], self.rsem.at[1], other(at, "c"))
        landed(self.buf.at[1 - at["x"], 1 - at["c"]], self.rsem.at[2], other(at, "c"))


class QuadSum:
    def __init__(self, at, log, part, cin, xin, total, ssem, rsem, width):
        self.at, self.log, self.part, self.cin, self.xin, self.total = at, log, part, cin, xin, total
        self.ssem, self.rsem, self.width = ssem, rsem, width

    def cols(self, n):
        return slice(n * self.width, (n + 1) * self.width)

    def start(self, n):
        at, s = self.at, self.cols(n)
        self.log.push(self.part.at[:, 1 - at["c"], :, s], self.cin.at[:, :, s], self.ssem.at[0, n], self.rsem.at[0, n], other(at, "c"))

    def middle(self, n):
        at, s = self.at, self.cols(n)
        landed(self.cin.at[:, :, s], self.rsem.at[0, n], other(at, "c"))
        far = self.part.at[1 - at["x"], at["c"], :, s]
        far[...] = (far[...].astype(F32) + self.cin[1 - at["x"], :, s].astype(F32)).astype(BF)
        self.log.push(far, self.xin.at[:, s], self.ssem.at[1, n], self.rsem.at[1, n], other(at, "x"))
        near = self.part[at["x"], at["c"], :, s].astype(F32) + self.cin[at["x"], :, s].astype(F32)
        self.total[:, s] = self.total[:, s] + near

    def finish(self, n):
        s = self.cols(n)
        landed(self.xin.at[:, s], self.rsem.at[1, n], other(self.at, "x"))
        self.total[:, s] = self.total[:, s] + self.xin[:, s].astype(F32)


class Spread:
    def __init__(self, at, log, buf, nrest, parts, sems):
        self.at, self.log, self.buf, self.n, self.parts = at, log, buf, nrest, parts
        self.s0, self.r0, self.s1, self.r1 = sems

    def block(self, o, flip=(), part=None):
        at = self.at
        r = lax.rem(at["dh"] * (self.n_zh()) + at["zh"] + o, self.n)
        dh, zh = r // self.n_zh(), lax.rem(r, self.n_zh())
        dl = 1 - at["dl"] if "dl" in flip else at["dl"]
        zl = 1 - at["zl"] if "zl" in flip else at["zl"]
        ref = self.buf.at[dh * 2 + dl, zh * 2 + zl]
        if part is None:
            return ref
        lo, w = self.parts[part][:2]
        return ref.at[(slice(None),) * (len(ref.shape) - 1) + (slice(lo, lo + w),)]

    def n_zh(self):
        return self.buf.shape[1] // 2

    def start(self):
        for o in range(1, self.n):
            ref = self.block(0)
            self.log.push(ref, ref, self.s0.at[o - 1], self.r0.at[o - 1], at_rest(self.at, o, self.n)[0])

    def arrive(self, o):
        if o:
            landed(self.block(self.n - o), self.r0.at[o - 1], other(self.at, "zl"))

    def send(self, o, k, flip, part, dim):
        ref = self.block((self.n - o) % self.n, flip, part)
        self.log.push(ref, ref, self.s1.at[o, k], self.r1.at[o, k], other(self.at, dim))

    def take(self, o, k, flip, part):
        landed(self.block((self.n - o) % self.n, flip, part), self.r1.at[o, k], other(self.at, "zl"))

    def stage1(self, o):
        self.arrive(o)
        for p, (_, _, a, b) in enumerate(self.parts):
            self.send(o, 3 * p, (), p, a)
        for p, (_, _, a, b) in enumerate(self.parts):
            self.send(o, 3 * p + 1, (), p, b)

    def stage2(self, o):
        for p, (_, _, a, b) in enumerate(self.parts):
            self.take(o, 3 * p, (a,), p)
            self.send(o, 3 * p + 2, (a,), p, b)

    def finish(self, o):
        for p, (_, _, a, b) in enumerate(self.parts):
            self.take(o, 3 * p + 1, (b,), p)
            self.take(o, 3 * p + 2, (a, b), p)


class Merge:
    def __init__(self, at, log, buf, in1, in2, far, nrest, parts, sems):
        self.at, self.log, self.buf, self.in1, self.in2, self.far = at, log, buf, in1, in2, far
        self.n, self.parts = nrest, parts
        self.s0, self.r0, self.s1, self.r1 = sems

    def cut(self, ref, p):
        lo, w = self.parts[p][:2]
        return ref.at[(slice(None),) * (len(ref.shape) - 1) + (slice(lo, lo + w),)]

    def block(self, o, flip, p):
        at, nzh = self.at, self.buf.shape[1] // 2
        r = lax.rem(at["dh"] * nzh + at["zh"] + o, self.n)
        dl = 1 - at["dl"] if "dl" in flip else at["dl"]
        zl = 1 - at["zl"] if "zl" in flip else at["zl"]
        return self.cut(self.buf.at[(r // nzh) * 2 + dl, lax.rem(r, nzh) * 2 + zl], p)

    def stage1(self, o):
        for p, (_, _, a, b) in enumerate(self.parts):
            for k, flip in enumerate(((a, b), (a,))):
                self.log.push(self.block(o, flip, p), self.cut(self.in1.at[o, k], p), self.s1.at[o, 3 * p + k], self.r1.at[o, 3 * p + k],
                              other(self.at, a))

    def add(self, o, flip, p, ref):
        blk = self.block(o, flip, p)
        blk[...] = (blk[...].astype(F32) + ref[...].astype(F32)).astype(BF)

    def stage2(self, o):
        for p, (_, _, a, b) in enumerate(self.parts):
            src = self.cut(self.in1.at[o, 0], p)
            landed(src, self.r1.at[o, 3 * p], other(self.at, a))
            self.add(o, (b,), p, src)
            self.log.push(self.block(o, (b,), p), self.cut(self.in2.at[o], p), self.s1.at[o, 3 * p + 2], self.r1.at[o, 3 * p + 2],
                          other(self.at, b))
        for p, (_, _, a, b) in enumerate(self.parts):
            src = self.cut(self.in1.at[o, 1], p)
            landed(src, self.r1.at[o, 3 * p + 1], other(self.at, a))
            self.add(o, (), p, src)

    def stage3(self, o):
        for p, (_, _, a, b) in enumerate(self.parts):
            src = self.cut(self.in2.at[o], p)
            landed(src, self.r1.at[o, 3 * p + 2], other(self.at, b))
            self.add(o, (), p, src)
        if o:
            nzh = self.buf.shape[1] // 2
            at = self.at
            r = lax.rem(at["dh"] * nzh + at["zh"] + o, self.n)
            ref = self.buf.at[(r // nzh) * 2 + at["dl"], lax.rem(r, nzh) * 2 + at["zl"]]
            self.log.push(ref, self.far.at[o - 1], self.s0.at[o - 1], self.r0.at[o - 1], at_rest(at, o, self.n)[0])

    def result(self):
        at = self.at
        nzh = self.buf.shape[1] // 2
        total = self.buf[at["dh"] * 2 + at["dl"], at["zh"] * 2 + at["zl"]].astype(F32)
        for o in range(1, self.n):
            landed(self.far.at[o - 1], self.r0.at[o - 1], at_rest(at, self.n - o, self.n)[0])
            total = total + self.far[o - 1].astype(F32)
        return total


class AllSum:
    DIMS = ("c", "x", "dl", "zl")

    def __init__(self, at, log, val, got, nrest, ssem, rsem):
        self.at, self.log, self.val, self.got, self.n, self.ssem, self.rsem = at, log, val, got, nrest, ssem, rsem

    def start(self, k):
        if k < 4:
            self.log.push(self.val.at[k], self.got.at[k], self.ssem.at[k], self.rsem.at[k], other(self.at, self.DIMS[k]))
        else:
            for o in range(1, self.n):
                i = 3 + o
                self.log.push(self.val.at[4], self.got.at[i], self.ssem.at[i], self.rsem.at[i], at_rest(self.at, o, self.n)[0])

    def take(self, k):
        if k < 4:
            landed(self.got.at[k], self.rsem.at[k], other(self.at, self.DIMS[k]))
            self.val[k + 1] = self.val[k] + self.got[k]
            return None
        total = self.val[4]
        for o in range(1, self.n):
            i = 3 + o
            landed(self.got.at[i], self.rsem.at[i], other(self.at, "c"))
            total = total + self.got[i]
        return total


class Pushes:
    def __init__(self, at, log, nrest, src, dst, ssem, rsem, back):
        self.args = at, log, nrest, src, dst, ssem, rsem, back

    def start(self):
        at, log, n, src, dst, ssem, rsem, back = self.args
        for o in range(1, n):
            dev, _ = at_rest(at, n - o if back else o, n)
            log.push(src(o), dst.at[o - 1], ssem.at[o - 1], rsem.at[o - 1], dev)

    def finish(self):
        at, log, n, src, dst, ssem, rsem, back = self.args
        for o in range(1, n):
            landed(dst.at[o - 1], rsem.at[o - 1], at_rest(at, o if back else n - o, n)[0])


class Gather:
    def __init__(self, at, buf, ssem, rsem, csend, crecv):
        self.at, self.buf, self.ssem, self.rsem, self.csend, self.crecv = at, buf, ssem, rsem, csend, crecv
        self.rows = buf.shape[3] // 2
        self.open = []

    def block(self, mask, core, p=None):
        i = cube_index(self.at, mask)
        r = pl.ds(pl.multiple_of(core * self.rows, self.rows), self.rows)
        if p is None:
            return self.buf.at[i[0], i[1], i[2], r, :]
        lo, w = PARTS[p]
        return self.buf.at[i[0], i[1], i[2], r, lo:lo + w]

    def send(self, p, mask, dim):
        ref = self.block(mask, self.at["c"], p)
        k = MASKS.index(tuple(a for a in mask_sorted(mask + (dim,))))
        cp = pltpu.make_async_remote_copy(ref, ref, self.ssem.at[p, k], self.rsem.at[p, k],
                                          device_id=other(self.at, dim), device_id_type=MESH)
        cp.start()
        self.open.append(cp)

    def arrived(self, p, mask):
        k = MASKS.index(mask)
        ref = self.block(mask, self.at["c"], p)
        pltpu.make_async_remote_copy(ref, ref, self.ssem.at[p, k], self.rsem.at[p, k],
                                     device_id=other(self.at, "x"), device_id_type=MESH).wait_recv()

    def pass_on(self, mask):
        k = MASKS.index(mask)
        ref = self.block(mask, self.at["c"])
        cp = pltpu.make_async_remote_copy(ref, ref, self.csend.at[k], self.crecv.at[k],
                                          device_id=other(self.at, "c"), device_id_type=MESH)
        cp.start()
        self.open.append(cp)

    def sibling_arrived(self, mask):
        k = MASKS.index(mask)
        ref = self.block(mask, 1 - self.at["c"])
        pltpu.make_async_remote_copy(ref, ref, self.csend.at[k], self.crecv.at[k],
                                     device_id=other(self.at, "c"), device_id_type=MESH).wait_recv()

    def first(self):
        for p in range(3):
            self.send(p, (), ORDERS[p][0])
        self.pass_on(())

    def second(self):
        for p in range(3):
            a, b, _ = ORDERS[p]
            self.send(p, (), b)
        for p in range(3):
            a, b, _ = ORDERS[p]
            self.arrived(p, (a,))
            self.send(p, (a,), b)

    def third(self):
        for p in range(3):
            a, b, c = ORDERS[p]
            self.send(p, (), c)
        for p in range(3):
            a, b, c = ORDERS[p]
            self.send(p, (a,), c)
        for p in range(3):
            a, b, c = ORDERS[p]
            self.arrived(p, (b,))
            self.send(p, (b,), c)
        for p in range(3):
            a, b, c = ORDERS[p]
            self.arrived(p, mask_sorted((a, b)))
            self.send(p, mask_sorted((a, b)), c)

    def complete(self, mask):
        for p in range(3):
            if ORDERS[p][2] in mask:
                self.arrived(p, mask)

    def close(self):
        for cp in self.open:
            cp.wait_send()


def mask_sorted(mask):
    for m in MASKS:
        if set(m) == set(mask):
            return m
    raise ValueError(mask)


class Scatter:
    def __init__(self, at, full, core_in, r0, r1, r2, ssem, rsem):
        self.at, self.full, self.core_in, self.r = at, full, core_in, (r0, r1, r2)
        self.ssem, self.rsem = ssem, rsem
        self.rows = r2.shape[0]
        self.open = []

    def own(self, core):
        if self.full.shape[3] == self.rows:
            return slice(None)
        return pl.ds(pl.multiple_of(core * self.rows, self.rows), self.rows)

    def core_copy(self, p):
        lo, w = PARTS[p]
        return pltpu.make_async_remote_copy(
            self.full.at[:, :, :, self.own(1 - self.at["c"]), lo:lo + w], self.core_in.at[:, :, :, :, lo:lo + w],
            self.ssem.at[p, 3], self.rsem.at[p, 3], device_id=other(self.at, "c"), device_id_type=MESH)

    def stage_copy(self, p, s):
        lo, w = PARTS[p]
        dims = ORDERS[p]
        ix = []
        for a in ("dl", "zl", "x"):
            if a == dims[s]:
                ix.append(1 - self.at[a])
            elif a in dims[:s]:
                ix.append(self.at[a])
            else:
                ix.append(slice(None))
        dst = self.r[s]
        dst = dst.at[(slice(None),) * (len(dst.shape) - 1) + (slice(lo, lo + w),)]
        return pltpu.make_async_remote_copy(
            self.full.at[ix[0], ix[1], ix[2], self.own(self.at["c"]), lo:lo + w], dst,
            self.ssem.at[p, s], self.rsem.at[p, s], device_id=other(self.at, dims[s]), device_id_type=MESH)

    def start(self, cp):
        cp.start()
        self.open.append(cp)

    def blocks(self, p, s):
        dims = ORDERS[p]
        rest = dims[s:]
        out = []
        for m in MASKS:
            if set(m) <= set(rest):
                out.append(m)
        if rest:
            out.sort(key=lambda m: 0 if rest[0] in m else 1)
        return out

    def add_core(self, p, go=True):
        cp = self.core_copy(p)
        cp.wait_recv()
        self.add_loop(p, 0, None)
        if go:
            self.start(self.stage_copy(p, 0))
        self.add_loop(p, 0, None, tail=True)

    def add_loop(self, p, s, src, tail=False):
        lo, w = PARTS[p]
        dims = ORDERS[p]
        for m in self.blocks(p, s):
            first = s < 3 and dims[s] in m
            if first == tail:
                continue
            i = cube_index(self.at, m)
            ref = self.full.at[i[0], i[1], i[2], self.own(self.at["c"]), lo:lo + w]
            if src is None:
                val = self.core_in[i[0], i[1], i[2], :, lo:lo + w]
            else:
                ix = [j for a, j in zip(("dl", "zl", "x"), i) if a in dims[s:]]
                val = src[tuple(ix) + (slice(None), slice(lo, lo + w))]
            ref[...] = (ref[...].astype(F32) + val.astype(F32)).astype(BF)

    def step(self, p, s):
        self.stage_copy(p, s).wait_recv()
        self.add_loop(p, s + 1, self.r[s])
        if s < 2:
            self.start(self.stage_copy(p, s + 1))
            self.add_loop(p, s + 1, self.r[s], tail=True)

    def finish(self, p, out, base=None):
        lo, w = PARTS[p]
        self.stage_copy(p, 2).wait_recv()
        i = cube_index(self.at, ())
        ref = self.full.at[i[0], i[1], i[2], self.own(self.at["c"]), lo:lo + w]
        total = ref[...].astype(F32) + self.r[2][:, lo:lo + w].astype(F32)
        if base is not None:
            total = total + base[:, lo:lo + w]
        out[:, lo:lo + w] = total.astype(out.dtype)

    def close(self):
        for cp in self.open:
            cp.wait_send()


def mlp_kernel(nrest, m_ref, gain_ref, cot_ref, wg_own, wu_own, wd_own, wg_far, wu_far, down_out, dn2_out, gwd_out, gwg_out, gwu_out, fd_out,
               rows, wgu, wd, gus, zb, dgu, fa, fb, core_in, a0, a1, a2,
               lsem, gs, gr, gcs, gcr, sas, sar, sbs, sbr, s_wd, r_wd, s_fd, r_fd, credit):
    at = place()
    log = Log()
    units = wd.shape[0]
    brows = m_ref.shape[0]
    part = wd_own.shape[0]
    far = units - part
    copies = [pltpu.make_async_copy(wd_own, wd.at[:part, :], lsem.at[4])]
    for k, (own_w, far_w, lo) in enumerate(((wg_own, wg_far, 0), (wu_own, wu_far, units))):
        copies.append(pltpu.make_async_copy(own_w, wgu.at[lo:lo + part, :], lsem.at[2 * k]))
        copies.append(pltpu.make_async_copy(far_w, wgu.at[lo + part:lo + units, :], lsem.at[2 * k + 1]))
    for cp in copies:
        cp.start()
    for flip in ("c", "x", "zl", "dl"):
        signal(other(at, flip))
    for o in range(1, nrest):
        signal(at_rest(at, o, nrest)[0])
    g = Gather(at, rows, gs, gr, gcs, gcr)
    own = pl.ds(pl.multiple_of(at["c"] * brows, brows), brows)
    m = m_ref[...]
    inv = lax.rsqrt(jnp.mean(m * m, axis=1, keepdims=True) + NORM_EPS)
    rows[at["dl"], at["zl"], at["x"], own, :] = (m * inv * gain_ref[...]).astype(BF)
    pl.semaphore_wait(pltpu.get_barrier_semaphore(), 3 + nrest)
    g.first()
    for o in range(1, nrest):
        log.push(wd_own, wd.at[o * part:(o + 1) * part, :], s_wd.at[o - 1], r_wd.at[o - 1], at_rest(at, o, nrest)[0])
    for cp in copies:
        cp.wait()

    def swiglu(i, gate, up, dz, lo, hi):
        sg = jax.nn.sigmoid(gate)
        sl = gate * sg
        zb[i[0], i[1], i[2], lo:hi, :] = (sl * up).astype(BF)
        dgu[i[0], i[1], i[2], lo:hi, :] = (dz * up * (sg * (1.0 + gate * (1.0 - sg)))).astype(BF)
        dgu[i[0], i[1], i[2], units + lo:units + hi, :] = (dz * sl).astype(BF)

    def units_of(mask):
        i = cube_index(at, mask)
        gu = nt(wgu[...], rows[i[0], i[1], i[2]])
        dz = nt(wd[:part, :], cot_ref[i[0], i[1], i[2]])
        gate, up = gu[:units], gu[units:]
        gus[i[0], i[1], i[2], :far, :] = gate[part:]
        gus[i[0], i[1], i[2], far:, :] = up[part:]
        swiglu(i, gate[:part], up[:part], dz, 0, part)

    g.second()
    g.sibling_arrived(())
    units_of(())
    g.third()
    last = None
    for k in MASKS[1:]:
        g.complete(k)
        g.pass_on(k)
        if last is not None:
            g.sibling_arrived(last)
            units_of(last)
        last = k
    g.sibling_arrived(last)
    units_of(last)
    for o in range(1, nrest):
        landed(wd.at[o * part:(o + 1) * part, :], r_wd.at[o - 1], at_rest(at, nrest - o, nrest)[0])

    @pl.loop(0, 8)
    def _(q):
        i = (q // 4, (q // 2) % 2, q % 2)
        dz = nt(wd[part:, :], cot_ref[i[0], i[1], i[2]])
        swiglu(i, gus[i[0], i[1], i[2], :far, :], gus[i[0], i[1], i[2], far:, :], dz, part, units)

    def partial(dst, lhs, rhs, p):
        lo, w = PARTS[p]

        @pl.loop(0, 8)
        def _(q):
            a, b, c = q // 4, (q // 2) % 2, q % 2
            dst[a, b, c, :, lo:lo + w] = tn(lhs[a, b, c], rhs[:, lo:lo + w]).astype(BF)

    cw = 512

    def grads(lhs, rhs, outs):
        @pl.loop(0, rows.shape[4] // cw)
        def _(n):
            s = pl.ds(pl.multiple_of(n * cw, cw), cw)
            acc = None
            for q in range(8):
                a, b, c = q // 4, (q // 2) % 2, q % 2
                v = nn(lhs[a, b, c], rhs[a, b, c, :, s])
                acc = v if acc is None else acc + v
            for k, o in enumerate(outs):
                o[:, s] = acc[k * units:(k + 1) * units].astype(BF)

    sa = Scatter(at, fa, core_in, a0, a1, a2, sas, sar)
    sb = Scatter(at, fb, core_in, a0, a1, a2, sbs, sbr)
    for p in range(3):
        partial(fa, dgu, wgu, p)
        sa.start(sa.core_copy(p))
        if p:
            sa.add_core(p - 1)
    sa.add_core(2)
    pl.semaphore_signal(credit, inc=1, device_id=other(at, "c"), device_id_type=MESH)
    grads(zb, cot_ref, (gwd_out,))
    for o in range(1, nrest):
        log.push(gwd_out.at[o * part:(o + 1) * part, :], fd_out.at[o - 1], s_fd.at[o - 1], r_fd.at[o - 1], at_rest(at, nrest - o, nrest)[0])
    partial(fb, zb, wd, 0)
    for p in range(3):
        sa.step(p, 0)
    pl.semaphore_wait(credit, 1)
    sb.start(sb.core_copy(0))
    for p in range(1, 3):
        partial(fb, zb, wd, p)
        sb.start(sb.core_copy(p))
    for p in range(3):
        sa.step(p, 1)
    for p in range(3):
        sb.add_core(p, go=False)
    save = pltpu.make_async_copy(fb.at[:, :, :, own, :], down_out, lsem.at[5])
    save.start()
    for p in range(3):
        sa.finish(p, dn2_out)
    grads(dgu, rows, (gwg_out, gwu_out))
    save.wait()
    for o in range(1, nrest):
        landed(fd_out.at[o - 1], r_fd.at[o - 1], at_rest(at, o, nrest)[0])
    g.close()
    sa.close()
    sb.close()
    log.close()


def mlp(nrest, m, gain, cot_all, own, far):
    rows, d = m.shape
    far = tuple(a.reshape(-1, d) for a in far)
    part = own[0].shape[0]
    units = part * nrest
    vm = pl.BlockSpec(memory_space=pltpu.VMEM)
    hbm = pl.BlockSpec(memory_space=pl.ANY)
    cube = (2, 2, 2)
    dma = pltpu.SemaphoreType.DMA
    sd = jax.ShapeDtypeStruct
    nf = max(nrest - 1, 1)
    return pl.pallas_call(
        functools.partial(mlp_kernel, nrest),
        out_shape=(sd(cube + (rows, d), BF), sd((rows, d), F32)) + (sd((units, d), BF),) * 3 + (sd((nrest - 1, part, d), BF),),
        in_specs=[vm, vm, vm] + [hbm] * 5,
        out_specs=(hbm,) + (vm,) * 4 + (hbm,),
        scratch_shapes=[
            pltpu.VMEM(cube + (2 * rows, d), BF),
            pltpu.VMEM((2 * units, d), BF),
            pltpu.VMEM((units, d), BF),
            pltpu.VMEM(cube + (2 * (units - part), 2 * rows), F32),
            pltpu.VMEM(cube + (units, 2 * rows), BF),
            pltpu.VMEM(cube + (2 * units, 2 * rows), BF),
            pltpu.VMEM(cube + (2 * rows, d), BF),
            pltpu.VMEM(cube + (2 * rows, d), BF),
            pltpu.VMEM(cube + (rows, d), BF),
            pltpu.VMEM((2, 2, rows, d), BF), pltpu.VMEM((2, rows, d), BF), pltpu.VMEM((rows, d), BF),
            dma((6,)), dma((3, 8)), dma((3, 8)), dma((8,)), dma((8,)),
            dma((3, 4)), dma((3, 4)), dma((3, 4)), dma((3, 4)), dma((nf,)), dma((nf,)), dma((nf,)), dma((nf,)), pltpu.SemaphoreType.REGULAR,
        ],
        compiler_params=pltpu.CompilerParams(collective_id=1, has_side_effects=True, vmem_limit_bytes=63 * 2**20),
        name="mlp",
    )(m, gain, cot_all, *own, *far)


def rot_rows(v, cos, sin):
    h = v.shape[0] // 2
    a, b = v[:h], v[h:]
    return jnp.concatenate([a * cos - b * sin, b * cos + a * sin], axis=0)


def attn_kernel(nz, ndp, tok_ref, wpack, wout_ref, gpack, cos_ref, sin_ref, start_ref, cot_ref, wg_ref, wu_ref,
                m_out, q_out, kv_out, o_out, lse_out, xg_out, wqkv_out, wo_out, gain_out, cot_out, wg_out, wu_out,
                xg, wbuf, wobuf, gbuf, kvbuf, qbuf, kn, vt, obuf, lbuf, bias, part, cin, xin, total,
                lsem, s_disp, r_disp, s_gd, r_gd, s_w0, r_w0, s_w1, r_w1, s_g0, r_g0, s_g1, r_g1, s_o0, r_o0, s_o1, r_o1,
                s_od, r_od, s_x, r_x, s_kv, r_kv, s_p, r_p, s_rest, r_rest, gs, gr, gcs, gcr):
    at = place()
    log = Log()
    rows, d = tok_ref.shape
    hd = HEAD_DIM
    zi = at["zh"] * 2 + at["zl"]
    di = at["dh"] * 2 + at["dl"]
    t = at["x"] * 2 + at["c"]
    nrest = nz * ndp // 4
    wr = wpack.shape[1]
    quad = (("c",), ("x",), ("x", "c"))
    npeers = nz * ndp
    lin = (di * nz + zi) * 4 + t
    target = lax.rem(lin, npeers) * 4 + lin // npeers
    source = lax.rem(lin, 4) * npeers + lin // 4
    for f in quad:
        signal(other(at, *f))
    signal(other(at, "zl"))
    signal(other(at, "dl"))
    for o in range(1, nrest):
        signal(at_rest(at, o, nrest)[0])

    @pl.when(source != lin)
    def _():
        signal(device_of(source, nz))

    pl.semaphore_wait(pltpu.get_barrier_semaphore(), 4 + nrest + (target != lin).astype(jnp.int32))
    g = Gather(at, cot_out, gs, gr, gcs, gcr)
    here = [pltpu.make_async_copy(cot_ref, g.block((), at["c"]), lsem.at[0])]
    for cp in here:
        cp.start()
    for k, f in enumerate(quad):
        dev = other(at, *f)
        tt = dev[4] * 2 + dev[5]
        log.push(wpack.at[tt], wbuf.at[di, zi, pl.ds(pl.multiple_of(t * wr, wr), wr), :], s_disp.at[k], r_disp.at[k], dev)
        log.push(gpack, gbuf.at[di, zi, t], s_gd.at[k], r_gd.at[k], dev)
    wbuf[di, zi, pl.ds(pl.multiple_of(t * wr, wr), wr), :] = wpack[t]
    gbuf[di, zi, t] = gpack[...]
    x = tok_ref[...].astype(F32)
    inv = lax.rsqrt(jnp.mean(x * x, axis=1, keepdims=True) + NORM_EPS)
    xg[at["x"], at["c"]] = (x * inv).astype(BF)
    total[...] = x
    qx = Quad(at, log, xg, s_x, r_x)
    qx.start()
    for k, f in enumerate(quad):
        dev = other(at, *f)
        tt = dev[4] * 2 + dev[5]
        landed(wbuf.at[di, zi, pl.ds(pl.multiple_of(tt * wr, wr), wr), :], r_disp.at[k], dev)
        landed(gbuf.at[di, zi, tt], r_gd.at[k], dev)
    sw = Spread(at, log, wbuf, nrest, ((0, wbuf.shape[3], "zl", "dl"),), (s_w0, r_w0, s_w1, r_w1))
    sg = Spread(at, log, gbuf, nrest, ((0, 128, "zl", "dl"),), (s_g0, r_g0, s_g1, r_g1))
    so = Spread(at, log, wobuf, nrest, ((0, d, "zl", "dl"),), (s_o0, r_o0, s_o1, r_o1))
    for sp in (sw, sg):
        sp.start()
        sp.stage1(0)
    qx.forward()
    here[0].wait()
    @pl.when(target != lin)
    def _():
        pltpu.make_async_remote_copy(wout_ref, wobuf.at[lax.rem(lin, npeers) // nz, lax.rem(lax.rem(lin, npeers), nz)], s_od, r_od,
                                     device_id=device_of(target, nz), device_id_type=MESH).start()

    @pl.when(target == lin)
    def _():
        wobuf[di, zi] = wout_ref[...]

    qn = bias.shape[2]
    nq = bias.shape[0]
    keys = bias.shape[1]
    kpos = lax.broadcasted_iota(jnp.int32, (keys, qn), 0)
    for b in range(nq):
        qpos = zi * (4 * rows) + b * qn + lax.broadcasted_iota(jnp.int32, (1, qn), 1)
        first = start_ref[:, b * qn:(b + 1) * qn]
        bias[b] = jnp.where((kpos >= first) & (kpos <= qpos), 0.0, MASKED)
    for sp in (sw, sg):
        sp.stage2(0)
    for o in range(1, nrest):
        for sp in (sw, sg):
            sp.stage1(o)
    swaps = [Pushes(at, log, nrest, (lambda o, a=a: a), b, s_rest.at[k], r_rest.at[k], False)
             for k, (a, b) in enumerate(((wg_ref, wg_out), (wu_ref, wu_out)))]
    for o in range(1, nrest):
        for sp in (sw, sg):
            sp.stage2(o)
    @pl.when(source != lin)
    def _():
        pltpu.make_async_remote_copy(wobuf.at[di, zi], wobuf.at[di, zi], s_od, r_od,
                                     device_id=device_of(source, nz), device_id_type=MESH).wait_recv()

    so.start()
    so.stage1(0)
    for o in range(nrest):
        for sp in (sw, sg):
            sp.finish(o)
    g.first()
    qx.finish()
    xa = xg[...].reshape(4 * rows, d)
    qkv = jnp.transpose(nn(xa, wbuf[...].reshape(d, wbuf.shape[3])))
    cos, sin = cos_ref[...], sin_ref[...]
    kvbuf[zi, :hd, :] = rot_rows(qkv[GROUP * hd:(GROUP + 1) * hd], cos, sin).astype(BF)
    kvbuf[zi, hd:, :] = qkv[(GROUP + 1) * hd:].astype(BF)
    nzh = nz // 2
    for o in range(1, nzh):
        log.push(kvbuf.at[zi], kvbuf.at[zi], s_kv.at[0, o], r_kv.at[0, o], at_z(at, 2 * o, nz)[0])
    log.push(kvbuf.at[zi], kvbuf.at[zi], s_kv.at[1, 0], r_kv.at[1, 0], other(at, "zl"))
    for h in range(GROUP):
        qbuf[h] = (rot_rows(qkv[h * hd:(h + 1) * hd], cos, sin).astype(BF) * 0.125).astype(BF)

    save = [pltpu.make_async_copy(xg, xg_out, lsem.at[4]), pltpu.make_async_copy(wbuf, wqkv_out, lsem.at[5]),
            pltpu.make_async_copy(gbuf, gain_out, lsem.at[6]), pltpu.make_async_copy(qbuf, q_out, lsem.at[7])]
    for cp in save:
        cp.start()
    for o in range(1, nzh):
        dev, i = at_z(at, nz - 2 * o, nz)
        landed(kvbuf.at[i], r_kv.at[0, o], dev)
        log.push(kvbuf.at[i], kvbuf.at[i], s_kv.at[1, o], r_kv.at[1, o], other(at, "zl"))
    for o in range(nzh):
        landed(kvbuf.at[zi], r_kv.at[1, o], other(at, "zl"))
    g.second()
    swaps[0].start()
    swaps[1].start()
    save.append(pltpu.make_async_copy(kvbuf, kv_out, lsem.at[8]))
    save[-1].start()
    tl = kvbuf.shape[2]
    for i in range(nz):
        kn[i * tl:(i + 1) * tl, :] = jnp.transpose(kvbuf[i, :hd, :].astype(F32)).astype(BF)
        vt[:hd, i * tl:(i + 1) * tl] = kvbuf[i, hd:, :]
    vt[hd:, :] = jnp.ones((vt.shape[0] - hd, keys), BF)

    def heads(b, lo, hi):
        @pl.loop(lo, hi)
        def _(h):
            s = nn(kn[...], qbuf[h, :, b * qn:(b + 1) * qn]) + bias[b]
            mx = jnp.max(s, axis=0, keepdims=True)
            e = jnp.exp(s - mx).astype(BF)
            oe = nn(vt[...], e)
            tot = oe[hd:hd + 1]
            obuf[h, :, b * qn:(b + 1) * qn] = (oe[:hd] / tot).astype(BF)
            lbuf[h, :, b * qn:(b + 1) * qn] = mx + jnp.log(tot)

    so.stage2(0)
    for o in range(1, nrest):
        so.stage1(o)
    heads(0, 0, 4)
    g.third()
    heads(0, 4, 8)
    for o in range(1, nrest):
        so.stage2(o)
    heads(1, 0, 4)
    heads(1, 4, 8)
    for m in MASKS[1:4]:
        g.complete(m)
        g.pass_on(m)
    for o in range(nrest):
        so.finish(o)
    save += [pltpu.make_async_copy(wobuf, wo_out, lsem.at[9]), pltpu.make_async_copy(obuf, o_out, lsem.at[10]),
             pltpu.make_async_copy(lbuf, lse_out, lsem.at[11])]
    for cp in save[-3:]:
        cp.start()
    cw = 512
    nc = d // cw
    oT = obuf[...].reshape(GROUP * hd, 4 * rows)
    red = QuadSum(at, log, part, cin, xin, total, s_p, r_p, cw)
    for n in range(nc):
        s = slice(n * cw, (n + 1) * cw)
        wo = wobuf[:, :, :, s].reshape(GROUP * hd, cw)
        part[:, :, :, s] = tn(oT, wo).astype(BF).reshape(2, 2, rows, cw)
        red.start(n)
        if n:
            red.middle(n - 1)
    red.middle(nc - 1)
    for m in MASKS[4:]:
        g.complete(m)
        g.pass_on(m)
    for n in range(nc):
        red.finish(n)
    m_out[...] = total[...]
    for m in MASKS:
        g.sibling_arrived(m)
    for sw_ in swaps:
        sw_.finish()
    for cp in save:
        cp.wait()

    @pl.when(target != lin)
    def _():
        pltpu.make_async_remote_copy(wout_ref, wobuf.at[di, zi], s_od, r_od,
                                     device_id=device_of(target, nz), device_id_type=MESH).wait_send()

    g.close()
    log.close()


def attn(nz, ndp, tokens, wpack, w_out, gpack, cosT, sinT, starts, cot, wg, wu):
    rows, d = tokens.shape
    wr, wc = wpack.shape[1:]
    hd = HEAD_DIM
    units = wg.shape[0]
    nrest = nz * ndp // 4
    keys = nz * 4 * rows
    qn = 2 * rows
    vm = pl.BlockSpec(memory_space=pltpu.VMEM)
    hbm = pl.BlockSpec(memory_space=pl.ANY)
    dma = pltpu.SemaphoreType.DMA
    sd = jax.ShapeDtypeStruct
    sh = dict(
        xg=(2, 2, rows, d), w=(ndp, nz, 4 * wr, wc), wo=(ndp, nz, wr, d), g=(ndp, nz, 4, 16, 128),
        kv=(nz, 2 * hd, 4 * rows), q=(GROUP, hd, 4 * rows), lse=(GROUP, 1, 4 * rows))
    outs = (sd((rows, d), F32), sd(sh["q"], BF), sd(sh["kv"], BF), sd(sh["q"], BF), sd(sh["lse"], F32), sd(sh["xg"], BF),
            sd(sh["w"], BF), sd(sh["wo"], BF), sd(sh["g"], BF), sd((2, 2, 2, 2 * rows, d), BF)) + (sd((nrest - 1, units, d), BF),) * 2
    nq = 4 * rows // qn
    zz = (max(nrest - 1, 1),)
    return pl.pallas_call(
        functools.partial(attn_kernel, nz, ndp),
        out_shape=outs,
        in_specs=[vm] * 8 + [hbm] * 2,
        out_specs=(vm,) + (hbm,) * (len(outs) - 1),
        scratch_shapes=[
            pltpu.VMEM(sh["xg"], BF), pltpu.VMEM(sh["w"], BF), pltpu.VMEM(sh["wo"], BF), pltpu.VMEM(sh["g"], BF),
            pltpu.VMEM(sh["kv"], BF), pltpu.VMEM(sh["q"], BF), pltpu.VMEM((keys, hd), BF), pltpu.VMEM((hd + 16, keys), BF),
            pltpu.VMEM(sh["q"], BF), pltpu.VMEM(sh["lse"], F32), pltpu.VMEM((nq, keys, qn), F32),
            pltpu.VMEM((2, 2, rows, d), BF), pltpu.VMEM((2, rows, d), BF), pltpu.VMEM((rows, d), BF), pltpu.VMEM((rows, d), F32),
            dma((12,)), dma((3,)), dma((3,)), dma((3,)), dma((3,))] + [dma((nrest,)), dma((nrest,)), dma((nrest, 6)), dma((nrest, 6))] * 3 + [
            dma, dma, dma((3,)), dma((3,)), dma((2, nz // 2)), dma((2, nz // 2)), dma((2, 4)), dma((2, 4)),
            dma((2, nrest)), dma((2, nrest)), dma((3, 8)), dma((3, 8)), dma((8,)), dma((8,)),
        ],
        compiler_params=pltpu.CompilerParams(collective_id=2, has_side_effects=True, vmem_limit_bytes=58 * 2**20),
        name="attention",
    )(tokens, wpack, w_out, gpack, cosT, sinT, starts, cot, wg, wu)


def back_kernel(nz, ndp, m_ref, dn2_ref, gain_ref, cot_ref, tok_ref, cos_ref, sin_ref, start_ref,
                xg_in, wqkv_in, wo_in, q_in, kv_in, o_in, lse_in, down_in, gg_in, gu_in,
                dx_out, block_out, gq_out, gkv_out, gwo_out, gain_out, fg_out, fu_out,
                xg, wqkv, wo, qbuf, kvbuf, obuf, lbuf, dag, dob, delta, kn, vn, kt, bias, dkv, dqb, kvp, kvin, dqkv,
                gob, go1, go2, gof, gqb, gq1, gq2, gqf, gkb, gk1, gk2, gkf, gsend, gpart, part, cin, xin, total, ogot, val, got, fb, b0, b1, b2,
                lsem, s_x, r_x, s_o0, r_o0, s_o1, r_o1, s_q0, r_q0, s_q1, r_q1, s_k0, r_k0, s_k1, r_k1,
                s_kv, r_kv, s_p, r_p, s_rest, r_rest, s_od, r_od, s_gq, r_gq, s_gk, r_gk, s_v, r_v, s_b, r_b):
    at = place()
    log = Log()
    rows, d = m_ref.shape
    hd = HEAD_DIM
    qc = GROUP * hd
    zi = at["zh"] * 2 + at["zl"]
    di = at["dh"] * 2 + at["dl"]
    t = at["x"] * 2 + at["c"]
    nrest = nz * ndp // 4
    npeers = nz * ndp
    nzh = nz // 2
    wr = gwo_out.shape[0]
    keys = kn.shape[0]
    tl = 4 * rows
    lin = (di * nz + zi) * 4 + t
    target = lax.rem(lin, npeers) * 4 + lin // npeers
    source = lax.rem(lin, 4) * npeers + lin // 4
    loads = [pltpu.make_async_copy(a, b, lsem.at[k]) for k, (a, b) in enumerate((
        (kv_in, kvbuf), (wo_in, wo), (o_in, obuf), (q_in, qbuf), (lse_in, lbuf), (down_in, fb), (xg_in, xg), (wqkv_in, wqkv)))]
    for cp in loads:
        cp.start()
    quad = (("c",), ("x",), ("x", "c"))
    for f in quad:
        signal(other(at, *f))
    signal(other(at, "zl"))
    signal(other(at, "dl"))
    for o in range(1, nrest):
        signal(at_rest(at, o, nrest)[0])

    @pl.when(target != lin)
    def _():
        signal(device_of(target, nz))

    m = m_ref[...]
    inv2 = lax.rsqrt(jnp.mean(m * m, axis=1, keepdims=True) + NORM_EPS)
    mh = m * inv2
    dn2 = dn2_ref[...].astype(F32)
    dy = dn2 * gain_ref[...]
    dm = cot_ref[...].astype(F32) + inv2 * (dy - mh * jnp.mean(dy * mh, axis=1, keepdims=True))
    dx_out[...] = dm
    dag[at["x"], at["c"]] = dm.astype(BF)
    total[...] = jnp.zeros_like(total)
    gsum = jnp.sum(dn2 * mh, axis=0, keepdims=True)
    for i in range(d // 128):
        val[0, i:i + 1, :] = gsum[:, i * 128:(i + 1) * 128]
    pl.semaphore_wait(pltpu.get_barrier_semaphore(), 4 + nrest + (source != lin).astype(jnp.int32))
    qx = Quad(at, log, dag, s_x, r_x)
    qx.start()
    gs = AllSum(at, log, val, got, nrest, s_v, r_v)
    gs.start(0)
    units = fg_out.shape[1]
    swaps = [Pushes(at, log, nrest, (lambda o, a=a: a.at[pl.ds(o * units, units), :]), c, s_rest.at[k], r_rest.at[k], True)
             for k, (a, c) in enumerate(((gg_in, fg_out), (gu_in, fu_out)))]
    swaps[0].start()
    swaps[1].start()
    loads[0].wait()
    for i in range(nz):
        kn[i * tl:(i + 1) * tl, :] = jnp.transpose(kvbuf[i, :hd, :].astype(F32)).astype(BF)
        vn[i * tl:(i + 1) * tl, :] = jnp.transpose(kvbuf[i, hd:, :].astype(F32)).astype(BF)
        kt[:, i * tl:(i + 1) * tl] = kvbuf[i, :hd, :]
    kpos = lax.broadcasted_iota(jnp.int32, (keys, tl), 0)
    qpos = zi * tl + lax.broadcasted_iota(jnp.int32, (1, tl), 1)
    bias[...] = jnp.where((kpos >= start_ref[...]) & (kpos <= qpos), 0.0, MASKED)
    dkv[...] = jnp.zeros_like(dkv)
    for cp in loads[1:]:
        cp.wait()
    gs.take(0)
    gs.start(1)
    qx.forward()
    sb = Scatter(at, fb, None, b0, b1, b2, s_b, r_b)
    for p in range(3):
        sb.start(sb.stage_copy(p, 0))
    qx.finish()
    da = dag[...].reshape(tl, d)
    doT = nt(wo[...].reshape(qc, d), da).astype(BF)
    dob[...] = doT.reshape(GROUP, hd, tl)
    delta[...] = jnp.sum((dob[...].astype(F32) * obuf[...].astype(F32)), axis=1, keepdims=True)
    gs.take(1)
    gs.start(2)
    cw = 512
    oT = obuf[...].reshape(qc, tl)
    for n in range(d // cw):
        s = slice(n * cw, (n + 1) * cw)
        gob[:, :, :, s] = nn(oT, dag[:, :, :, s].reshape(tl, cw)).astype(BF).reshape(ndp, nz, wr, cw)
    mo = Merge(at, log, gob, go1, go2, gof, nrest, ((0, d // 2, "dl", "zl"), (d // 2, d // 2, "zl", "dl")), (s_o0, r_o0, s_o1, r_o1))
    far_first = tuple(range(1, nrest)) + (0,)
    for o in far_first:
        mo.stage1(o)

    def heads(lo, hi):
        @pl.loop(lo, hi)
        def _(h):
            qT, dT = qbuf[h], dob[h]
            p = jnp.exp(nn(kn[...], qT) + bias[...] - lbuf[h])
            ds = (p * (nn(vn[...], dT) - delta[h])).astype(BF)
            pb = p.astype(BF)
            dkv[:hd, :] += nt(qT, ds)
            dkv[hd:, :] += nt(dT, pb)
            dqb[pl.ds(pl.multiple_of(h * hd, hd), hd), :] = rot_rows(nn(kt[...], ds) * 0.125, cos_ref[...], -sin_ref[...])

    heads(0, 3)
    for p in range(3):
        sb.step(p, 0)
    gs.take(2)
    gs.start(3)
    for o in far_first:
        mo.stage2(o)
    heads(3, 6)
    for p in range(3):
        sb.step(p, 1)
    gs.take(3)
    gs.start(4)
    for o in far_first:
        mo.stage3(o)
    heads(6, 8)
    for p in range(3):
        sb.finish(p, block_out, m_ref)
    for i in range(nz):
        kvp[i] = dkv[:, i * tl:(i + 1) * tl].astype(BF)
    for o in range(1, nz):
        dev, i = at_z(at, o, nz)
        log.push(kvp.at[i], kvin.at[o - 1], s_kv.at[o - 1], r_kv.at[o - 1], dev)
    dqkv[:, :qc] = jnp.transpose(dqb[...]).astype(BF)
    mq = Merge(at, log, gqb, gq1, gq2, gqf, nrest, ((0, qc // 2, "dl", "zl"), (qc // 2, qc // 2, "zl", "dl")), (s_q0, r_q0, s_q1, r_q1))
    mk = Merge(at, log, gkb, gk1, gk2, gkf, nrest, ((0, 2 * hd, "dl", "zl"),), (s_k0, r_k0, s_k1, r_k1))

    def weight_grad(dst, lo, hi):
        step = 256
        per = step // (4 * wr)
        for n in range(d // step):
            xs = xg[:, :, :, n * step:(n + 1) * step].reshape(tl, step)
            v = tn(xs, dqkv[:, lo:hi]).astype(BF)
            for b in range(per):
                f = n * per + b
                dst[f // nz, f % nz] = v[b * 4 * wr:(b + 1) * 4 * wr]

    weight_grad(gqb, 0, qc)
    for o in far_first:
        mq.stage1(o)
    acc = dkv[:, pl.ds(pl.multiple_of(zi * tl, tl), tl)]
    for o in range(1, nz):
        dev, _ = at_z(at, nz - o, nz)
        landed(kvin.at[o - 1], r_kv.at[o - 1], dev)
        acc = acc + kvin[o - 1].astype(F32)
    dk = rot_rows(acc[:hd], cos_ref[...], -sin_ref[...])
    dqkv[:, qc:] = jnp.transpose(jnp.concatenate([dk, acc[hd:]], axis=0)).astype(BF)
    weight_grad(gkb, qc, qc + 2 * hd)
    for o in far_first:
        mk.stage1(o)
    red = QuadSum(at, log, part, cin, xin, total, s_p, r_p, cw)
    w = wqkv[...].reshape(d, qc + 2 * hd)
    nc = d // cw
    for n in range(nc):
        part[:, :, :, n * cw:(n + 1) * cw] = nt(dqkv[...], w[n * cw:(n + 1) * cw]).astype(BF).reshape(2, 2, rows, cw)
        red.start(n)
        if n:
            red.middle(n - 1)
    for o in far_first:
        mq.stage2(o)
    red.middle(nc - 1)
    for o in far_first:
        mk.stage2(o)
    for o in far_first:
        mq.stage3(o)
    for o in far_first:
        mk.stage3(o)
    gsend[...] = mo.result().astype(BF)

    @pl.when(source != lin)
    def _():
        pltpu.make_async_remote_copy(gsend, ogot, s_od, r_od, device_id=device_of(source, nz), device_id_type=MESH).start()

    @pl.when(source == lin)
    def _():
        ogot[...] = gsend[...]

    for n in range(nc):
        red.finish(n)
    x = tok_ref[...].astype(F32)
    inv1 = lax.rsqrt(jnp.mean(x * x, axis=1, keepdims=True) + NORM_EPS)
    xh = x * inv1
    dy1 = total[...]
    dx_out[...] = dx_out[...] + inv1 * (dy1 - xh * jnp.mean(dy1 * xh, axis=1, keepdims=True))
    gain_out[...] = gs.take(4)
    for merge, dst, sp, ss, rs, lo, hi in ((mq, gq_out, gpart.at[:, :qc], s_gq, r_gq, 0, qc), (mk, gkv_out, gpart.at[:, qc:], s_gk, r_gk, qc, qc + 2 * hd)):
        gpart[:, lo:hi] = merge.result().astype(BF)
        dst[t] = gpart[pl.ds(pl.multiple_of(t * wr, wr), wr), lo:hi]
        for k, f in enumerate(quad):
            dev = other(at, *f)
            tt = dev[4] * 2 + dev[5]
            log.push(gpart.at[pl.ds(pl.multiple_of(tt * wr, wr), wr), lo:hi], dst.at[t], ss.at[k], rs.at[k], dev)
    @pl.when(target != lin)
    def _():
        pltpu.make_async_remote_copy(gsend, ogot, s_od, r_od, device_id=device_of(target, nz), device_id_type=MESH).wait_recv()

    gwo_out[...] = ogot[...].astype(F32)
    for dst, rs in ((gq_out, r_gq), (gkv_out, r_gk)):
        for k, f in enumerate(quad):
            dev = other(at, *f)
            tt = dev[4] * 2 + dev[5]
            landed(dst.at[tt], rs.at[k], dev)
    for sw_ in swaps:
        sw_.finish()

    @pl.when(source != lin)
    def _():
        pltpu.make_async_remote_copy(gsend, ogot, s_od, r_od, device_id=device_of(source, nz), device_id_type=MESH).wait_send()

    sb.close()
    log.close()


def back(nz, ndp, m, dn2, gain, cot, tokens, cosT, sinT, starts, xg, wqkv, wo, q, kv, o, lse, down, grads):
    rows, d = m.shape
    hd = HEAD_DIM
    qc = GROUP * hd
    nrest = nz * ndp // 4
    wr = wo.shape[2]
    keys = nz * 4 * rows
    tl = 4 * rows
    units = grads[0].shape[0] // nrest
    vm = pl.BlockSpec(memory_space=pltpu.VMEM)
    hbm = pl.BlockSpec(memory_space=pl.ANY)
    dma = pltpu.SemaphoreType.DMA
    sd = jax.ShapeDtypeStruct
    nf = max(nrest - 1, 1)
    outs = (sd((rows, d), F32), sd((rows, d), BF), sd((4, wr, qc), BF), sd((4, wr, 2 * hd), BF), sd((wr, d), F32), sd((16, 128), F32)) + (
        sd((nrest - 1, units, d), BF),) * 2
    V = pltpu.VMEM

    def merge_bufs(r, c):
        return [V((ndp, nz, r, c), BF), V((nrest, 2, r, c), BF), V((nrest, r, c), BF), V((nf, r, c), BF)]

    return pl.pallas_call(
        functools.partial(back_kernel, nz, ndp),
        out_shape=outs,
        in_specs=[vm] * 8 + [hbm] * 10,
        out_specs=(vm,) * 6 + (hbm,) * 2,
        scratch_shapes=[
            V(xg.shape, BF), V(wqkv.shape, BF), V(wo.shape, BF), V(q.shape, BF), V(kv.shape, BF), V(o.shape, BF), V(lse.shape, F32),
            V((2, 2, rows, d), BF), V(q.shape, BF), V(lse.shape, F32), V((keys, hd), BF), V((keys, hd), BF), V((hd, keys), BF),
            V((keys, tl), F32), V((2 * hd, keys), F32), V((qc, tl), F32), V(kv.shape, BF), V((max(nz - 1, 1), 2 * hd, tl), BF),
            V((tl, qc + 2 * hd), BF)]
        + merge_bufs(wr, d) + merge_bufs(4 * wr, qc) + merge_bufs(4 * wr, 2 * hd) + [
            V((wr, d), BF), V((4 * wr, qc + 2 * hd), BF), V((2, 2, rows, d), BF), V((2, rows, d), BF), V((rows, d), BF), V((rows, d), F32),
            V((wr, d), BF), V((5, 16, 128), F32), V((4 + nf, 16, 128), F32),
            V(down.shape, BF), V((2, 2, rows, d), BF), V((2, rows, d), BF), V((rows, d), BF),
            dma((8,)), dma((3,)), dma((3,))] + [dma((nf,)), dma((nf,)), dma((nrest, 6)), dma((nrest, 6))] * 3 + [
            dma((nz,)), dma((nz,)), dma((2, 4)), dma((2, 4)), dma((2, nrest)), dma((2, nrest)), dma, dma, dma((3,)), dma((3,)), dma((3,)), dma((3,)),
            dma((4 + nf,)), dma((4 + nf,)), dma((3, 4)), dma((3, 4))],
        compiler_params=pltpu.CompilerParams(collective_id=3, has_side_effects=True, vmem_limit_bytes=62 * 2**20),
        name="backward",
    )(m, dn2, gain, cot, tokens, cosT, sinT, starts, xg, wqkv, wo, q, kv, o, lse, down, *grads)


def local(tokens, gain_attn, w_query, w_key, w_value, w_out, gain_mlp, w_gate_t, w_up_t, w_down, doc_ids, cotangent, nz, ndp):
    rows, d = tokens.shape
    wr = w_query.shape[0]
    grows = rows * 4
    seq_ids = doc_ids[0]
    length = seq_ids.shape[0]
    zi = lax.axis_index(Z)
    hd = HEAD_DIM
    qc = GROUP * hd
    ga = gain_attn.astype(F32)[:, None]
    wall = jnp.concatenate([w_query.reshape(wr, 4, qc), w_key.reshape(wr, 4, hd), w_value.reshape(wr, 4, hd)], axis=2).transpose(1, 0, 2)
    wpack = (wall.astype(F32) * ga[None]).astype(BF)
    gpack = jnp.pad(gain_mlp[None], ((0, 15), (0, 128 - wr)))
    first = zi * grows
    own_ids = lax.dynamic_slice_in_dim(seq_ids, first, grows, 0)
    qpos = first + jnp.arange(grows, dtype=jnp.int32)
    starts = jnp.sum((seq_ids[:, None] < own_ids[None, :]).astype(jnp.int32), axis=0)
    freq = 10000.0 ** (-jnp.arange(hd // 2, dtype=F32) / (hd // 2))
    ph = (qpos - starts).astype(F32)[None, :] * freq[:, None]
    cosT, sinT = jnp.cos(ph), jnp.sin(ph)
    units = w_down.shape[0]
    fill = -units % 16
    if fill:
        w_gate_t, w_up_t, w_down = (jnp.pad(w, ((0, fill), (0, 0))) for w in (w_gate_t, w_up_t, w_down))
    m, q, kv, o, lse, xg, wqkv, wo, gains, cot_all, wgt, wut = attn(
        nz, ndp, tokens, wpack, w_out, gpack, cosT, sinT, starts[None], cotangent, w_gate_t, w_up_t)
    gm = gains[:, :, :, 0, :wr].reshape(1, d).astype(F32)
    down, dn2, gwd, gwg, gwu, fd = mlp(nz * ndp // 4, m, gm, cot_all, (w_gate_t, w_up_t, w_down), (wgt, wut))
    dx, block_out, gq, gkv, gwo, gsum, fg, fu = back(
        nz, ndp, m, dn2, gm, cotangent, tokens, cosT, sinT, starts[None], xg, wqkv, wo, q, kv, o, lse, down, (gwg, gwu))

    def own(a, far):
        return (a[:units + fill].astype(F32) + jnp.sum(far.astype(F32), axis=0))[:units]

    gw = jnp.concatenate([gq, gkv], axis=2).astype(F32)
    gga = jnp.sum(gw * wall.astype(F32), axis=(0, 2))
    gw = (gw * ga[None]).transpose(1, 0, 2)
    gwq = gw[:, :, :qc].reshape(wr, 4 * qc)
    gwk = gw[:, :, qc:qc + hd].reshape(wr, 4 * hd)
    gwv = gw[:, :, qc + hd:].reshape(wr, 4 * hd)
    ggm = lax.dynamic_slice_in_dim(gsum.reshape(d), lax.axis_index(AXES) * wr, wr, 0)
    return block_out, dx, gga, gwq, gwk, gwv, gwo, ggm, own(gwg, fg), own(gwu, fu), own(gwd, fd)


def solution(mesh):
    dp, seq = mesh.shape["dp"], mesh.shape["seq"]
    m6 = Mesh(mesh.devices.reshape(dp // 2, 2, seq // 8, 2, 2, 2), AXES)
    row = P(AXES, None)
    vec = P(AXES)
    col = P(None, AXES)
    inner = jax.shard_map(
        functools.partial(local, nz=seq // 4, ndp=dp), mesh=m6,
        in_specs=(row, vec, row, row, row, row, vec, row, row, row, P(DP, None), row),
        out_specs=(row, row, vec, row, row, row, row, vec, row, row, row),
        check_vma=False,
    )

    def run(tokens, gain_attn, w_query, w_key, w_value, w_out, gain_mlp, w_gate, w_up, w_down, doc_ids, cotangent):
        outs = inner(tokens, gain_attn, w_query, w_key, w_value, w_out, gain_mlp, w_gate.T, w_up.T, w_down, doc_ids, cotangent)
        return outs[:8] + (outs[8].T, outs[9].T, outs[10])

    return run
```

```python
import functools

import jax
import jax.numpy as jnp
from jax import lax
from jax.experimental import pallas as pl
from jax.experimental.pallas import tpu as pltpu
from jax.sharding import Mesh, PartitionSpec as P

HEADS = 32
KV_HEADS = 4
HEAD_DIM = 64
GROUP = HEADS // KV_HEADS
NORM_EPS = 1e-05
MASKED = -1e30
AXES = ("dh", "dl", "zh", "zl", "x", "c")
T = ("x", "c")
Z = ("zh", "zl")
DP = ("dh", "dl")
CUBE = ("dl", "zl", "x", "c")
REST = ("dh", "zh")
BF = jnp.bfloat16
F32 = jnp.float32


def nn(a, b):
    return jnp.dot(a, b, preferred_element_type=F32)


def nt(a, b):
    return lax.dot_general(a, b, (((1,), (1,)), ((), ())), preferred_element_type=F32)


def tn(a, b):
    return lax.dot_general(a, b, (((0,), (0,)), ((), ())), preferred_element_type=F32)


def rotate(v, cos, sin, sign):
    h = v.shape[-1] // 2
    a, b = v[..., :h], v[..., h:]
    s = sin * sign
    return jnp.concatenate([a * cos - b * s, b * cos + a * s], axis=-1)


PARTS = ((0, 768), (768, 640), (1408, 640))
MESH = pl.DeviceIdType.MESH


def place():
    return {a: lax.axis_index(a) for a in AXES}


def other(at, *flip):
    return tuple(1 - at[a] if a in flip else at[a] for a in AXES)


def greet(at, partners):
    barrier = pltpu.get_barrier_semaphore()
    for flip in partners:
        pl.semaphore_signal(barrier, inc=1, device_id=other(at, *flip), device_id_type=MESH)
    pl.semaphore_wait(barrier, len(partners))


CDIMS = ("x", "zl", "dl")
MASKS = ((), ("x",), ("zl",), ("dl",), ("x", "zl"), ("zl", "dl"), ("dl", "x"), ("x", "zl", "dl"))


def cube_index(at, mask):
    return tuple(1 - at[a] if a in mask else at[a] for a in ("dl", "zl", "x"))


ORDERS = tuple(tuple(CDIMS[(p + s) % 3] for s in range(3)) for p in range(3))


class Log:
    def __init__(self):
        self.open = []

    def push(self, src, dst, ssem, rsem, device):
        cp = pltpu.make_async_remote_copy(src, dst, ssem, rsem, device_id=device, device_id_type=MESH)
        cp.start()
        self.open.append(cp)

    def close(self):
        for cp in self.open:
            cp.wait_send()


def landed(dst, sem, device):
    pltpu.make_async_remote_copy(dst, dst, sem, sem, device_id=device, device_id_type=MESH).wait_recv()


def at_z(at, o, n):
    i = lax.rem(at["zh"] * 2 + at["zl"] + o, n)
    return tuple(i // 2 if a == "zh" else lax.rem(i, 2) if a == "zl" else at[a] for a in AXES), i


def at_dp(at, o, n):
    i = lax.rem(at["dh"] * 2 + at["dl"] + o, n)
    return tuple(i // 2 if a == "dh" else lax.rem(i, 2) if a == "dl" else at[a] for a in AXES), i


def at_rest(at, o, n):
    i = lax.rem(at["dh"] * 2 + at["zh"] + o, n)
    return tuple(i // 2 if a == "dh" else lax.rem(i, 2) if a == "zh" else at[a] for a in AXES), i


def signal(device):
    pl.semaphore_signal(pltpu.get_barrier_semaphore(), inc=1, device_id=device, device_id_type=MESH)


def device_of(i, nz):
    t, j = lax.rem(i, 4), i // 4
    z, p = lax.rem(j, nz), j // nz
    return (p // 2, lax.rem(p, 2), z // 2, lax.rem(z, 2), t // 2, lax.rem(t, 2))


class Quad:
    def __init__(self, at, log, buf, ssem, rsem):
        self.at, self.log, self.buf, self.ssem, self.rsem = at, log, buf, ssem, rsem

    def start(self):
        at = self.at
        own = self.buf.at[at["x"], at["c"]]
        self.log.push(own, own, self.ssem.at[0], self.rsem.at[0], other(at, "x"))
        self.log.push(own, own, self.ssem.at[1], self.rsem.at[1], other(at, "c"))

    def forward(self):
        at = self.at
        far = self.buf.at[1 - at["x"], at["c"]]
        landed(far, self.rsem.at[0], other(at, "x"))
        self.log.push(far, far, self.ssem.at[2], self.rsem.at[2], other(at, "c"))

    def finish(self):
        at = self.at
        landed(self.buf.at[at["x"], 1 - at["c"]], self.rsem.at[1], other(at, "c"))
        landed(self.buf.at[1 - at["x"], 1 - at["c"]], self.rsem.at[2], other(at, "c"))


class QuadSum:
    def __init__(self, at, log, part, cin, xin, total, ssem, rsem, width):
        self.at, self.log, self.part, self.cin, self.xin, self.total = at, log, part, cin, xin, total
        self.ssem, self.rsem, self.width = ssem, rsem, width

    def cols(self, n):
        return slice(n * self.width, (n + 1) * self.width)

    def start(self, n):
        at, s = self.at, self.cols(n)
        self.log.push(self.part.at[:, 1 - at["c"], :, s], self.cin.at[:, :, s], self.ssem.at[0, n], self.rsem.at[0, n], other(at, "c"))

    def middle(self, n):
        at, s = self.at, self.cols(n)
        landed(self.cin.at[:, :, s], self.rsem.at[0, n], other(at, "c"))
        far = self.part.at[1 - at["x"], at["c"], :, s]
        far[...] = (far[...].astype(F32) + self.cin[1 - at["x"], :, s].astype(F32)).astype(BF)
        self.log.push(far, self.xin.at[:, s], self.ssem.at[1, n], self.rsem.at[1, n], other(at, "x"))
        near = self.part[at["x"], at["c"], :, s].astype(F32) + self.cin[at["x"], :, s].astype(F32)
        self.total[:, s] = self.total[:, s] + near

    def finish(self, n):
        s = self.cols(n)
        landed(self.xin.at[:, s], self.rsem.at[1, n], other(self.at, "x"))
        self.total[:, s] = self.total[:, s] + self.xin[:, s].astype(F32)


class Spread:
    def __init__(self, at, log, buf, nrest, parts, sems):
        self.at, self.log, self.buf, self.n, self.parts = at, log, buf, nrest, parts
        self.s0, self.r0, self.s1, self.r1 = sems

    def block(self, o, flip=(), part=None):
        at = self.at
        r = lax.rem(at["dh"] * (self.n_zh()) + at["zh"] + o, self.n)
        dh, zh = r // self.n_zh(), lax.rem(r, self.n_zh())
        dl = 1 - at["dl"] if "dl" in flip else at["dl"]
        zl = 1 - at["zl"] if "zl" in flip else at["zl"]
        ref = self.buf.at[dh * 2 + dl, zh * 2 + zl]
        if part is None:
            return ref
        lo, w = self.parts[part][:2]
        return ref.at[(slice(None),) * (len(ref.shape) - 1) + (slice(lo, lo + w),)]

    def n_zh(self):
        return self.buf.shape[1] // 2

    def start(self):
        for o in range(1, self.n):
            ref = self.block(0)
            self.log.push(ref, ref, self.s0.at[o - 1], self.r0.at[o - 1], at_rest(self.at, o, self.n)[0])

    def arrive(self, o):
        if o:
            landed(self.block(self.n - o), self.r0.at[o - 1], other(self.at, "zl"))

    def send(self, o, k, flip, part, dim):
        ref = self.block((self.n - o) % self.n, flip, part)
        self.log.push(ref, ref, self.s1.at[o, k], self.r1.at[o, k], other(self.at, dim))

    def take(self, o, k, flip, part):
        landed(self.block((self.n - o) % self.n, flip, part), self.r1.at[o, k], other(self.at, "zl"))

    def stage1(self, o):
        self.arrive(o)
        for p, (_, _, a, b) in enumerate(self.parts):
            self.send(o, 3 * p, (), p, a)
        for p, (_, _, a, b) in enumerate(self.parts):
            self.send(o, 3 * p + 1, (), p, b)

    def stage2(self, o):
        for p, (_, _, a, b) in enumerate(self.parts):
            self.take(o, 3 * p, (a,), p)
            self.send(o, 3 * p + 2, (a,), p, b)

    def finish(self, o):
        for p, (_, _, a, b) in enumerate(self.parts):
            self.take(o, 3 * p + 1, (b,), p)
            self.take(o, 3 * p + 2, (a, b), p)


class Merge:
    def __init__(self, at, log, buf, in1, in2, far, nrest, parts, sems):
        self.at, self.log, self.buf, self.in1, self.in2, self.far = at, log, buf, in1, in2, far
        self.n, self.parts = nrest, parts
        self.s0, self.r0, self.s1, self.r1 = sems

    def cut(self, ref, p):
        lo, w = self.parts[p][:2]
        return ref.at[(slice(None),) * (len(ref.shape) - 1) + (slice(lo, lo + w),)]

    def block(self, o, flip, p):
        at, nzh = self.at, self.buf.shape[1] // 2
        r = lax.rem(at["dh"] * nzh + at["zh"] + o, self.n)
        dl = 1 - at["dl"] if "dl" in flip else at["dl"]
        zl = 1 - at["zl"] if "zl" in flip else at["zl"]
        return self.cut(self.buf.at[(r // nzh) * 2 + dl, lax.rem(r, nzh) * 2 + zl], p)

    def stage1(self, o):
        for p, (_, _, a, b) in enumerate(self.parts):
            for k, flip in enumerate(((a, b), (a,))):
                self.log.push(self.block(o, flip, p), self.cut(self.in1.at[o, k], p), self.s1.at[o, 3 * p + k], self.r1.at[o, 3 * p + k],
                              other(self.at, a))

    def add(self, o, flip, p, ref):
        blk = self.block(o, flip, p)
        blk[...] = (blk[...].astype(F32) + ref[...].astype(F32)).astype(BF)

    def stage2(self, o):
        for p, (_, _, a, b) in enumerate(self.parts):
            src = self.cut(self.in1.at[o, 0], p)
            landed(src, self.r1.at[o, 3 * p], other(self.at, a))
            self.add(o, (b,), p, src)
            self.log.push(self.block(o, (b,), p), self.cut(self.in2.at[o], p), self.s1.at[o, 3 * p + 2], self.r1.at[o, 3 * p + 2],
                          other(self.at, b))
        for p, (_, _, a, b) in enumerate(self.parts):
            src = self.cut(self.in1.at[o, 1], p)
            landed(src, self.r1.at[o, 3 * p + 1], other(self.at, a))
            self.add(o, (), p, src)

    def stage3(self, o):
        for p, (_, _, a, b) in enumerate(self.parts):
            src = self.cut(self.in2.at[o], p)
            landed(src, self.r1.at[o, 3 * p + 2], other(self.at, b))
            self.add(o, (), p, src)
        if o:
            nzh = self.buf.shape[1] // 2
            at = self.at
            r = lax.rem(at["dh"] * nzh + at["zh"] + o, self.n)
            ref = self.buf.at[(r // nzh) * 2 + at["dl"], lax.rem(r, nzh) * 2 + at["zl"]]
            self.log.push(ref, self.far.at[o - 1], self.s0.at[o - 1], self.r0.at[o - 1], at_rest(at, o, self.n)[0])

    def result(self):
        at = self.at
        nzh = self.buf.shape[1] // 2
        total = self.buf[at["dh"] * 2 + at["dl"], at["zh"] * 2 + at["zl"]].astype(F32)
        for o in range(1, self.n):
            landed(self.far.at[o - 1], self.r0.at[o - 1], at_rest(at, self.n - o, self.n)[0])
            total = total + self.far[o - 1].astype(F32)
        return total


class AllSum:
    DIMS = ("c", "x", "dl", "zl")

    def __init__(self, at, log, val, got, nrest, ssem, rsem):
        self.at, self.log, self.val, self.got, self.n, self.ssem, self.rsem = at, log, val, got, nrest, ssem, rsem

    def start(self, k):
        if k < 4:
            self.log.push(self.val.at[k], self.got.at[k], self.ssem.at[k], self.rsem.at[k], other(self.at, self.DIMS[k]))
        else:
            for o in range(1, self.n):
                i = 3 + o
                self.log.push(self.val.at[4], self.got.at[i], self.ssem.at[i], self.rsem.at[i], at_rest(self.at, o, self.n)[0])

    def take(self, k):
        if k < 4:
            landed(self.got.at[k], self.rsem.at[k], other(self.at, self.DIMS[k]))
            self.val[k + 1] = self.val[k] + self.got[k]
            return None
        total = self.val[4]
        for o in range(1, self.n):
            i = 3 + o
            landed(self.got.at[i], self.rsem.at[i], other(self.at, "c"))
            total = total + self.got[i]
        return total


class Pushes:
    def __init__(self, at, log, nrest, src, dst, ssem, rsem, back):
        self.args = at, log, nrest, src, dst, ssem, rsem, back

    def start(self):
        at, log, n, src, dst, ssem, rsem, back = self.args
        for o in range(1, n):
            dev, _ = at_rest(at, n - o if back else o, n)
            log.push(src(o), dst.at[o - 1], ssem.at[o - 1], rsem.at[o - 1], dev)

    def finish(self):
        at, log, n, src, dst, ssem, rsem, back = self.args
        for o in range(1, n):
            landed(dst.at[o - 1], rsem.at[o - 1], at_rest(at, o if back else n - o, n)[0])


class Gather:
    def __init__(self, at, buf, ssem, rsem, csend, crecv):
        self.at, self.buf, self.ssem, self.rsem, self.csend, self.crecv = at, buf, ssem, rsem, csend, crecv
        self.rows = buf.shape[3] // 2
        self.open = []

    def block(self, mask, core, p=None):
        i = cube_index(self.at, mask)
        r = pl.ds(pl.multiple_of(core * self.rows, self.rows), self.rows)
        if p is None:
            return self.buf.at[i[0], i[1], i[2], r, :]
        lo, w = PARTS[p]
        return self.buf.at[i[0], i[1], i[2], r, lo:lo + w]

    def send(self, p, mask, dim):
        ref = self.block(mask, self.at["c"], p)
        k = MASKS.index(tuple(a for a in mask_sorted(mask + (dim,))))
        cp = pltpu.make_async_remote_copy(ref, ref, self.ssem.at[p, k], self.rsem.at[p, k],
                                          device_id=other(self.at, dim), device_id_type=MESH)
        cp.start()
        self.open.append(cp)

    def arrived(self, p, mask):
        k = MASKS.index(mask)
        ref = self.block(mask, self.at["c"], p)
        pltpu.make_async_remote_copy(ref, ref, self.ssem.at[p, k], self.rsem.at[p, k],
                                     device_id=other(self.at, "x"), device_id_type=MESH).wait_recv()

    def pass_on(self, mask):
        k = MASKS.index(mask)
        ref = self.block(mask, self.at["c"])
        cp = pltpu.make_async_remote_copy(ref, ref, self.csend.at[k], self.crecv.at[k],
                                          device_id=other(self.at, "c"), device_id_type=MESH)
        cp.start()
        self.open.append(cp)

    def sibling_arrived(self, mask):
        k = MASKS.index(mask)
        ref = self.block(mask, 1 - self.at["c"])
        pltpu.make_async_remote_copy(ref, ref, self.csend.at[k], self.crecv.at[k],
                                     device_id=other(self.at, "c"), device_id_type=MESH).wait_recv()

    def first(self):
        for p in range(3):
            self.send(p, (), ORDERS[p][0])
        self.pass_on(())

    def second(self):
        for p in range(3):
            a, b, _ = ORDERS[p]
            self.send(p, (), b)
        for p in range(3):
            a, b, _ = ORDERS[p]
            self.arrived(p, (a,))
            self.send(p, (a,), b)

    def third(self):
        for p in range(3):
            a, b, c = ORDERS[p]
            self.send(p, (), c)
        for p in range(3):
            a, b, c = ORDERS[p]
            self.send(p, (a,), c)
        for p in range(3):
            a, b, c = ORDERS[p]
            self.arrived(p, (b,))
            self.send(p, (b,), c)
        for p in range(3):
            a, b, c = ORDERS[p]
            self.arrived(p, mask_sorted((a, b)))
            self.send(p, mask_sorted((a, b)), c)

    def complete(self, mask):
        for p in range(3):
            if ORDERS[p][2] in mask:
                self.arrived(p, mask)

    def close(self):
        for cp in self.open:
            cp.wait_send()


def mask_sorted(mask):
    for m in MASKS:
        if set(m) == set(mask):
            return m
    raise ValueError(mask)


class Scatter:
    def __init__(self, at, full, core_in, r0, r1, r2, ssem, rsem):
        self.at, self.full, self.core_in, self.r = at, full, core_in, (r0, r1, r2)
        self.ssem, self.rsem = ssem, rsem
        self.rows = r2.shape[0]
        self.open = []

    def own(self, core):
        if self.full.shape[3] == self.rows:
            return slice(None)
        return pl.ds(pl.multiple_of(core * self.rows, self.rows), self.rows)

    def core_copy(self, p):
        lo, w = PARTS[p]
        return pltpu.make_async_remote_copy(
            self.full.at[:, :, :, self.own(1 - self.at["c"]), lo:lo + w], self.core_in.at[:, :, :, :, lo:lo + w],
            self.ssem.at[p, 3], self.rsem.at[p, 3], device_id=other(self.at, "c"), device_id_type=MESH)

    def stage_copy(self, p, s):
        lo, w = PARTS[p]
        dims = ORDERS[p]
        ix = []
        for a in ("dl", "zl", "x"):
            if a == dims[s]:
                ix.append(1 - self.at[a])
            elif a in dims[:s]:
                ix.append(self.at[a])
            else:
                ix.append(slice(None))
        dst = self.r[s]
        dst = dst.at[(slice(None),) * (len(dst.shape) - 1) + (slice(lo, lo + w),)]
        return pltpu.make_async_remote_copy(
            self.full.at[ix[0], ix[1], ix[2], self.own(self.at["c"]), lo:lo + w], dst,
            self.ssem.at[p, s], self.rsem.at[p, s], device_id=other(self.at, dims[s]), device_id_type=MESH)

    def start(self, cp):
        cp.start()
        self.open.append(cp)

    def blocks(self, p, s):
        dims = ORDERS[p]
        rest = dims[s:]
        out = []
        for m in MASKS:
            if set(m) <= set(rest):
                out.append(m)
        if rest:
            out.sort(key=lambda m: 0 if rest[0] in m else 1)
        return out

    def add_core(self, p, go=True):
        cp = self.core_copy(p)
        cp.wait_recv()
        self.add_loop(p, 0, None)
        if go:
            self.start(self.stage_copy(p, 0))
        self.add_loop(p, 0, None, tail=True)

    def add_loop(self, p, s, src, tail=False):
        lo, w = PARTS[p]
        dims = ORDERS[p]
        for m in self.blocks(p, s):
            first = s < 3 and dims[s] in m
            if first == tail:
                continue
            i = cube_index(self.at, m)
            ref = self.full.at[i[0], i[1], i[2], self.own(self.at["c"]), lo:lo + w]
            if src is None:
                val = self.core_in[i[0], i[1], i[2], :, lo:lo + w]
            else:
                ix = [j for a, j in zip(("dl", "zl", "x"), i) if a in dims[s:]]
                val = src[tuple(ix) + (slice(None), slice(lo, lo + w))]
            ref[...] = (ref[...].astype(F32) + val.astype(F32)).astype(BF)

    def step(self, p, s):
        self.stage_copy(p, s).wait_recv()
        self.add_loop(p, s + 1, self.r[s])
        if s < 2:
            self.start(self.stage_copy(p, s + 1))
            self.add_loop(p, s + 1, self.r[s], tail=True)

    def finish(self, p, out, base=None):
        lo, w = PARTS[p]
        self.stage_copy(p, 2).wait_recv()
        i = cube_index(self.at, ())
        ref = self.full.at[i[0], i[1], i[2], self.own(self.at["c"]), lo:lo + w]
        total = ref[...].astype(F32) + self.r[2][:, lo:lo + w].astype(F32)
        if base is not None:
            total = total + base[:, lo:lo + w]
        out[:, lo:lo + w] = total.astype(out.dtype)

    def close(self):
        for cp in self.open:
            cp.wait_send()


def mlp_kernel(nrest, m_ref, gain_ref, cot_in, wg_own, wu_own, wd_own, wg_far, wu_far, down_out, dn2_out, gwd_out, gwg_out, gwu_out, fd_out,
               cot_ref, rows, wgu, wd, gus, zb, dgu, fa, fb, core_in, a0, a1, a2,
               lsem, gs, gr, gcs, gcr, sas, sar, sbs, sbr, s_wd, r_wd, s_fd, r_fd, credit):
    at = place()
    log = Log()
    units = wd.shape[0]
    brows = m_ref.shape[0]
    part = wd_own.shape[0]
    far = units - part
    copies = [pltpu.make_async_copy(wd_own, wd.at[:part, :], lsem.at[4])]
    for k, (own_w, far_w, lo) in enumerate(((wg_own, wg_far, 0), (wu_own, wu_far, units))):
        copies.append(pltpu.make_async_copy(own_w, wgu.at[lo:lo + part, :], lsem.at[2 * k]))
        copies.append(pltpu.make_async_copy(far_w, wgu.at[lo + part:lo + units, :], lsem.at[2 * k + 1]))
    copies.append(pltpu.make_async_copy(cot_in, cot_ref, lsem.at[6]))
    for cp in copies:
        cp.start()
    for flip in ("c", "x", "zl", "dl"):
        signal(other(at, flip))
    for o in range(1, nrest):
        signal(at_rest(at, o, nrest)[0])
    g = Gather(at, rows, gs, gr, gcs, gcr)
    own = pl.ds(pl.multiple_of(at["c"] * brows, brows), brows)
    m = m_ref[...]
    inv = lax.rsqrt(jnp.mean(m * m, axis=1, keepdims=True) + NORM_EPS)
    rows[at["dl"], at["zl"], at["x"], own, :] = (m * inv * gain_ref[...]).astype(BF)
    pl.semaphore_wait(pltpu.get_barrier_semaphore(), 3 + nrest)
    g.first()
    for o in range(1, nrest):
        log.push(wd_own, wd.at[o * part:(o + 1) * part, :], s_wd.at[o - 1], r_wd.at[o - 1], at_rest(at, o, nrest)[0])
    for cp in copies:
        cp.wait()

    def swiglu(i, gate, up, dz, lo, hi):
        sg = jax.nn.sigmoid(gate)
        sl = gate * sg
        zb[i[0], i[1], i[2], lo:hi, :] = (sl * up).astype(BF)
        dgu[i[0], i[1], i[2], lo:hi, :] = (dz * up * (sg * (1.0 + gate * (1.0 - sg)))).astype(BF)
        dgu[i[0], i[1], i[2], units + lo:units + hi, :] = (dz * sl).astype(BF)

    def units_of(mask):
        i = cube_index(at, mask)
        gu = nt(wgu[...], rows[i[0], i[1], i[2]])
        dz = nt(wd[:part, :], cot_ref[i[0], i[1], i[2]])
        gate, up = gu[:units], gu[units:]
        gus[i[0], i[1], i[2], :far, :] = gate[part:]
        gus[i[0], i[1], i[2], far:, :] = up[part:]
        swiglu(i, gate[:part], up[:part], dz, 0, part)

    g.second()
    g.sibling_arrived(())
    units_of(())
    g.third()
    last = None
    for k in MASKS[1:]:
        g.complete(k)
        g.pass_on(k)
        if last is not None:
            g.sibling_arrived(last)
            units_of(last)
        last = k
    g.sibling_arrived(last)
    units_of(last)
    for o in range(1, nrest):
        landed(wd.at[o * part:(o + 1) * part, :], r_wd.at[o - 1], at_rest(at, nrest - o, nrest)[0])

    @pl.loop(0, 8)
    def _(q):
        i = (q // 4, (q // 2) % 2, q % 2)
        dz = nt(wd[part:, :], cot_ref[i[0], i[1], i[2]])
        swiglu(i, gus[i[0], i[1], i[2], :far, :], gus[i[0], i[1], i[2], far:, :], dz, part, units)

    def partial(dst, lhs, rhs, p):
        lo, w = PARTS[p]

        @pl.loop(0, 8)
        def _(q):
            a, b, c = q // 4, (q // 2) % 2, q % 2
            dst[a, b, c, :, lo:lo + w] = tn(lhs[a, b, c], rhs[:, lo:lo + w]).astype(BF)

    cw = 512

    def grads(lhs, rhs, outs):
        @pl.loop(0, rows.shape[4] // cw)
        def _(n):
            s = pl.ds(pl.multiple_of(n * cw, cw), cw)
            acc = None
            for q in range(8):
                a, b, c = q // 4, (q // 2) % 2, q % 2
                v = nn(lhs[a, b, c], rhs[a, b, c, :, s])
                acc = v if acc is None else acc + v
            for k, o in enumerate(outs):
                o[:, s] = acc[k * units:(k + 1) * units].astype(BF)

    sa = Scatter(at, fa, core_in, a0, a1, a2, sas, sar)
    sb = Scatter(at, fb, core_in, a0, a1, a2, sbs, sbr)
    for p in range(3):
        partial(fa, dgu, wgu, p)
        sa.start(sa.core_copy(p))
        if p:
            sa.add_core(p - 1)
    sa.add_core(2)
    pl.semaphore_signal(credit, inc=1, device_id=other(at, "c"), device_id_type=MESH)
    grads(zb, cot_ref, (gwd_out,))
    for o in range(1, nrest):
        log.push(gwd_out.at[o * part:(o + 1) * part, :], fd_out.at[o - 1], s_fd.at[o - 1], r_fd.at[o - 1], at_rest(at, nrest - o, nrest)[0])
    partial(fb, zb, wd, 0)
    for p in range(3):
        sa.step(p, 0)
    pl.semaphore_wait(credit, 1)
    sb.start(sb.core_copy(0))
    for p in range(1, 3):
        partial(fb, zb, wd, p)
        sb.start(sb.core_copy(p))
    for p in range(3):
        sa.step(p, 1)
    for p in range(3):
        sb.add_core(p, go=False)
    save = pltpu.make_async_copy(fb.at[:, :, :, own, :], down_out, lsem.at[5])
    save.start()
    for p in range(3):
        sa.finish(p, dn2_out)
    grads(dgu, rows, (gwg_out, gwu_out))
    save.wait()
    for o in range(1, nrest):
        landed(fd_out.at[o - 1], r_fd.at[o - 1], at_rest(at, o, nrest)[0])
    g.close()
    sa.close()
    sb.close()
    log.close()


def mlp(nrest, m, gain, cot_all, own, far):
    rows, d = m.shape
    far = tuple(a.reshape(-1, d) for a in far)
    part = own[0].shape[0]
    units = part * nrest
    vm = pl.BlockSpec(memory_space=pltpu.VMEM)
    hbm = pl.BlockSpec(memory_space=pl.ANY)
    cube = (2, 2, 2)
    dma = pltpu.SemaphoreType.DMA
    sd = jax.ShapeDtypeStruct
    nf = max(nrest - 1, 1)
    return pl.pallas_call(
        functools.partial(mlp_kernel, nrest),
        out_shape=(sd(cube + (rows, d), BF), sd((rows, d), F32)) + (sd((units, d), BF),) * 3 + (sd((nrest - 1, part, d), BF),),
        in_specs=[vm, vm] + [hbm] * 6,
        out_specs=(hbm,) + (vm,) * 4 + (hbm,),
        scratch_shapes=[
            pltpu.VMEM(cube + (2 * rows, d), BF),
            pltpu.VMEM(cube + (2 * rows, d), BF),
            pltpu.VMEM((2 * units, d), BF),
            pltpu.VMEM((units, d), BF),
            pltpu.VMEM(cube + (2 * (units - part), 2 * rows), F32),
            pltpu.VMEM(cube + (units, 2 * rows), BF),
            pltpu.VMEM(cube + (2 * units, 2 * rows), BF),
            pltpu.VMEM(cube + (2 * rows, d), BF),
            pltpu.VMEM(cube + (2 * rows, d), BF),
            pltpu.VMEM(cube + (rows, d), BF),
            pltpu.VMEM((2, 2, rows, d), BF), pltpu.VMEM((2, rows, d), BF), pltpu.VMEM((rows, d), BF),
            dma((7,)), dma((3, 8)), dma((3, 8)), dma((8,)), dma((8,)),
            dma((3, 4)), dma((3, 4)), dma((3, 4)), dma((3, 4)), dma((nf,)), dma((nf,)), dma((nf,)), dma((nf,)), pltpu.SemaphoreType.REGULAR,
        ],
        compiler_params=pltpu.CompilerParams(collective_id=1, has_side_effects=True, vmem_limit_bytes=63 * 2**20),
        name="mlp",
    )(m, gain, cot_all, *own, *far)


def rot_rows(v, cos, sin):
    h = v.shape[0] // 2
    a, b = v[:h], v[h:]
    return jnp.concatenate([a * cos - b * sin, b * cos + a * sin], axis=0)


def attn_kernel(nz, ndp, tok_ref, wpack, wout_ref, gain_ref, cos_ref, sin_ref, start_ref, cot_ref, wg_ref, wu_ref,
                m_out, q_out, kv_out, o_out, lse_out, xg_out, wqkv_out, wo_out, gain_out, cot_out, wg_out, wu_out,
                xg, wbuf, wobuf, gbuf, kvbuf, qbuf, kn, vt, obuf, lbuf, bias, part, cin, xin, total, gpack,
                lsem, s_disp, r_disp, s_gd, r_gd, s_w0, r_w0, s_w1, r_w1, s_g0, r_g0, s_g1, r_g1, s_o0, r_o0, s_o1, r_o1,
                s_od, r_od, s_x, r_x, s_kv, r_kv, s_p, r_p, s_rest, r_rest, gs, gr, gcs, gcr):
    at = place()
    log = Log()
    rows, d = tok_ref.shape
    hd = HEAD_DIM
    zi = at["zh"] * 2 + at["zl"]
    di = at["dh"] * 2 + at["dl"]
    t = at["x"] * 2 + at["c"]
    nrest = nz * ndp // 4
    wr = wpack.shape[1]
    quad = (("c",), ("x",), ("x", "c"))
    npeers = nz * ndp
    lin = (di * nz + zi) * 4 + t
    target = lax.rem(lin, npeers) * 4 + lin // npeers
    source = lax.rem(lin, 4) * npeers + lin // 4
    for f in quad:
        signal(other(at, *f))
    signal(other(at, "zl"))
    signal(other(at, "dl"))
    for o in range(1, nrest):
        signal(at_rest(at, o, nrest)[0])

    @pl.when(source != lin)
    def _():
        signal(device_of(source, nz))

    pl.semaphore_wait(pltpu.get_barrier_semaphore(), 4 + nrest + (target != lin).astype(jnp.int32))
    g = Gather(at, cot_out, gs, gr, gcs, gcr)
    here = [pltpu.make_async_copy(cot_ref, g.block((), at["c"]), lsem.at[0])]
    for cp in here:
        cp.start()
    gpack[...] = jnp.zeros_like(gpack)
    gpack[:, :wr] = jnp.broadcast_to(gain_ref[...].astype(F32), (16, wr)).astype(BF)
    for k, f in enumerate(quad):
        dev = other(at, *f)
        tt = dev[4] * 2 + dev[5]
        log.push(wpack.at[tt], wbuf.at[di, zi, pl.ds(pl.multiple_of(t * wr, wr), wr), :], s_disp.at[k], r_disp.at[k], dev)
        log.push(gpack, gbuf.at[di, zi, t], s_gd.at[k], r_gd.at[k], dev)
    wbuf[di, zi, pl.ds(pl.multiple_of(t * wr, wr), wr), :] = wpack[t]
    gbuf[di, zi, t] = gpack[...]
    x = tok_ref[...].astype(F32)
    inv = lax.rsqrt(jnp.mean(x * x, axis=1, keepdims=True) + NORM_EPS)
    xg[at["x"], at["c"]] = (x * inv).astype(BF)
    total[...] = x
    qx = Quad(at, log, xg, s_x, r_x)
    qx.start()
    for k, f in enumerate(quad):
        dev = other(at, *f)
        tt = dev[4] * 2 + dev[5]
        landed(wbuf.at[di, zi, pl.ds(pl.multiple_of(tt * wr, wr), wr), :], r_disp.at[k], dev)
        landed(gbuf.at[di, zi, tt], r_gd.at[k], dev)
    sw = Spread(at, log, wbuf, nrest, ((0, wbuf.shape[3], "zl", "dl"),), (s_w0, r_w0, s_w1, r_w1))
    sg = Spread(at, log, gbuf, nrest, ((0, 128, "zl", "dl"),), (s_g0, r_g0, s_g1, r_g1))
    so = Spread(at, log, wobuf, nrest, ((0, d, "zl", "dl"),), (s_o0, r_o0, s_o1, r_o1))
    for sp in (sw, sg):
        sp.start()
        sp.stage1(0)
    qx.forward()
    here[0].wait()
    @pl.when(target != lin)
    def _():
        pltpu.make_async_remote_copy(wout_ref, wobuf.at[lax.rem(lin, npeers) // nz, lax.rem(lax.rem(lin, npeers), nz)], s_od, r_od,
                                     device_id=device_of(target, nz), device_id_type=MESH).start()

    @pl.when(target == lin)
    def _():
        wobuf[di, zi] = wout_ref[...]

    qn = bias.shape[2]
    nq = bias.shape[0]
    keys = bias.shape[1]
    kpos = lax.broadcasted_iota(jnp.int32, (keys, qn), 0)
    for b in range(nq):
        qpos = zi * (4 * rows) + b * qn + lax.broadcasted_iota(jnp.int32, (1, qn), 1)
        first = start_ref[:, b * qn:(b + 1) * qn]
        bias[b] = jnp.where((kpos >= first) & (kpos <= qpos), 0.0, MASKED)
    for sp in (sw, sg):
        sp.stage2(0)
    for o in range(1, nrest):
        for sp in (sw, sg):
            sp.stage1(o)
    swaps = [Pushes(at, log, nrest, (lambda o, a=a: a), b, s_rest.at[k], r_rest.at[k], False)
             for k, (a, b) in enumerate(((wg_ref, wg_out), (wu_ref, wu_out)))]
    for o in range(1, nrest):
        for sp in (sw, sg):
            sp.stage2(o)
    @pl.when(source != lin)
    def _():
        pltpu.make_async_remote_copy(wobuf.at[di, zi], wobuf.at[di, zi], s_od, r_od,
                                     device_id=device_of(source, nz), device_id_type=MESH).wait_recv()

    so.start()
    so.stage1(0)
    for o in range(nrest):
        for sp in (sw, sg):
            sp.finish(o)
    g.first()
    qx.finish()
    xa = xg[...].reshape(4 * rows, d)
    qkv = jnp.transpose(nn(xa, wbuf[...].reshape(d, wbuf.shape[3])))
    cos, sin = cos_ref[...], sin_ref[...]
    kvbuf[zi, :hd, :] = rot_rows(qkv[GROUP * hd:(GROUP + 1) * hd], cos, sin).astype(BF)
    kvbuf[zi, hd:, :] = qkv[(GROUP + 1) * hd:].astype(BF)
    nzh = nz // 2
    for o in range(1, nzh):
        log.push(kvbuf.at[zi], kvbuf.at[zi], s_kv.at[0, o], r_kv.at[0, o], at_z(at, 2 * o, nz)[0])
    log.push(kvbuf.at[zi], kvbuf.at[zi], s_kv.at[1, 0], r_kv.at[1, 0], other(at, "zl"))
    for h in range(GROUP):
        qbuf[h] = (rot_rows(qkv[h * hd:(h + 1) * hd], cos, sin).astype(BF) * 0.125).astype(BF)

    save = [pltpu.make_async_copy(xg, xg_out, lsem.at[4]), pltpu.make_async_copy(wbuf, wqkv_out, lsem.at[5]),
            pltpu.make_async_copy(gbuf, gain_out, lsem.at[6]), pltpu.make_async_copy(qbuf, q_out, lsem.at[7])]
    for cp in save:
        cp.start()
    for o in range(1, nzh):
        dev, i = at_z(at, nz - 2 * o, nz)
        landed(kvbuf.at[i], r_kv.at[0, o], dev)
        log.push(kvbuf.at[i], kvbuf.at[i], s_kv.at[1, o], r_kv.at[1, o], other(at, "zl"))
    for o in range(nzh):
        landed(kvbuf.at[zi], r_kv.at[1, o], other(at, "zl"))
    g.second()
    swaps[0].start()
    save.append(pltpu.make_async_copy(kvbuf, kv_out, lsem.at[8]))
    save[-1].start()
    tl = kvbuf.shape[2]
    for i in range(nz):
        kn[i * tl:(i + 1) * tl, :] = jnp.transpose(kvbuf[i, :hd, :].astype(F32)).astype(BF)
        vt[:hd, i * tl:(i + 1) * tl] = kvbuf[i, hd:, :]
    vt[hd:, :] = jnp.ones((vt.shape[0] - hd, keys), BF)

    def heads(b, lo, hi):
        @pl.loop(lo, hi)
        def _(h):
            s = nn(kn[...], qbuf[h, :, b * qn:(b + 1) * qn]) + bias[b]
            mx = jnp.max(s, axis=0, keepdims=True)
            e = jnp.exp(s - mx).astype(BF)
            oe = nn(vt[...], e)
            tot = oe[hd:hd + 1]
            obuf[h, :, b * qn:(b + 1) * qn] = (oe[:hd] / tot).astype(BF)
            lbuf[h, :, b * qn:(b + 1) * qn] = mx + jnp.log(tot)

    so.stage2(0)
    for o in range(1, nrest):
        so.stage1(o)
    heads(0, 0, 4)
    swaps[1].start()
    g.third()
    heads(0, 4, 8)
    for o in range(1, nrest):
        so.stage2(o)
    heads(1, 0, 4)
    heads(1, 4, 8)
    for m in MASKS[1:4]:
        g.complete(m)
        g.pass_on(m)
    for o in range(nrest):
        so.finish(o)
    save += [pltpu.make_async_copy(wobuf, wo_out, lsem.at[9]), pltpu.make_async_copy(obuf, o_out, lsem.at[10]),
             pltpu.make_async_copy(lbuf, lse_out, lsem.at[11])]
    for cp in save[-3:]:
        cp.start()
    cw = 512
    nc = d // cw
    oT = obuf[...].reshape(GROUP * hd, 4 * rows)
    red = QuadSum(at, log, part, cin, xin, total, s_p, r_p, cw)
    for n in range(nc):
        s = slice(n * cw, (n + 1) * cw)
        wo = wobuf[:, :, :, s].reshape(GROUP * hd, cw)
        part[:, :, :, s] = tn(oT, wo).astype(BF).reshape(2, 2, rows, cw)
        red.start(n)
        if n:
            red.middle(n - 1)
    red.middle(nc - 1)
    for m in MASKS[4:]:
        g.complete(m)
        g.pass_on(m)
    for n in range(nc):
        red.finish(n)
    m_out[...] = total[...]
    for m in MASKS:
        g.sibling_arrived(m)
    for sw_ in swaps:
        sw_.finish()
    for cp in save:
        cp.wait()

    @pl.when(target != lin)
    def _():
        pltpu.make_async_remote_copy(wout_ref, wobuf.at[di, zi], s_od, r_od,
                                     device_id=device_of(target, nz), device_id_type=MESH).wait_send()

    g.close()
    log.close()


def attn(nz, ndp, tokens, wpack, w_out, gpack, cosT, sinT, starts, cot, wg, wu):
    rows, d = tokens.shape
    wr, wc = wpack.shape[1:]
    hd = HEAD_DIM
    units = wg.shape[0]
    nrest = nz * ndp // 4
    keys = nz * 4 * rows
    qn = 2 * rows
    vm = pl.BlockSpec(memory_space=pltpu.VMEM)
    hbm = pl.BlockSpec(memory_space=pl.ANY)
    dma = pltpu.SemaphoreType.DMA
    sd = jax.ShapeDtypeStruct
    sh = dict(
        xg=(2, 2, rows, d), w=(ndp, nz, 4 * wr, wc), wo=(ndp, nz, wr, d), g=(ndp, nz, 4, 16, 128),
        kv=(nz, 2 * hd, 4 * rows), q=(GROUP, hd, 4 * rows), lse=(GROUP, 1, 4 * rows))
    outs = (sd((rows, d), F32), sd(sh["q"], BF), sd(sh["kv"], BF), sd(sh["q"], BF), sd(sh["lse"], F32), sd(sh["xg"], BF),
            sd(sh["w"], BF), sd(sh["wo"], BF), sd(sh["g"], BF), sd((2, 2, 2, 2 * rows, d), BF)) + (sd((nrest - 1, units, d), BF),) * 2
    nq = 4 * rows // qn
    zz = (max(nrest - 1, 1),)
    return pl.pallas_call(
        functools.partial(attn_kernel, nz, ndp),
        out_shape=outs,
        in_specs=[vm] * 8 + [hbm] * 2,
        out_specs=(vm,) + (hbm,) * (len(outs) - 1),
        scratch_shapes=[
            pltpu.VMEM(sh["xg"], BF), pltpu.VMEM(sh["w"], BF), pltpu.VMEM(sh["wo"], BF), pltpu.VMEM(sh["g"], BF),
            pltpu.VMEM(sh["kv"], BF), pltpu.VMEM(sh["q"], BF), pltpu.VMEM((keys, hd), BF), pltpu.VMEM((hd + 16, keys), BF),
            pltpu.VMEM(sh["q"], BF), pltpu.VMEM(sh["lse"], F32), pltpu.VMEM((nq, keys, qn), F32),
            pltpu.VMEM((2, 2, rows, d), BF), pltpu.VMEM((2, rows, d), BF), pltpu.VMEM((rows, d), BF), pltpu.VMEM((rows, d), F32),
            pltpu.VMEM((16, 128), BF),
            dma((12,)), dma((3,)), dma((3,)), dma((3,)), dma((3,))] + [dma((nrest,)), dma((nrest,)), dma((nrest, 6)), dma((nrest, 6))] * 3 + [
            dma, dma, dma((3,)), dma((3,)), dma((2, nz // 2)), dma((2, nz // 2)), dma((2, 4)), dma((2, 4)),
            dma((2, nrest)), dma((2, nrest)), dma((3, 8)), dma((3, 8)), dma((8,)), dma((8,)),
        ],
        compiler_params=pltpu.CompilerParams(collective_id=2, has_side_effects=True, vmem_limit_bytes=58 * 2**20),
        name="attention",
    )(tokens, wpack, w_out, gpack, cosT, sinT, starts, cot, wg, wu)


def back_kernel(nz, ndp, m_ref, dn2_ref, gain_ref, cot_ref, tok_ref, cos_ref, sin_ref, start_ref,
                xg_in, wqkv_in, wo_in, q_in, kv_in, o_in, lse_in, down_in, gg_in, gu_in,
                dx_out, block_out, gq_out, gkv_out, gwo_out, gain_out, fg_out, fu_out,
                xg, wqkv, wo, qbuf, kvbuf, obuf, lbuf, dag, dob, delta, kn, vn, kt, bias, dkv, dqb, kvp, kvin, dqkv,
                gob, go1, go2, gof, gqb, gq1, gq2, gqf, gkb, gk1, gk2, gkf, gsend, gpart, part, cin, xin, total, ogot, val, got, fb, b0, b1, b2,
                lsem, s_x, r_x, s_o0, r_o0, s_o1, r_o1, s_q0, r_q0, s_q1, r_q1, s_k0, r_k0, s_k1, r_k1,
                s_kv, r_kv, s_p, r_p, s_rest, r_rest, s_od, r_od, s_gq, r_gq, s_gk, r_gk, s_v, r_v, s_b, r_b):
    at = place()
    log = Log()
    rows, d = m_ref.shape
    hd = HEAD_DIM
    qc = GROUP * hd
    zi = at["zh"] * 2 + at["zl"]
    di = at["dh"] * 2 + at["dl"]
    t = at["x"] * 2 + at["c"]
    nrest = nz * ndp // 4
    npeers = nz * ndp
    nzh = nz // 2
    wr = gwo_out.shape[0]
    keys = kn.shape[0]
    tl = 4 * rows
    lin = (di * nz + zi) * 4 + t
    target = lax.rem(lin, npeers) * 4 + lin // npeers
    source = lax.rem(lin, 4) * npeers + lin // 4
    loads = [pltpu.make_async_copy(a, b, lsem.at[k]) for k, (a, b) in enumerate((
        (kv_in, kvbuf), (wo_in, wo), (o_in, obuf), (q_in, qbuf), (lse_in, lbuf), (down_in, fb), (xg_in, xg), (wqkv_in, wqkv)))]
    for cp in loads:
        cp.start()
    quad = (("c",), ("x",), ("x", "c"))
    for f in quad:
        signal(other(at, *f))
    signal(other(at, "zl"))
    signal(other(at, "dl"))
    for o in range(1, nrest):
        signal(at_rest(at, o, nrest)[0])

    @pl.when(target != lin)
    def _():
        signal(device_of(target, nz))

    m = m_ref[...]
    inv2 = lax.rsqrt(jnp.mean(m * m, axis=1, keepdims=True) + NORM_EPS)
    mh = m * inv2
    dn2 = dn2_ref[...].astype(F32)
    dy = dn2 * gain_ref[...]
    dm = cot_ref[...].astype(F32) + inv2 * (dy - mh * jnp.mean(dy * mh, axis=1, keepdims=True))
    dx_out[...] = dm
    dag[at["x"], at["c"]] = dm.astype(BF)
    total[...] = jnp.zeros_like(total)
    gsum = jnp.sum(dn2 * mh, axis=0, keepdims=True)
    for i in range(d // 128):
        val[0, i:i + 1, :] = gsum[:, i * 128:(i + 1) * 128]
    pl.semaphore_wait(pltpu.get_barrier_semaphore(), 4 + nrest + (source != lin).astype(jnp.int32))
    qx = Quad(at, log, dag, s_x, r_x)
    qx.start()
    gs = AllSum(at, log, val, got, nrest, s_v, r_v)
    gs.start(0)
    units = fg_out.shape[1]
    swaps = [Pushes(at, log, nrest, (lambda o, a=a: a.at[pl.ds(o * units, units), :]), c, s_rest.at[k], r_rest.at[k], True)
             for k, (a, c) in enumerate(((gg_in, fg_out), (gu_in, fu_out)))]
    swaps[0].start()
    swaps[1].start()
    loads[0].wait()
    for i in range(nz):
        kn[i * tl:(i + 1) * tl, :] = jnp.transpose(kvbuf[i, :hd, :].astype(F32)).astype(BF)
        vn[i * tl:(i + 1) * tl, :] = jnp.transpose(kvbuf[i, hd:, :].astype(F32)).astype(BF)
        kt[:, i * tl:(i + 1) * tl] = kvbuf[i, :hd, :]
    kpos = lax.broadcasted_iota(jnp.int32, (keys, tl), 0)
    qpos = zi * tl + lax.broadcasted_iota(jnp.int32, (1, tl), 1)
    bias[...] = jnp.where((kpos >= start_ref[...]) & (kpos <= qpos), 0.0, MASKED)
    dkv[...] = jnp.zeros_like(dkv)
    for cp in loads[1:]:
        cp.wait()
    gs.take(0)
    gs.start(1)
    qx.forward()
    sb = Scatter(at, fb, None, b0, b1, b2, s_b, r_b)
    for p in range(3):
        sb.start(sb.stage_copy(p, 0))
    qx.finish()
    da = dag[...].reshape(tl, d)
    doT = nt(wo[...].reshape(qc, d), da).astype(BF)
    dob[...] = doT.reshape(GROUP, hd, tl)
    delta[...] = jnp.sum((dob[...].astype(F32) * obuf[...].astype(F32)), axis=1, keepdims=True)
    gs.take(1)
    gs.start(2)
    cw = 512
    oT = obuf[...].reshape(qc, tl)
    for n in range(d // cw):
        s = slice(n * cw, (n + 1) * cw)
        gob[:, :, :, s] = nn(oT, dag[:, :, :, s].reshape(tl, cw)).astype(BF).reshape(ndp, nz, wr, cw)
    mo = Merge(at, log, gob, go1, go2, gof, nrest, ((0, d // 2, "dl", "zl"), (d // 2, d // 2, "zl", "dl")), (s_o0, r_o0, s_o1, r_o1))
    far_first = tuple(range(1, nrest)) + (0,)
    for o in far_first:
        mo.stage1(o)

    def heads(lo, hi):
        @pl.loop(lo, hi)
        def _(h):
            qT, dT = qbuf[h], dob[h]
            p = jnp.exp(nn(kn[...], qT) + bias[...] - lbuf[h])
            ds = (p * (nn(vn[...], dT) - delta[h])).astype(BF)
            pb = p.astype(BF)
            dkv[:hd, :] += nt(qT, ds)
            dkv[hd:, :] += nt(dT, pb)
            dqb[pl.ds(pl.multiple_of(h * hd, hd), hd), :] = rot_rows(nn(kt[...], ds) * 0.125, cos_ref[...], -sin_ref[...])

    heads(0, 3)
    for p in range(3):
        sb.step(p, 0)
    gs.take(2)
    gs.start(3)
    for o in far_first:
        mo.stage2(o)
    heads(3, 6)
    for p in range(3):
        sb.step(p, 1)
    gs.take(3)
    gs.start(4)
    for o in far_first:
        mo.stage3(o)
    heads(6, 8)
    for p in range(3):
        sb.finish(p, block_out, m_ref)
    for i in range(nz):
        kvp[i] = dkv[:, i * tl:(i + 1) * tl].astype(BF)
    for o in range(1, nz):
        dev, i = at_z(at, o, nz)
        log.push(kvp.at[i], kvin.at[o - 1], s_kv.at[o - 1], r_kv.at[o - 1], dev)
    dqkv[:, :qc] = jnp.transpose(dqb[...]).astype(BF)
    mq = Merge(at, log, gqb, gq1, gq2, gqf, nrest, ((0, qc // 2, "dl", "zl"), (qc // 2, qc // 2, "zl", "dl")), (s_q0, r_q0, s_q1, r_q1))
    mk = Merge(at, log, gkb, gk1, gk2, gkf, nrest, ((0, 2 * hd, "dl", "zl"),), (s_k0, r_k0, s_k1, r_k1))

    def weight_grad(dst, lo, hi):
        step = 256
        per = step // (4 * wr)
        for n in range(d // step):
            xs = xg[:, :, :, n * step:(n + 1) * step].reshape(tl, step)
            v = tn(xs, dqkv[:, lo:hi]).astype(BF)
            for b in range(per):
                f = n * per + b
                dst[f // nz, f % nz] = v[b * 4 * wr:(b + 1) * 4 * wr]

    weight_grad(gqb, 0, qc)
    for o in far_first:
        mq.stage1(o)
    acc = dkv[:, pl.ds(pl.multiple_of(zi * tl, tl), tl)]
    for o in range(1, nz):
        dev, _ = at_z(at, nz - o, nz)
        landed(kvin.at[o - 1], r_kv.at[o - 1], dev)
        acc = acc + kvin[o - 1].astype(F32)
    dk = rot_rows(acc[:hd], cos_ref[...], -sin_ref[...])
    dqkv[:, qc:] = jnp.transpose(jnp.concatenate([dk, acc[hd:]], axis=0)).astype(BF)
    weight_grad(gkb, qc, qc + 2 * hd)
    for o in far_first:
        mk.stage1(o)
    red = QuadSum(at, log, part, cin, xin, total, s_p, r_p, cw)
    w = wqkv[...].reshape(d, qc + 2 * hd)
    nc = d // cw
    for n in range(nc):
        part[:, :, :, n * cw:(n + 1) * cw] = nt(dqkv[...], w[n * cw:(n + 1) * cw]).astype(BF).reshape(2, 2, rows, cw)
        red.start(n)
        if n:
            red.middle(n - 1)
    for o in far_first:
        mq.stage2(o)
    red.middle(nc - 1)
    for o in far_first:
        mk.stage2(o)
    for o in far_first:
        mq.stage3(o)
    for o in far_first:
        mk.stage3(o)
    gsend[...] = mo.result().astype(BF)

    @pl.when(source != lin)
    def _():
        pltpu.make_async_remote_copy(gsend, ogot, s_od, r_od, device_id=device_of(source, nz), device_id_type=MESH).start()

    @pl.when(source == lin)
    def _():
        ogot[...] = gsend[...]

    for n in range(nc):
        red.finish(n)
    x = tok_ref[...].astype(F32)
    inv1 = lax.rsqrt(jnp.mean(x * x, axis=1, keepdims=True) + NORM_EPS)
    xh = x * inv1
    dy1 = total[...]
    dx_out[...] = dx_out[...] + inv1 * (dy1 - xh * jnp.mean(dy1 * xh, axis=1, keepdims=True))
    gain_out[...] = gs.take(4)
    for merge, dst, sp, ss, rs, lo, hi in ((mq, gq_out, gpart.at[:, :qc], s_gq, r_gq, 0, qc), (mk, gkv_out, gpart.at[:, qc:], s_gk, r_gk, qc, qc + 2 * hd)):
        gpart[:, lo:hi] = merge.result().astype(BF)
        dst[t] = gpart[pl.ds(pl.multiple_of(t * wr, wr), wr), lo:hi]
        for k, f in enumerate(quad):
            dev = other(at, *f)
            tt = dev[4] * 2 + dev[5]
            log.push(gpart.at[pl.ds(pl.multiple_of(tt * wr, wr), wr), lo:hi], dst.at[t], ss.at[k], rs.at[k], dev)
    @pl.when(target != lin)
    def _():
        pltpu.make_async_remote_copy(gsend, ogot, s_od, r_od, device_id=device_of(target, nz), device_id_type=MESH).wait_recv()

    gwo_out[...] = ogot[...].astype(F32)
    for dst, rs in ((gq_out, r_gq), (gkv_out, r_gk)):
        for k, f in enumerate(quad):
            dev = other(at, *f)
            tt = dev[4] * 2 + dev[5]
            landed(dst.at[tt], rs.at[k], dev)
    for sw_ in swaps:
        sw_.finish()

    @pl.when(source != lin)
    def _():
        pltpu.make_async_remote_copy(gsend, ogot, s_od, r_od, device_id=device_of(source, nz), device_id_type=MESH).wait_send()

    sb.close()
    log.close()


def back(nz, ndp, m, dn2, gain, cot, tokens, cosT, sinT, starts, xg, wqkv, wo, q, kv, o, lse, down, grads):
    rows, d = m.shape
    hd = HEAD_DIM
    qc = GROUP * hd
    nrest = nz * ndp // 4
    wr = wo.shape[2]
    keys = nz * 4 * rows
    tl = 4 * rows
    units = grads[0].shape[0] // nrest
    vm = pl.BlockSpec(memory_space=pltpu.VMEM)
    hbm = pl.BlockSpec(memory_space=pl.ANY)
    dma = pltpu.SemaphoreType.DMA
    sd = jax.ShapeDtypeStruct
    nf = max(nrest - 1, 1)
    outs = (sd((rows, d), F32), sd((rows, d), BF), sd((4, wr, qc), BF), sd((4, wr, 2 * hd), BF), sd((wr, d), F32), sd((16, 128), F32)) + (
        sd((nrest - 1, units, d), BF),) * 2
    V = pltpu.VMEM

    def merge_bufs(r, c):
        return [V((ndp, nz, r, c), BF), V((nrest, 2, r, c), BF), V((nrest, r, c), BF), V((nf, r, c), BF)]

    return pl.pallas_call(
        functools.partial(back_kernel, nz, ndp),
        out_shape=outs,
        in_specs=[vm] * 8 + [hbm] * 10,
        out_specs=(vm,) * 6 + (hbm,) * 2,
        scratch_shapes=[
            V(xg.shape, BF), V(wqkv.shape, BF), V(wo.shape, BF), V(q.shape, BF), V(kv.shape, BF), V(o.shape, BF), V(lse.shape, F32),
            V((2, 2, rows, d), BF), V(q.shape, BF), V(lse.shape, F32), V((keys, hd), BF), V((keys, hd), BF), V((hd, keys), BF),
            V((keys, tl), F32), V((2 * hd, keys), F32), V((qc, tl), F32), V(kv.shape, BF), V((max(nz - 1, 1), 2 * hd, tl), BF),
            V((tl, qc + 2 * hd), BF)]
        + merge_bufs(wr, d) + merge_bufs(4 * wr, qc) + merge_bufs(4 * wr, 2 * hd) + [
            V((wr, d), BF), V((4 * wr, qc + 2 * hd), BF), V((2, 2, rows, d), BF), V((2, rows, d), BF), V((rows, d), BF), V((rows, d), F32),
            V((wr, d), BF), V((5, 16, 128), F32), V((4 + nf, 16, 128), F32),
            V(down.shape, BF), V((2, 2, rows, d), BF), V((2, rows, d), BF), V((rows, d), BF),
            dma((8,)), dma((3,)), dma((3,))] + [dma((nf,)), dma((nf,)), dma((nrest, 6)), dma((nrest, 6))] * 3 + [
            dma((nz,)), dma((nz,)), dma((2, 4)), dma((2, 4)), dma((2, nrest)), dma((2, nrest)), dma, dma, dma((3,)), dma((3,)), dma((3,)), dma((3,)),
            dma((4 + nf,)), dma((4 + nf,)), dma((3, 4)), dma((3, 4))],
        compiler_params=pltpu.CompilerParams(collective_id=3, has_side_effects=True, vmem_limit_bytes=62 * 2**20),
        name="backward",
    )(m, dn2, gain, cot, tokens, cosT, sinT, starts, xg, wqkv, wo, q, kv, o, lse, down, *grads)


def local(tokens, gain_attn, w_query, w_key, w_value, w_out, gain_mlp, w_gate_t, w_up_t, w_down, doc_ids, cotangent, nz, ndp):
    rows, d = tokens.shape
    wr = w_query.shape[0]
    grows = rows * 4
    seq_ids = doc_ids[0]
    length = seq_ids.shape[0]
    zi = lax.axis_index(Z)
    hd = HEAD_DIM
    qc = GROUP * hd
    ga = gain_attn.astype(F32)[:, None]
    wall = jnp.concatenate([w_query.reshape(wr, 4, qc), w_key.reshape(wr, 4, hd), w_value.reshape(wr, 4, hd)], axis=2).transpose(1, 0, 2)
    wpack = (wall.astype(F32) * ga[None]).astype(BF)
    gpack = gain_mlp[None]
    first = zi * grows
    own_ids = lax.dynamic_slice_in_dim(seq_ids, first, grows, 0)
    qpos = first + jnp.arange(grows, dtype=jnp.int32)
    starts = jnp.sum((seq_ids[:, None] < own_ids[None, :]).astype(jnp.int32), axis=0)
    freq = 10000.0 ** (-jnp.arange(hd // 2, dtype=F32) / (hd // 2))
    ph = (qpos - starts).astype(F32)[None, :] * freq[:, None]
    cosT, sinT = jnp.cos(ph), jnp.sin(ph)
    units = w_down.shape[0]
    fill = -units % 16
    if fill:
        w_gate_t, w_up_t, w_down = (jnp.pad(w, ((0, fill), (0, 0))) for w in (w_gate_t, w_up_t, w_down))
    m, q, kv, o, lse, xg, wqkv, wo, gains, cot_all, wgt, wut = attn(
        nz, ndp, tokens, wpack, w_out, gpack, cosT, sinT, starts[None], cotangent, w_gate_t, w_up_t)
    gm = gains[:, :, :, 0, :wr].reshape(1, d).astype(F32)
    down, dn2, gwd, gwg, gwu, fd = mlp(nz * ndp // 4, m, gm, cot_all, (w_gate_t, w_up_t, w_down), (wgt, wut))
    dx, block_out, gq, gkv, gwo, gsum, fg, fu = back(
        nz, ndp, m, dn2, gm, cotangent, tokens, cosT, sinT, starts[None], xg, wqkv, wo, q, kv, o, lse, down, (gwg, gwu))

    def own(a, far):
        return (a[:units + fill].astype(F32) + jnp.sum(far.astype(F32), axis=0))[:units]

    gw = jnp.concatenate([gq, gkv], axis=2).astype(F32)
    gga = jnp.sum(gw * wall.astype(F32), axis=(0, 2))
    gw = (gw * ga[None]).transpose(1, 0, 2)
    gwq = gw[:, :, :qc].reshape(wr, 4 * qc)
    gwk = gw[:, :, qc:qc + hd].reshape(wr, 4 * hd)
    gwv = gw[:, :, qc + hd:].reshape(wr, 4 * hd)
    ggm = lax.dynamic_slice_in_dim(gsum.reshape(d), lax.axis_index(AXES) * wr, wr, 0)
    return block_out, dx, gga, gwq, gwk, gwv, gwo, ggm, own(gwg, fg), own(gwu, fu), own(gwd, fd)


def solution(mesh):
    dp, seq = mesh.shape["dp"], mesh.shape["seq"]
    m6 = Mesh(mesh.devices.reshape(dp // 2, 2, seq // 8, 2, 2, 2), AXES)
    row = P(AXES, None)
    vec = P(AXES)
    col = P(None, AXES)
    inner = jax.shard_map(
        functools.partial(local, nz=seq // 4, ndp=dp), mesh=m6,
        in_specs=(row, vec, row, row, row, row, vec, row, row, row, P(DP, None), row),
        out_specs=(row, row, vec, row, row, row, row, vec, row, row, row),
        check_vma=False,
    )

    def run(tokens, gain_attn, w_query, w_key, w_value, w_out, gain_mlp, w_gate, w_up, w_down, doc_ids, cotangent):
        outs = inner(tokens, gain_attn, w_query, w_key, w_value, w_out, gain_mlp, w_gate.T, w_up.T, w_down, doc_ids, cotangent)
        return outs[:8] + (outs[8].T, outs[9].T, outs[10])

    return run
```

```python
import functools

import jax
import jax.numpy as jnp
from jax import lax
from jax.experimental import pallas as pl
from jax.experimental.pallas import tpu as pltpu
from jax.sharding import Mesh, PartitionSpec as P

HEADS = 32
KV_HEADS = 4
HEAD_DIM = 64
GROUP = HEADS // KV_HEADS
NORM_EPS = 1e-05
MASKED = -1e30
AXES = ("dh", "dl", "zh", "zl", "x", "c")
T = ("x", "c")
Z = ("zh", "zl")
DP = ("dh", "dl")
CUBE = ("dl", "zl", "x", "c")
REST = ("dh", "zh")
BF = jnp.bfloat16
F32 = jnp.float32


def nn(a, b):
    return jnp.dot(a, b, preferred_element_type=F32)


def nt(a, b):
    return lax.dot_general(a, b, (((1,), (1,)), ((), ())), preferred_element_type=F32)


def tn(a, b):
    return lax.dot_general(a, b, (((0,), (0,)), ((), ())), preferred_element_type=F32)


def rotate(v, cos, sin, sign):
    h = v.shape[-1] // 2
    a, b = v[..., :h], v[..., h:]
    s = sin * sign
    return jnp.concatenate([a * cos - b * s, b * cos + a * s], axis=-1)


PARTS = ((0, 768), (768, 640), (1408, 640))
MESH = pl.DeviceIdType.MESH


def place():
    return {a: lax.axis_index(a) for a in AXES}


def other(at, *flip):
    return tuple(1 - at[a] if a in flip else at[a] for a in AXES)


def greet(at, partners):
    barrier = pltpu.get_barrier_semaphore()
    for flip in partners:
        pl.semaphore_signal(barrier, inc=1, device_id=other(at, *flip), device_id_type=MESH)
    pl.semaphore_wait(barrier, len(partners))


CDIMS = ("x", "zl", "dl")
MASKS = ((), ("x",), ("zl",), ("dl",), ("x", "zl"), ("zl", "dl"), ("dl", "x"), ("x", "zl", "dl"))


def cube_index(at, mask):
    return tuple(1 - at[a] if a in mask else at[a] for a in ("dl", "zl", "x"))


ORDERS = tuple(tuple(CDIMS[(p + s) % 3] for s in range(3)) for p in range(3))


class Log:
    def __init__(self):
        self.open = []

    def push(self, src, dst, ssem, rsem, device):
        cp = pltpu.make_async_remote_copy(src, dst, ssem, rsem, device_id=device, device_id_type=MESH)
        cp.start()
        self.open.append(cp)

    def close(self):
        for cp in self.open:
            cp.wait_send()


def landed(dst, sem, device):
    pltpu.make_async_remote_copy(dst, dst, sem, sem, device_id=device, device_id_type=MESH).wait_recv()


def at_z(at, o, n):
    i = lax.rem(at["zh"] * 2 + at["zl"] + o, n)
    return tuple(i // 2 if a == "zh" else lax.rem(i, 2) if a == "zl" else at[a] for a in AXES), i


def at_dp(at, o, n):
    i = lax.rem(at["dh"] * 2 + at["dl"] + o, n)
    return tuple(i // 2 if a == "dh" else lax.rem(i, 2) if a == "dl" else at[a] for a in AXES), i


def at_rest(at, o, n):
    i = lax.rem(at["dh"] * 2 + at["zh"] + o, n)
    return tuple(i // 2 if a == "dh" else lax.rem(i, 2) if a == "zh" else at[a] for a in AXES), i


def signal(device):
    pl.semaphore_signal(pltpu.get_barrier_semaphore(), inc=1, device_id=device, device_id_type=MESH)


def device_of(i, nz):
    t, j = lax.rem(i, 4), i // 4
    z, p = lax.rem(j, nz), j // nz
    return (p // 2, lax.rem(p, 2), z // 2, lax.rem(z, 2), t // 2, lax.rem(t, 2))


class Quad:
    def __init__(self, at, log, buf, ssem, rsem):
        self.at, self.log, self.buf, self.ssem, self.rsem = at, log, buf, ssem, rsem

    def start(self):
        at = self.at
        own = self.buf.at[at["x"], at["c"]]
        self.log.push(own, own, self.ssem.at[0], self.rsem.at[0], other(at, "x"))
        self.log.push(own, own, self.ssem.at[1], self.rsem.at[1], other(at, "c"))

    def forward(self):
        at = self.at
        far = self.buf.at[1 - at["x"], at["c"]]
        landed(far, self.rsem.at[0], other(at, "x"))
        self.log.push(far, far, self.ssem.at[2], self.rsem.at[2], other(at, "c"))

    def finish(self):
        at = self.at
        landed(self.buf.at[at["x"], 1 - at["c"]], self.rsem.at[1], other(at, "c"))
        landed(self.buf.at[1 - at["x"], 1 - at["c"]], self.rsem.at[2], other(at, "c"))


class QuadSum:
    def __init__(self, at, log, part, cin, xin, total, ssem, rsem, width):
        self.at, self.log, self.part, self.cin, self.xin, self.total = at, log, part, cin, xin, total
        self.ssem, self.rsem, self.width = ssem, rsem, width

    def cols(self, n):
        return slice(n * self.width, (n + 1) * self.width)

    def start(self, n):
        at, s = self.at, self.cols(n)
        self.log.push(self.part.at[:, 1 - at["c"], :, s], self.cin.at[:, :, s], self.ssem.at[0, n], self.rsem.at[0, n], other(at, "c"))

    def middle(self, n):
        at, s = self.at, self.cols(n)
        landed(self.cin.at[:, :, s], self.rsem.at[0, n], other(at, "c"))
        far = self.part.at[1 - at["x"], at["c"], :, s]
        far[...] = (far[...].astype(F32) + self.cin[1 - at["x"], :, s].astype(F32)).astype(BF)
        self.log.push(far, self.xin.at[:, s], self.ssem.at[1, n], self.rsem.at[1, n], other(at, "x"))
        near = self.part[at["x"], at["c"], :, s].astype(F32) + self.cin[at["x"], :, s].astype(F32)
        self.total[:, s] = self.total[:, s] + near

    def finish(self, n):
        s = self.cols(n)
        landed(self.xin.at[:, s], self.rsem.at[1, n], other(self.at, "x"))
        self.total[:, s] = self.total[:, s] + self.xin[:, s].astype(F32)


class Spread:
    def __init__(self, at, log, buf, nrest, parts, sems):
        self.at, self.log, self.buf, self.n, self.parts = at, log, buf, nrest, parts
        self.s0, self.r0, self.s1, self.r1 = sems

    def block(self, o, flip=(), part=None):
        at = self.at
        r = lax.rem(at["dh"] * (self.n_zh()) + at["zh"] + o, self.n)
        dh, zh = r // self.n_zh(), lax.rem(r, self.n_zh())
        dl = 1 - at["dl"] if "dl" in flip else at["dl"]
        zl = 1 - at["zl"] if "zl" in flip else at["zl"]
        ref = self.buf.at[dh * 2 + dl, zh * 2 + zl]
        if part is None:
            return ref
        lo, w = self.parts[part][:2]
        return ref.at[(slice(None),) * (len(ref.shape) - 1) + (slice(lo, lo + w),)]

    def n_zh(self):
        return self.buf.shape[1] // 2

    def start(self):
        for o in range(1, self.n):
            ref = self.block(0)
            self.log.push(ref, ref, self.s0.at[o - 1], self.r0.at[o - 1], at_rest(self.at, o, self.n)[0])

    def arrive(self, o):
        if o:
            landed(self.block(self.n - o), self.r0.at[o - 1], other(self.at, "zl"))

    def send(self, o, k, flip, part, dim):
        ref = self.block((self.n - o) % self.n, flip, part)
        self.log.push(ref, ref, self.s1.at[o, k], self.r1.at[o, k], other(self.at, dim))

    def take(self, o, k, flip, part):
        landed(self.block((self.n - o) % self.n, flip, part), self.r1.at[o, k], other(self.at, "zl"))

    def stage1(self, o):
        self.arrive(o)
        for p, (_, _, a, b) in enumerate(self.parts):
            self.send(o, 3 * p, (), p, a)
        for p, (_, _, a, b) in enumerate(self.parts):
            self.send(o, 3 * p + 1, (), p, b)

    def stage2(self, o):
        for p, (_, _, a, b) in enumerate(self.parts):
            self.take(o, 3 * p, (a,), p)
            self.send(o, 3 * p + 2, (a,), p, b)

    def finish(self, o):
        for p, (_, _, a, b) in enumerate(self.parts):
            self.take(o, 3 * p + 1, (b,), p)
            self.take(o, 3 * p + 2, (a, b), p)


class Merge:
    def __init__(self, at, log, buf, in1, in2, far, nrest, parts, sems):
        self.at, self.log, self.buf, self.in1, self.in2, self.far = at, log, buf, in1, in2, far
        self.n, self.parts = nrest, parts
        self.s0, self.r0, self.s1, self.r1 = sems

    def cut(self, ref, p):
        lo, w = self.parts[p][:2]
        return ref.at[(slice(None),) * (len(ref.shape) - 1) + (slice(lo, lo + w),)]

    def block(self, o, flip, p):
        at, nzh = self.at, self.buf.shape[1] // 2
        r = lax.rem(at["dh"] * nzh + at["zh"] + o, self.n)
        dl = 1 - at["dl"] if "dl" in flip else at["dl"]
        zl = 1 - at["zl"] if "zl" in flip else at["zl"]
        return self.cut(self.buf.at[(r // nzh) * 2 + dl, lax.rem(r, nzh) * 2 + zl], p)

    def stage1(self, o):
        for p, (_, _, a, b) in enumerate(self.parts):
            for k, flip in enumerate(((a, b), (a,))):
                self.log.push(self.block(o, flip, p), self.cut(self.in1.at[o, k], p), self.s1.at[o, 3 * p + k], self.r1.at[o, 3 * p + k],
                              other(self.at, a))

    def add(self, o, flip, p, ref):
        blk = self.block(o, flip, p)
        blk[...] = (blk[...].astype(F32) + ref[...].astype(F32)).astype(BF)

    def stage2(self, o):
        for p, (_, _, a, b) in enumerate(self.parts):
            src = self.cut(self.in1.at[o, 0], p)
            landed(src, self.r1.at[o, 3 * p], other(self.at, a))
            self.add(o, (b,), p, src)
            self.log.push(self.block(o, (b,), p), self.cut(self.in2.at[o], p), self.s1.at[o, 3 * p + 2], self.r1.at[o, 3 * p + 2],
                          other(self.at, b))
        for p, (_, _, a, b) in enumerate(self.parts):
            src = self.cut(self.in1.at[o, 1], p)
            landed(src, self.r1.at[o, 3 * p + 1], other(self.at, a))
            self.add(o, (), p, src)

    def stage3(self, o):
        for p, (_, _, a, b) in enumerate(self.parts):
            src = self.cut(self.in2.at[o], p)
            landed(src, self.r1.at[o, 3 * p + 2], other(self.at, b))
            self.add(o, (), p, src)
        if o:
            nzh = self.buf.shape[1] // 2
            at = self.at
            r = lax.rem(at["dh"] * nzh + at["zh"] + o, self.n)
            ref = self.buf.at[(r // nzh) * 2 + at["dl"], lax.rem(r, nzh) * 2 + at["zl"]]
            self.log.push(ref, self.far.at[o - 1], self.s0.at[o - 1], self.r0.at[o - 1], at_rest(at, o, self.n)[0])

    def result(self):
        at = self.at
        nzh = self.buf.shape[1] // 2
        total = self.buf[at["dh"] * 2 + at["dl"], at["zh"] * 2 + at["zl"]].astype(F32)
        for o in range(1, self.n):
            landed(self.far.at[o - 1], self.r0.at[o - 1], at_rest(at, self.n - o, self.n)[0])
            total = total + self.far[o - 1].astype(F32)
        return total


class AllSum:
    DIMS = ("c", "x", "dl", "zl")

    def __init__(self, at, log, val, got, nrest, ssem, rsem):
        self.at, self.log, self.val, self.got, self.n, self.ssem, self.rsem = at, log, val, got, nrest, ssem, rsem

    def start(self, k):
        if k < 4:
            self.log.push(self.val.at[k], self.got.at[k], self.ssem.at[k], self.rsem.at[k], other(self.at, self.DIMS[k]))
        else:
            for o in range(1, self.n):
                i = 3 + o
                self.log.push(self.val.at[4], self.got.at[i], self.ssem.at[i], self.rsem.at[i], at_rest(self.at, o, self.n)[0])

    def take(self, k):
        if k < 4:
            landed(self.got.at[k], self.rsem.at[k], other(self.at, self.DIMS[k]))
            self.val[k + 1] = self.val[k] + self.got[k]
            return None
        total = self.val[4]
        for o in range(1, self.n):
            i = 3 + o
            landed(self.got.at[i], self.rsem.at[i], other(self.at, "c"))
            total = total + self.got[i]
        return total


class Pushes:
    def __init__(self, at, log, nrest, src, dst, ssem, rsem, back):
        self.args = at, log, nrest, src, dst, ssem, rsem, back

    def start(self):
        at, log, n, src, dst, ssem, rsem, back = self.args
        for o in range(1, n):
            dev, _ = at_rest(at, n - o if back else o, n)
            log.push(src(o), dst.at[o - 1], ssem.at[o - 1], rsem.at[o - 1], dev)

    def finish(self):
        at, log, n, src, dst, ssem, rsem, back = self.args
        for o in range(1, n):
            landed(dst.at[o - 1], rsem.at[o - 1], at_rest(at, o if back else n - o, n)[0])


class Gather:
    def __init__(self, at, buf, ssem, rsem, csend, crecv):
        self.at, self.buf, self.ssem, self.rsem, self.csend, self.crecv = at, buf, ssem, rsem, csend, crecv
        self.rows = buf.shape[3] // 2
        self.open = []

    def block(self, mask, core, p=None):
        i = cube_index(self.at, mask)
        r = pl.ds(pl.multiple_of(core * self.rows, self.rows), self.rows)
        if p is None:
            return self.buf.at[i[0], i[1], i[2], r, :]
        lo, w = PARTS[p]
        return self.buf.at[i[0], i[1], i[2], r, lo:lo + w]

    def send(self, p, mask, dim):
        ref = self.block(mask, self.at["c"], p)
        k = MASKS.index(tuple(a for a in mask_sorted(mask + (dim,))))
        cp = pltpu.make_async_remote_copy(ref, ref, self.ssem.at[p, k], self.rsem.at[p, k],
                                          device_id=other(self.at, dim), device_id_type=MESH)
        cp.start()
        self.open.append(cp)

    def arrived(self, p, mask):
        k = MASKS.index(mask)
        ref = self.block(mask, self.at["c"], p)
        pltpu.make_async_remote_copy(ref, ref, self.ssem.at[p, k], self.rsem.at[p, k],
                                     device_id=other(self.at, "x"), device_id_type=MESH).wait_recv()

    def pass_on(self, mask):
        k = MASKS.index(mask)
        ref = self.block(mask, self.at["c"])
        cp = pltpu.make_async_remote_copy(ref, ref, self.csend.at[k], self.crecv.at[k],
                                          device_id=other(self.at, "c"), device_id_type=MESH)
        cp.start()
        self.open.append(cp)

    def sibling_arrived(self, mask):
        k = MASKS.index(mask)
        ref = self.block(mask, 1 - self.at["c"])
        pltpu.make_async_remote_copy(ref, ref, self.csend.at[k], self.crecv.at[k],
                                     device_id=other(self.at, "c"), device_id_type=MESH).wait_recv()

    def first(self):
        for p in range(3):
            self.send(p, (), ORDERS[p][0])
        self.pass_on(())

    def second(self):
        for p in range(3):
            a, b, _ = ORDERS[p]
            self.send(p, (), b)
        for p in range(3):
            a, b, _ = ORDERS[p]
            self.arrived(p, (a,))
            self.send(p, (a,), b)

    def third(self):
        for p in range(3):
            a, b, c = ORDERS[p]
            self.send(p, (), c)
        for p in range(3):
            a, b, c = ORDERS[p]
            self.send(p, (a,), c)
        for p in range(3):
            a, b, c = ORDERS[p]
            self.arrived(p, (b,))
            self.send(p, (b,), c)
        for p in range(3):
            a, b, c = ORDERS[p]
            self.arrived(p, mask_sorted((a, b)))
            self.send(p, mask_sorted((a, b)), c)

    def complete(self, mask):
        for p in range(3):
            if ORDERS[p][2] in mask:
                self.arrived(p, mask)

    def close(self):
        for cp in self.open:
            cp.wait_send()


def mask_sorted(mask):
    for m in MASKS:
        if set(m) == set(mask):
            return m
    raise ValueError(mask)


class Scatter:
    def __init__(self, at, full, core_in, r0, r1, r2, ssem, rsem):
        self.at, self.full, self.core_in, self.r = at, full, core_in, (r0, r1, r2)
        self.ssem, self.rsem = ssem, rsem
        self.rows = r2.shape[0]
        self.open = []

    def own(self, core):
        if self.full.shape[3] == self.rows:
            return slice(None)
        return pl.ds(pl.multiple_of(core * self.rows, self.rows), self.rows)

    def core_copy(self, p):
        lo, w = PARTS[p]
        return pltpu.make_async_remote_copy(
            self.full.at[:, :, :, self.own(1 - self.at["c"]), lo:lo + w], self.core_in.at[:, :, :, :, lo:lo + w],
            self.ssem.at[p, 3], self.rsem.at[p, 3], device_id=other(self.at, "c"), device_id_type=MESH)

    def stage_copy(self, p, s):
        lo, w = PARTS[p]
        dims = ORDERS[p]
        ix = []
        for a in ("dl", "zl", "x"):
            if a == dims[s]:
                ix.append(1 - self.at[a])
            elif a in dims[:s]:
                ix.append(self.at[a])
            else:
                ix.append(slice(None))
        dst = self.r[s]
        dst = dst.at[(slice(None),) * (len(dst.shape) - 1) + (slice(lo, lo + w),)]
        return pltpu.make_async_remote_copy(
            self.full.at[ix[0], ix[1], ix[2], self.own(self.at["c"]), lo:lo + w], dst,
            self.ssem.at[p, s], self.rsem.at[p, s], device_id=other(self.at, dims[s]), device_id_type=MESH)

    def start(self, cp):
        cp.start()
        self.open.append(cp)

    def blocks(self, p, s):
        dims = ORDERS[p]
        rest = dims[s:]
        out = []
        for m in MASKS:
            if set(m) <= set(rest):
                out.append(m)
        if rest:
            out.sort(key=lambda m: 0 if rest[0] in m else 1)
        return out

    def add_core(self, p, go=True):
        cp = self.core_copy(p)
        cp.wait_recv()
        self.add_loop(p, 0, None)
        if go:
            self.start(self.stage_copy(p, 0))
        self.add_loop(p, 0, None, tail=True)

    def add_loop(self, p, s, src, tail=False):
        lo, w = PARTS[p]
        dims = ORDERS[p]
        for m in self.blocks(p, s):
            first = s < 3 and dims[s] in m
            if first == tail:
                continue
            i = cube_index(self.at, m)
            ref = self.full.at[i[0], i[1], i[2], self.own(self.at["c"]), lo:lo + w]
            if src is None:
                val = self.core_in[i[0], i[1], i[2], :, lo:lo + w]
            else:
                ix = [j for a, j in zip(("dl", "zl", "x"), i) if a in dims[s:]]
                val = src[tuple(ix) + (slice(None), slice(lo, lo + w))]
            ref[...] = (ref[...].astype(F32) + val.astype(F32)).astype(BF)

    def step(self, p, s):
        self.stage_copy(p, s).wait_recv()
        self.add_loop(p, s + 1, self.r[s])
        if s < 2:
            self.start(self.stage_copy(p, s + 1))
            self.add_loop(p, s + 1, self.r[s], tail=True)

    def finish(self, p, out, base=None):
        lo, w = PARTS[p]
        self.stage_copy(p, 2).wait_recv()
        i = cube_index(self.at, ())
        ref = self.full.at[i[0], i[1], i[2], self.own(self.at["c"]), lo:lo + w]
        total = ref[...].astype(F32) + self.r[2][:, lo:lo + w].astype(F32)
        if base is not None:
            total = total + base[:, lo:lo + w]
        out[:, lo:lo + w] = total.astype(out.dtype)

    def close(self):
        for cp in self.open:
            cp.wait_send()


def mlp_kernel(nrest, m_ref, gain_ref, cot_in, wg_own, wu_own, wd_own, wg_far, wu_far, down_out, dn2_out, gwd_out, gwg_out, gwu_out, fd_out,
               cot_ref, rows, wgu, wd, gus, zb, dgu, fa, fb, core_in, a0, a1, a2,
               lsem, gs, gr, gcs, gcr, sas, sar, sbs, sbr, s_wd, r_wd, s_fd, r_fd, credit):
    at = place()
    log = Log()
    units = wd.shape[0]
    brows = m_ref.shape[0]
    part = wd_own.shape[0]
    far = units - part
    copies = [pltpu.make_async_copy(wd_own, wd.at[:part, :], lsem.at[4])]
    for k, (own_w, far_w, lo) in enumerate(((wg_own, wg_far, 0), (wu_own, wu_far, units))):
        copies.append(pltpu.make_async_copy(own_w, wgu.at[lo:lo + part, :], lsem.at[2 * k]))
        copies.append(pltpu.make_async_copy(far_w, wgu.at[lo + part:lo + units, :], lsem.at[2 * k + 1]))
    copies.append(pltpu.make_async_copy(cot_in, cot_ref, lsem.at[6]))
    for cp in copies:
        cp.start()
    for flip in ("c", "x", "zl", "dl"):
        signal(other(at, flip))
    for o in range(1, nrest):
        signal(at_rest(at, o, nrest)[0])
    g = Gather(at, rows, gs, gr, gcs, gcr)
    own = pl.ds(pl.multiple_of(at["c"] * brows, brows), brows)
    m = m_ref[...]
    inv = lax.rsqrt(jnp.mean(m * m, axis=1, keepdims=True) + NORM_EPS)
    rows[at["dl"], at["zl"], at["x"], own, :] = (m * inv * gain_ref[...]).astype(BF)
    pl.semaphore_wait(pltpu.get_barrier_semaphore(), 3 + nrest)
    g.first()
    for cp in copies:
        cp.wait()

    def swiglu(i, gate, up, dz, lo, hi):
        sg = jax.nn.sigmoid(gate)
        sl = gate * sg
        zb[i[0], i[1], i[2], lo:hi, :] = (sl * up).astype(BF)
        dgu[i[0], i[1], i[2], lo:hi, :] = (dz * up * (sg * (1.0 + gate * (1.0 - sg)))).astype(BF)
        dgu[i[0], i[1], i[2], units + lo:units + hi, :] = (dz * sl).astype(BF)

    def units_of(mask):
        i = cube_index(at, mask)
        gu = nt(wgu[...], rows[i[0], i[1], i[2]])
        dz = nt(wd[:part, :], cot_ref[i[0], i[1], i[2]])
        gate, up = gu[:units], gu[units:]
        gus[i[0], i[1], i[2], :far, :] = gate[part:]
        gus[i[0], i[1], i[2], far:, :] = up[part:]
        swiglu(i, gate[:part], up[:part], dz, 0, part)

    g.second()
    g.sibling_arrived(())
    units_of(())
    g.third()
    for o in range(1, nrest):
        log.push(wd_own, wd.at[o * part:(o + 1) * part, :], s_wd.at[o - 1], r_wd.at[o - 1], at_rest(at, o, nrest)[0])
    last = None
    for k in MASKS[1:]:
        g.complete(k)
        g.pass_on(k)
        if last is not None:
            g.sibling_arrived(last)
            units_of(last)
        last = k
    g.sibling_arrived(last)
    units_of(last)
    for o in range(1, nrest):
        landed(wd.at[o * part:(o + 1) * part, :], r_wd.at[o - 1], at_rest(at, nrest - o, nrest)[0])

    @pl.loop(0, 8)
    def _(q):
        i = (q // 4, (q // 2) % 2, q % 2)
        dz = nt(wd[part:, :], cot_ref[i[0], i[1], i[2]])
        swiglu(i, gus[i[0], i[1], i[2], :far, :], gus[i[0], i[1], i[2], far:, :], dz, part, units)

    def partial(dst, lhs, rhs, p):
        lo, w = PARTS[p]

        @pl.loop(0, 8)
        def _(q):
            a, b, c = q // 4, (q // 2) % 2, q % 2
            dst[a, b, c, :, lo:lo + w] = tn(lhs[a, b, c], rhs[:, lo:lo + w]).astype(BF)

    cw = 512

    def grads(lhs, rhs, outs):
        @pl.loop(0, rows.shape[4] // cw)
        def _(n):
            s = pl.ds(pl.multiple_of(n * cw, cw), cw)
            acc = None
            for q in range(8):
                a, b, c = q // 4, (q // 2) % 2, q % 2
                v = nn(lhs[a, b, c], rhs[a, b, c, :, s])
                acc = v if acc is None else acc + v
            for k, o in enumerate(outs):
                o[:, s] = acc[k * units:(k + 1) * units].astype(BF)

    sa = Scatter(at, fa, core_in, a0, a1, a2, sas, sar)
    sb = Scatter(at, fb, core_in, a0, a1, a2, sbs, sbr)
    for p in range(3):
        partial(fa, dgu, wgu, p)
        sa.start(sa.core_copy(p))
        if p:
            sa.add_core(p - 1)
    sa.add_core(2)
    pl.semaphore_signal(credit, inc=1, device_id=other(at, "c"), device_id_type=MESH)
    grads(zb, cot_ref, (gwd_out,))
    for o in range(1, nrest):
        log.push(gwd_out.at[o * part:(o + 1) * part, :], fd_out.at[o - 1], s_fd.at[o - 1], r_fd.at[o - 1], at_rest(at, nrest - o, nrest)[0])
    partial(fb, zb, wd, 0)
    for p in range(3):
        sa.step(p, 0)
    pl.semaphore_wait(credit, 1)
    sb.start(sb.core_copy(0))
    for p in range(1, 3):
        partial(fb, zb, wd, p)
        sb.start(sb.core_copy(p))
    for p in range(3):
        sa.step(p, 1)
    for p in range(3):
        sb.add_core(p, go=False)
    save = pltpu.make_async_copy(fb.at[:, :, :, own, :], down_out, lsem.at[5])
    save.start()
    for p in range(3):
        sa.finish(p, dn2_out)
    grads(dgu, rows, (gwg_out, gwu_out))
    save.wait()
    for o in range(1, nrest):
        landed(fd_out.at[o - 1], r_fd.at[o - 1], at_rest(at, o, nrest)[0])
    g.close()
    sa.close()
    sb.close()
    log.close()


def mlp(nrest, m, gain, cot_all, own, far):
    rows, d = m.shape
    far = tuple(a.reshape(-1, d) for a in far)
    part = own[0].shape[0]
    units = part * nrest
    vm = pl.BlockSpec(memory_space=pltpu.VMEM)
    hbm = pl.BlockSpec(memory_space=pl.ANY)
    cube = (2, 2, 2)
    dma = pltpu.SemaphoreType.DMA
    sd = jax.ShapeDtypeStruct
    nf = max(nrest - 1, 1)
    return pl.pallas_call(
        functools.partial(mlp_kernel, nrest),
        out_shape=(sd(cube + (rows, d), BF), sd((rows, d), F32)) + (sd((units, d), BF),) * 3 + (sd((nrest - 1, part, d), BF),),
        in_specs=[vm, vm] + [hbm] * 6,
        out_specs=(hbm,) + (vm,) * 4 + (hbm,),
        scratch_shapes=[
            pltpu.VMEM(cube + (2 * rows, d), BF),
            pltpu.VMEM(cube + (2 * rows, d), BF),
            pltpu.VMEM((2 * units, d), BF),
            pltpu.VMEM((units, d), BF),
            pltpu.VMEM(cube + (2 * (units - part), 2 * rows), F32),
            pltpu.VMEM(cube + (units, 2 * rows), BF),
            pltpu.VMEM(cube + (2 * units, 2 * rows), BF),
            pltpu.VMEM(cube + (2 * rows, d), BF),
            pltpu.VMEM(cube + (2 * rows, d), BF),
            pltpu.VMEM(cube + (rows, d), BF),
            pltpu.VMEM((2, 2, rows, d), BF), pltpu.VMEM((2, rows, d), BF), pltpu.VMEM((rows, d), BF),
            dma((7,)), dma((3, 8)), dma((3, 8)), dma((8,)), dma((8,)),
            dma((3, 4)), dma((3, 4)), dma((3, 4)), dma((3, 4)), dma((nf,)), dma((nf,)), dma((nf,)), dma((nf,)), pltpu.SemaphoreType.REGULAR,
        ],
        compiler_params=pltpu.CompilerParams(collective_id=1, has_side_effects=True, vmem_limit_bytes=63 * 2**20),
        name="mlp",
    )(m, gain, cot_all, *own, *far)


def rot_rows(v, cos, sin):
    h = v.shape[0] // 2
    a, b = v[:h], v[h:]
    return jnp.concatenate([a * cos - b * sin, b * cos + a * sin], axis=0)


def attn_kernel(nz, ndp, tok_ref, wpack, wout_ref, gain_ref, cos_ref, sin_ref, start_ref, cot_ref, wg_ref, wu_ref,
                m_out, q_out, kv_out, o_out, lse_out, xg_out, wqkv_out, wo_out, gain_out, cot_out, wg_out, wu_out,
                xg, wbuf, wobuf, gbuf, kvbuf, qbuf, kn, vt, obuf, lbuf, bias, part, cin, xin, total, gpack,
                lsem, s_disp, r_disp, s_gd, r_gd, s_w0, r_w0, s_w1, r_w1, s_g0, r_g0, s_g1, r_g1, s_o0, r_o0, s_o1, r_o1,
                s_od, r_od, s_x, r_x, s_kv, r_kv, s_p, r_p, s_rest, r_rest, gs, gr, gcs, gcr):
    at = place()
    log = Log()
    rows, d = tok_ref.shape
    hd = HEAD_DIM
    zi = at["zh"] * 2 + at["zl"]
    di = at["dh"] * 2 + at["dl"]
    t = at["x"] * 2 + at["c"]
    nrest = nz * ndp // 4
    wr = wpack.shape[1]
    quad = (("c",), ("x",), ("x", "c"))
    npeers = nz * ndp
    lin = (di * nz + zi) * 4 + t
    target = lax.rem(lin, npeers) * 4 + lin // npeers
    source = lax.rem(lin, 4) * npeers + lin // 4
    for f in quad:
        signal(other(at, *f))
    signal(other(at, "zl"))
    signal(other(at, "dl"))
    for o in range(1, nrest):
        signal(at_rest(at, o, nrest)[0])

    @pl.when(source != lin)
    def _():
        signal(device_of(source, nz))

    pl.semaphore_wait(pltpu.get_barrier_semaphore(), 4 + nrest + (target != lin).astype(jnp.int32))
    g = Gather(at, cot_out, gs, gr, gcs, gcr)
    here = [pltpu.make_async_copy(cot_ref, g.block((), at["c"]), lsem.at[0])]
    for cp in here:
        cp.start()
    gpack[...] = jnp.zeros_like(gpack)
    gpack[:, :wr] = jnp.broadcast_to(gain_ref[...].astype(F32), (16, wr)).astype(BF)
    for k, f in enumerate(quad):
        dev = other(at, *f)
        tt = dev[4] * 2 + dev[5]
        log.push(wpack.at[tt], wbuf.at[di, zi, pl.ds(pl.multiple_of(t * wr, wr), wr), :], s_disp.at[k], r_disp.at[k], dev)
        log.push(gpack, gbuf.at[di, zi, t], s_gd.at[k], r_gd.at[k], dev)
    wbuf[di, zi, pl.ds(pl.multiple_of(t * wr, wr), wr), :] = wpack[t]
    gbuf[di, zi, t] = gpack[...]
    x = tok_ref[...].astype(F32)
    inv = lax.rsqrt(jnp.mean(x * x, axis=1, keepdims=True) + NORM_EPS)
    xg[at["x"], at["c"]] = (x * inv).astype(BF)
    total[...] = x
    qx = Quad(at, log, xg, s_x, r_x)
    qx.start()
    for k, f in enumerate(quad):
        dev = other(at, *f)
        tt = dev[4] * 2 + dev[5]
        landed(wbuf.at[di, zi, pl.ds(pl.multiple_of(tt * wr, wr), wr), :], r_disp.at[k], dev)
        landed(gbuf.at[di, zi, tt], r_gd.at[k], dev)
    sw = Spread(at, log, wbuf, nrest, ((0, wbuf.shape[3], "zl", "dl"),), (s_w0, r_w0, s_w1, r_w1))
    sg = Spread(at, log, gbuf, nrest, ((0, 128, "zl", "dl"),), (s_g0, r_g0, s_g1, r_g1))
    so = Spread(at, log, wobuf, nrest, ((0, d, "zl", "dl"),), (s_o0, r_o0, s_o1, r_o1))
    for sp in (sw, sg):
        sp.start()
        sp.stage1(0)
    qx.forward()
    here[0].wait()
    @pl.when(target != lin)
    def _():
        pltpu.make_async_remote_copy(wout_ref, wobuf.at[lax.rem(lin, npeers) // nz, lax.rem(lax.rem(lin, npeers), nz)], s_od, r_od,
                                     device_id=device_of(target, nz), device_id_type=MESH).start()

    @pl.when(target == lin)
    def _():
        wobuf[di, zi] = wout_ref[...]

    qn = bias.shape[2]
    nq = bias.shape[0]
    keys = bias.shape[1]
    kpos = lax.broadcasted_iota(jnp.int32, (keys, qn), 0)
    for b in range(nq):
        qpos = zi * (4 * rows) + b * qn + lax.broadcasted_iota(jnp.int32, (1, qn), 1)
        first = start_ref[:, b * qn:(b + 1) * qn]
        bias[b] = jnp.where((kpos >= first) & (kpos <= qpos), 0.0, MASKED)
    for sp in (sw, sg):
        sp.stage2(0)
    for o in range(1, nrest):
        for sp in (sw, sg):
            sp.stage1(o)
    swaps = [Pushes(at, log, nrest, (lambda o, a=a: a), b, s_rest.at[k], r_rest.at[k], False)
             for k, (a, b) in enumerate(((wg_ref, wg_out), (wu_ref, wu_out)))]
    for o in range(1, nrest):
        for sp in (sw, sg):
            sp.stage2(o)
    @pl.when(source != lin)
    def _():
        pltpu.make_async_remote_copy(wobuf.at[di, zi], wobuf.at[di, zi], s_od, r_od,
                                     device_id=device_of(source, nz), device_id_type=MESH).wait_recv()

    so.start()
    so.stage1(0)
    for o in range(nrest):
        for sp in (sw, sg):
            sp.finish(o)
    g.first()
    qx.finish()
    xa = xg[...].reshape(4 * rows, d)
    qkv = jnp.transpose(nn(xa, wbuf[...].reshape(d, wbuf.shape[3])))
    cos, sin = cos_ref[...], sin_ref[...]
    kvbuf[zi, :hd, :] = rot_rows(qkv[GROUP * hd:(GROUP + 1) * hd], cos, sin).astype(BF)
    kvbuf[zi, hd:, :] = qkv[(GROUP + 1) * hd:].astype(BF)
    nzh = nz // 2
    for o in range(1, nzh):
        log.push(kvbuf.at[zi], kvbuf.at[zi], s_kv.at[0, o], r_kv.at[0, o], at_z(at, 2 * o, nz)[0])
    log.push(kvbuf.at[zi], kvbuf.at[zi], s_kv.at[1, 0], r_kv.at[1, 0], other(at, "zl"))
    for h in range(GROUP):
        qbuf[h] = (rot_rows(qkv[h * hd:(h + 1) * hd], cos, sin).astype(BF) * 0.125).astype(BF)

    save = [pltpu.make_async_copy(xg, xg_out, lsem.at[4]), pltpu.make_async_copy(wbuf, wqkv_out, lsem.at[5]),
            pltpu.make_async_copy(gbuf, gain_out, lsem.at[6]), pltpu.make_async_copy(qbuf, q_out, lsem.at[7])]
    for cp in save:
        cp.start()
    for o in range(1, nzh):
        dev, i = at_z(at, nz - 2 * o, nz)
        landed(kvbuf.at[i], r_kv.at[0, o], dev)
        log.push(kvbuf.at[i], kvbuf.at[i], s_kv.at[1, o], r_kv.at[1, o], other(at, "zl"))
    for o in range(nzh):
        landed(kvbuf.at[zi], r_kv.at[1, o], other(at, "zl"))
    g.second()
    swaps[0].start()
    save.append(pltpu.make_async_copy(kvbuf, kv_out, lsem.at[8]))
    save[-1].start()
    tl = kvbuf.shape[2]
    for i in range(nz):
        kn[i * tl:(i + 1) * tl, :] = jnp.transpose(kvbuf[i, :hd, :].astype(F32)).astype(BF)
        vt[:hd, i * tl:(i + 1) * tl] = kvbuf[i, hd:, :]
    vt[hd:, :] = jnp.ones((vt.shape[0] - hd, keys), BF)

    def heads(b, lo, hi):
        @pl.loop(lo, hi)
        def _(h):
            s = nn(kn[...], qbuf[h, :, b * qn:(b + 1) * qn]) + bias[b]
            mx = jnp.max(s, axis=0, keepdims=True)
            e = jnp.exp(s - mx).astype(BF)
            oe = nn(vt[...], e)
            tot = oe[hd:hd + 1]
            obuf[h, :, b * qn:(b + 1) * qn] = (oe[:hd] / tot).astype(BF)
            lbuf[h, :, b * qn:(b + 1) * qn] = mx + jnp.log(tot)

    so.stage2(0)
    for o in range(1, nrest):
        so.stage1(o)
    heads(0, 0, 4)
    g.third()
    heads(0, 4, 8)
    for o in range(1, nrest):
        so.stage2(o)
    swaps[1].start()
    heads(1, 0, 4)
    heads(1, 4, 8)
    for m in MASKS[1:4]:
        g.complete(m)
        g.pass_on(m)
    for o in range(nrest):
        so.finish(o)
    save += [pltpu.make_async_copy(wobuf, wo_out, lsem.at[9]), pltpu.make_async_copy(obuf, o_out, lsem.at[10]),
             pltpu.make_async_copy(lbuf, lse_out, lsem.at[11])]
    for cp in save[-3:]:
        cp.start()
    cw = 512
    nc = d // cw
    oT = obuf[...].reshape(GROUP * hd, 4 * rows)
    red = QuadSum(at, log, part, cin, xin, total, s_p, r_p, cw)
    for n in range(nc):
        s = slice(n * cw, (n + 1) * cw)
        wo = wobuf[:, :, :, s].reshape(GROUP * hd, cw)
        part[:, :, :, s] = tn(oT, wo).astype(BF).reshape(2, 2, rows, cw)
        red.start(n)
        if n:
            red.middle(n - 1)
    red.middle(nc - 1)
    for m in MASKS[4:]:
        g.complete(m)
        g.pass_on(m)
    for n in range(nc):
        red.finish(n)
    m_out[...] = total[...]
    for m in MASKS:
        g.sibling_arrived(m)
    for sw_ in swaps:
        sw_.finish()
    for cp in save:
        cp.wait()

    @pl.when(target != lin)
    def _():
        pltpu.make_async_remote_copy(wout_ref, wobuf.at[di, zi], s_od, r_od,
                                     device_id=device_of(target, nz), device_id_type=MESH).wait_send()

    g.close()
    log.close()


def attn(nz, ndp, tokens, wpack, w_out, gpack, cosT, sinT, starts, cot, wg, wu):
    rows, d = tokens.shape
    wr, wc = wpack.shape[1:]
    hd = HEAD_DIM
    units = wg.shape[0]
    nrest = nz * ndp // 4
    keys = nz * 4 * rows
    qn = 2 * rows
    vm = pl.BlockSpec(memory_space=pltpu.VMEM)
    hbm = pl.BlockSpec(memory_space=pl.ANY)
    dma = pltpu.SemaphoreType.DMA
    sd = jax.ShapeDtypeStruct
    sh = dict(
        xg=(2, 2, rows, d), w=(ndp, nz, 4 * wr, wc), wo=(ndp, nz, wr, d), g=(ndp, nz, 4, 16, 128),
        kv=(nz, 2 * hd, 4 * rows), q=(GROUP, hd, 4 * rows), lse=(GROUP, 1, 4 * rows))
    outs = (sd((rows, d), F32), sd(sh["q"], BF), sd(sh["kv"], BF), sd(sh["q"], BF), sd(sh["lse"], F32), sd(sh["xg"], BF),
            sd(sh["w"], BF), sd(sh["wo"], BF), sd(sh["g"], BF), sd((2, 2, 2, 2 * rows, d), BF)) + (sd((nrest - 1, units, d), BF),) * 2
    nq = 4 * rows // qn
    zz = (max(nrest - 1, 1),)
    return pl.pallas_call(
        functools.partial(attn_kernel, nz, ndp),
        out_shape=outs,
        in_specs=[vm] * 8 + [hbm] * 2,
        out_specs=(vm,) + (hbm,) * (len(outs) - 1),
        scratch_shapes=[
            pltpu.VMEM(sh["xg"], BF), pltpu.VMEM(sh["w"], BF), pltpu.VMEM(sh["wo"], BF), pltpu.VMEM(sh["g"], BF),
            pltpu.VMEM(sh["kv"], BF), pltpu.VMEM(sh["q"], BF), pltpu.VMEM((keys, hd), BF), pltpu.VMEM((hd + 16, keys), BF),
            pltpu.VMEM(sh["q"], BF), pltpu.VMEM(sh["lse"], F32), pltpu.VMEM((nq, keys, qn), F32),
            pltpu.VMEM((2, 2, rows, d), BF), pltpu.VMEM((2, rows, d), BF), pltpu.VMEM((rows, d), BF), pltpu.VMEM((rows, d), F32),
            pltpu.VMEM((16, 128), BF),
            dma((12,)), dma((3,)), dma((3,)), dma((3,)), dma((3,))] + [dma((nrest,)), dma((nrest,)), dma((nrest, 6)), dma((nrest, 6))] * 3 + [
            dma, dma, dma((3,)), dma((3,)), dma((2, nz // 2)), dma((2, nz // 2)), dma((2, 4)), dma((2, 4)),
            dma((2, nrest)), dma((2, nrest)), dma((3, 8)), dma((3, 8)), dma((8,)), dma((8,)),
        ],
        compiler_params=pltpu.CompilerParams(collective_id=2, has_side_effects=True, vmem_limit_bytes=58 * 2**20),
        name="attention",
    )(tokens, wpack, w_out, gpack, cosT, sinT, starts, cot, wg, wu)


def back_kernel(nz, ndp, m_ref, dn2_ref, gain_ref, cot_ref, tok_ref, cos_ref, sin_ref, start_ref,
                xg_in, wqkv_in, wo_in, q_in, kv_in, o_in, lse_in, down_in, gg_in, gu_in,
                dx_out, block_out, gq_out, gkv_out, gwo_out, gain_out, fg_out, fu_out,
                xg, wqkv, wo, qbuf, kvbuf, obuf, lbuf, dag, dob, delta, kn, vn, kt, bias, dkv, dqb, kvp, kvin, dqkv,
                gob, go1, go2, gof, gqb, gq1, gq2, gqf, gkb, gk1, gk2, gkf, gsend, gpart, part, cin, xin, total, ogot, val, got, fb, b0, b1, b2,
                lsem, s_x, r_x, s_o0, r_o0, s_o1, r_o1, s_q0, r_q0, s_q1, r_q1, s_k0, r_k0, s_k1, r_k1,
                s_kv, r_kv, s_p, r_p, s_rest, r_rest, s_od, r_od, s_gq, r_gq, s_gk, r_gk, s_v, r_v, s_b, r_b):
    at = place()
    log = Log()
    rows, d = m_ref.shape
    hd = HEAD_DIM
    qc = GROUP * hd
    zi = at["zh"] * 2 + at["zl"]
    di = at["dh"] * 2 + at["dl"]
    t = at["x"] * 2 + at["c"]
    nrest = nz * ndp // 4
    npeers = nz * ndp
    nzh = nz // 2
    wr = gwo_out.shape[0]
    keys = kn.shape[0]
    tl = 4 * rows
    lin = (di * nz + zi) * 4 + t
    target = lax.rem(lin, npeers) * 4 + lin // npeers
    source = lax.rem(lin, 4) * npeers + lin // 4
    loads = [pltpu.make_async_copy(a, b, lsem.at[k]) for k, (a, b) in enumerate((
        (kv_in, kvbuf), (wo_in, wo), (o_in, obuf), (q_in, qbuf), (lse_in, lbuf), (down_in, fb), (xg_in, xg), (wqkv_in, wqkv)))]
    for cp in loads:
        cp.start()
    quad = (("c",), ("x",), ("x", "c"))
    for f in quad:
        signal(other(at, *f))
    signal(other(at, "zl"))
    signal(other(at, "dl"))
    for o in range(1, nrest):
        signal(at_rest(at, o, nrest)[0])

    @pl.when(target != lin)
    def _():
        signal(device_of(target, nz))

    m = m_ref[...]
    inv2 = lax.rsqrt(jnp.mean(m * m, axis=1, keepdims=True) + NORM_EPS)
    mh = m * inv2
    dn2 = dn2_ref[...].astype(F32)
    dy = dn2 * gain_ref[...]
    dm = cot_ref[...].astype(F32) + inv2 * (dy - mh * jnp.mean(dy * mh, axis=1, keepdims=True))
    dx_out[...] = dm
    dag[at["x"], at["c"]] = dm.astype(BF)
    total[...] = jnp.zeros_like(total)
    gsum = jnp.sum(dn2 * mh, axis=0, keepdims=True)
    for i in range(d // 128):
        val[0, i:i + 1, :] = gsum[:, i * 128:(i + 1) * 128]
    pl.semaphore_wait(pltpu.get_barrier_semaphore(), 4 + nrest + (source != lin).astype(jnp.int32))
    qx = Quad(at, log, dag, s_x, r_x)
    qx.start()
    gs = AllSum(at, log, val, got, nrest, s_v, r_v)
    gs.start(0)
    units = fg_out.shape[1]
    swaps = [Pushes(at, log, nrest, (lambda o, a=a: a.at[pl.ds(o * units, units), :]), c, s_rest.at[k], r_rest.at[k], True)
             for k, (a, c) in enumerate(((gg_in, fg_out), (gu_in, fu_out)))]
    swaps[0].start()
    swaps[1].start()
    loads[0].wait()
    for i in range(nz):
        kn[i * tl:(i + 1) * tl, :] = jnp.transpose(kvbuf[i, :hd, :].astype(F32)).astype(BF)
        vn[i * tl:(i + 1) * tl, :] = jnp.transpose(kvbuf[i, hd:, :].astype(F32)).astype(BF)
        kt[:, i * tl:(i + 1) * tl] = kvbuf[i, :hd, :]
    kpos = lax.broadcasted_iota(jnp.int32, (keys, tl), 0)
    qpos = zi * tl + lax.broadcasted_iota(jnp.int32, (1, tl), 1)
    bias[...] = jnp.where((kpos >= start_ref[...]) & (kpos <= qpos), 0.0, MASKED)
    dkv[...] = jnp.zeros_like(dkv)
    for cp in loads[1:]:
        cp.wait()
    gs.take(0)
    gs.start(1)
    qx.forward()
    sb = Scatter(at, fb, None, b0, b1, b2, s_b, r_b)
    for p in range(3):
        sb.start(sb.stage_copy(p, 0))
    qx.finish()
    da = dag[...].reshape(tl, d)
    doT = nt(wo[...].reshape(qc, d), da).astype(BF)
    dob[...] = doT.reshape(GROUP, hd, tl)
    delta[...] = jnp.sum((dob[...].astype(F32) * obuf[...].astype(F32)), axis=1, keepdims=True)
    gs.take(1)
    gs.start(2)
    cw = 512
    oT = obuf[...].reshape(qc, tl)
    for n in range(d // cw):
        s = slice(n * cw, (n + 1) * cw)
        gob[:, :, :, s] = nn(oT, dag[:, :, :, s].reshape(tl, cw)).astype(BF).reshape(ndp, nz, wr, cw)
    mo = Merge(at, log, gob, go1, go2, gof, nrest, ((0, d // 2, "dl", "zl"), (d // 2, d // 2, "zl", "dl")), (s_o0, r_o0, s_o1, r_o1))
    far_first = tuple(range(1, nrest)) + (0,)
    for o in far_first:
        mo.stage1(o)

    def heads(lo, hi):
        @pl.loop(lo, hi)
        def _(h):
            qT, dT = qbuf[h], dob[h]
            p = jnp.exp(nn(kn[...], qT) + bias[...] - lbuf[h])
            ds = (p * (nn(vn[...], dT) - delta[h])).astype(BF)
            pb = p.astype(BF)
            dkv[:hd, :] += nt(qT, ds)
            dkv[hd:, :] += nt(dT, pb)
            dqb[pl.ds(pl.multiple_of(h * hd, hd), hd), :] = rot_rows(nn(kt[...], ds) * 0.125, cos_ref[...], -sin_ref[...])

    heads(0, 3)
    for p in range(3):
        sb.step(p, 0)
    gs.take(2)
    gs.start(3)
    for o in far_first:
        mo.stage2(o)
    heads(3, 6)
    for p in range(3):
        sb.step(p, 1)
    gs.take(3)
    gs.start(4)
    for o in far_first:
        mo.stage3(o)
    heads(6, 8)
    for p in range(3):
        sb.finish(p, block_out, m_ref)
    for i in range(nz):
        kvp[i] = dkv[:, i * tl:(i + 1) * tl].astype(BF)
    for o in range(1, nz):
        dev, i = at_z(at, o, nz)
        log.push(kvp.at[i], kvin.at[o - 1], s_kv.at[o - 1], r_kv.at[o - 1], dev)
    dqkv[:, :qc] = jnp.transpose(dqb[...]).astype(BF)
    mq = Merge(at, log, gqb, gq1, gq2, gqf, nrest, ((0, qc // 2, "dl", "zl"), (qc // 2, qc // 2, "zl", "dl")), (s_q0, r_q0, s_q1, r_q1))
    mk = Merge(at, log, gkb, gk1, gk2, gkf, nrest, ((0, 2 * hd, "dl", "zl"),), (s_k0, r_k0, s_k1, r_k1))

    def weight_grad(dst, lo, hi):
        step = 256
        per = step // (4 * wr)
        for n in range(d // step):
            xs = xg[:, :, :, n * step:(n + 1) * step].reshape(tl, step)
            v = tn(xs, dqkv[:, lo:hi]).astype(BF)
            for b in range(per):
                f = n * per + b
                dst[f // nz, f % nz] = v[b * 4 * wr:(b + 1) * 4 * wr]

    weight_grad(gqb, 0, qc)
    for o in far_first:
        mq.stage1(o)
    acc = dkv[:, pl.ds(pl.multiple_of(zi * tl, tl), tl)]
    for o in range(1, nz):
        dev, _ = at_z(at, nz - o, nz)
        landed(kvin.at[o - 1], r_kv.at[o - 1], dev)
        acc = acc + kvin[o - 1].astype(F32)
    dk = rot_rows(acc[:hd], cos_ref[...], -sin_ref[...])
    dqkv[:, qc:] = jnp.transpose(jnp.concatenate([dk, acc[hd:]], axis=0)).astype(BF)
    weight_grad(gkb, qc, qc + 2 * hd)
    for o in far_first:
        mk.stage1(o)
    red = QuadSum(at, log, part, cin, xin, total, s_p, r_p, cw)
    w = wqkv[...].reshape(d, qc + 2 * hd)
    nc = d // cw
    for n in range(nc):
        part[:, :, :, n * cw:(n + 1) * cw] = nt(dqkv[...], w[n * cw:(n + 1) * cw]).astype(BF).reshape(2, 2, rows, cw)
        red.start(n)
        if n:
            red.middle(n - 1)
    for o in far_first:
        mq.stage2(o)
    red.middle(nc - 1)
    for o in far_first:
        mk.stage2(o)
    for o in far_first:
        mq.stage3(o)
    for o in far_first:
        mk.stage3(o)
    gsend[...] = mo.result().astype(BF)

    @pl.when(source != lin)
    def _():
        pltpu.make_async_remote_copy(gsend, ogot, s_od, r_od, device_id=device_of(source, nz), device_id_type=MESH).start()

    @pl.when(source == lin)
    def _():
        ogot[...] = gsend[...]

    for n in range(nc):
        red.finish(n)
    x = tok_ref[...].astype(F32)
    inv1 = lax.rsqrt(jnp.mean(x * x, axis=1, keepdims=True) + NORM_EPS)
    xh = x * inv1
    dy1 = total[...]
    dx_out[...] = dx_out[...] + inv1 * (dy1 - xh * jnp.mean(dy1 * xh, axis=1, keepdims=True))
    gain_out[...] = gs.take(4)
    for merge, dst, sp, ss, rs, lo, hi in ((mq, gq_out, gpart.at[:, :qc], s_gq, r_gq, 0, qc), (mk, gkv_out, gpart.at[:, qc:], s_gk, r_gk, qc, qc + 2 * hd)):
        gpart[:, lo:hi] = merge.result().astype(BF)
        dst[t] = gpart[pl.ds(pl.multiple_of(t * wr, wr), wr), lo:hi]
        for k, f in enumerate(quad):
            dev = other(at, *f)
            tt = dev[4] * 2 + dev[5]
            log.push(gpart.at[pl.ds(pl.multiple_of(tt * wr, wr), wr), lo:hi], dst.at[t], ss.at[k], rs.at[k], dev)
    @pl.when(target != lin)
    def _():
        pltpu.make_async_remote_copy(gsend, ogot, s_od, r_od, device_id=device_of(target, nz), device_id_type=MESH).wait_recv()

    gwo_out[...] = ogot[...].astype(F32)
    for dst, rs in ((gq_out, r_gq), (gkv_out, r_gk)):
        for k, f in enumerate(quad):
            dev = other(at, *f)
            tt = dev[4] * 2 + dev[5]
            landed(dst.at[tt], rs.at[k], dev)
    for sw_ in swaps:
        sw_.finish()

    @pl.when(source != lin)
    def _():
        pltpu.make_async_remote_copy(gsend, ogot, s_od, r_od, device_id=device_of(source, nz), device_id_type=MESH).wait_send()

    sb.close()
    log.close()


def back(nz, ndp, m, dn2, gain, cot, tokens, cosT, sinT, starts, xg, wqkv, wo, q, kv, o, lse, down, grads):
    rows, d = m.shape
    hd = HEAD_DIM
    qc = GROUP * hd
    nrest = nz * ndp // 4
    wr = wo.shape[2]
    keys = nz * 4 * rows
    tl = 4 * rows
    units = grads[0].shape[0] // nrest
    vm = pl.BlockSpec(memory_space=pltpu.VMEM)
    hbm = pl.BlockSpec(memory_space=pl.ANY)
    dma = pltpu.SemaphoreType.DMA
    sd = jax.ShapeDtypeStruct
    nf = max(nrest - 1, 1)
    outs = (sd((rows, d), F32), sd((rows, d), BF), sd((4, wr, qc), BF), sd((4, wr, 2 * hd), BF), sd((wr, d), F32), sd((16, 128), F32)) + (
        sd((nrest - 1, units, d), BF),) * 2
    V = pltpu.VMEM

    def merge_bufs(r, c):
        return [V((ndp, nz, r, c), BF), V((nrest, 2, r, c), BF), V((nrest, r, c), BF), V((nf, r, c), BF)]

    return pl.pallas_call(
        functools.partial(back_kernel, nz, ndp),
        out_shape=outs,
        in_specs=[vm] * 8 + [hbm] * 10,
        out_specs=(vm,) * 6 + (hbm,) * 2,
        scratch_shapes=[
            V(xg.shape, BF), V(wqkv.shape, BF), V(wo.shape, BF), V(q.shape, BF), V(kv.shape, BF), V(o.shape, BF), V(lse.shape, F32),
            V((2, 2, rows, d), BF), V(q.shape, BF), V(lse.shape, F32), V((keys, hd), BF), V((keys, hd), BF), V((hd, keys), BF),
            V((keys, tl), F32), V((2 * hd, keys), F32), V((qc, tl), F32), V(kv.shape, BF), V((max(nz - 1, 1), 2 * hd, tl), BF),
            V((tl, qc + 2 * hd), BF)]
        + merge_bufs(wr, d) + merge_bufs(4 * wr, qc) + merge_bufs(4 * wr, 2 * hd) + [
            V((wr, d), BF), V((4 * wr, qc + 2 * hd), BF), V((2, 2, rows, d), BF), V((2, rows, d), BF), V((rows, d), BF), V((rows, d), F32),
            V((wr, d), BF), V((5, 16, 128), F32), V((4 + nf, 16, 128), F32),
            V(down.shape, BF), V((2, 2, rows, d), BF), V((2, rows, d), BF), V((rows, d), BF),
            dma((8,)), dma((3,)), dma((3,))] + [dma((nf,)), dma((nf,)), dma((nrest, 6)), dma((nrest, 6))] * 3 + [
            dma((nz,)), dma((nz,)), dma((2, 4)), dma((2, 4)), dma((2, nrest)), dma((2, nrest)), dma, dma, dma((3,)), dma((3,)), dma((3,)), dma((3,)),
            dma((4 + nf,)), dma((4 + nf,)), dma((3, 4)), dma((3, 4))],
        compiler_params=pltpu.CompilerParams(collective_id=3, has_side_effects=True, vmem_limit_bytes=62 * 2**20),
        name="backward",
    )(m, dn2, gain, cot, tokens, cosT, sinT, starts, xg, wqkv, wo, q, kv, o, lse, down, *grads)


def local(tokens, gain_attn, w_query, w_key, w_value, w_out, gain_mlp, w_gate_t, w_up_t, w_down, doc_ids, cotangent, nz, ndp):
    rows, d = tokens.shape
    wr = w_query.shape[0]
    grows = rows * 4
    seq_ids = doc_ids[0]
    length = seq_ids.shape[0]
    zi = lax.axis_index(Z)
    hd = HEAD_DIM
    qc = GROUP * hd
    ga = gain_attn.astype(F32)[:, None]
    wall = jnp.concatenate([w_query.reshape(wr, 4, qc), w_key.reshape(wr, 4, hd), w_value.reshape(wr, 4, hd)], axis=2).transpose(1, 0, 2)
    wpack = (wall.astype(F32) * ga[None]).astype(BF)
    gpack = gain_mlp[None]
    first = zi * grows
    own_ids = lax.dynamic_slice_in_dim(seq_ids, first, grows, 0)
    qpos = first + jnp.arange(grows, dtype=jnp.int32)
    starts = jnp.sum((seq_ids[:, None] < own_ids[None, :]).astype(jnp.int32), axis=0)
    freq = 10000.0 ** (-jnp.arange(hd // 2, dtype=F32) / (hd // 2))
    ph = (qpos - starts).astype(F32)[None, :] * freq[:, None]
    cosT, sinT = jnp.cos(ph), jnp.sin(ph)
    units = w_down.shape[0]
    fill = -units % 16
    if fill:
        w_gate_t, w_up_t, w_down = (jnp.pad(w, ((0, fill), (0, 0))) for w in (w_gate_t, w_up_t, w_down))
    m, q, kv, o, lse, xg, wqkv, wo, gains, cot_all, wgt, wut = attn(
        nz, ndp, tokens, wpack, w_out, gpack, cosT, sinT, starts[None], cotangent, w_gate_t, w_up_t)
    gm = gains[:, :, :, 0, :wr].reshape(1, d).astype(F32)
    down, dn2, gwd, gwg, gwu, fd = mlp(nz * ndp // 4, m, gm, cot_all, (w_gate_t, w_up_t, w_down), (wgt, wut))
    dx, block_out, gq, gkv, gwo, gsum, fg, fu = back(
        nz, ndp, m, dn2, gm, cotangent, tokens, cosT, sinT, starts[None], xg, wqkv, wo, q, kv, o, lse, down, (gwg, gwu))

    def own(a, far):
        return (a[:units + fill].astype(F32) + jnp.sum(far.astype(F32), axis=0))[:units]

    gw = jnp.concatenate([gq, gkv], axis=2).astype(F32)
    gga = jnp.sum(gw * wall.astype(F32), axis=(0, 2))
    gw = (gw * ga[None]).transpose(1, 0, 2)
    gwq = gw[:, :, :qc].reshape(wr, 4 * qc)
    gwk = gw[:, :, qc:qc + hd].reshape(wr, 4 * hd)
    gwv = gw[:, :, qc + hd:].reshape(wr, 4 * hd)
    ggm = lax.dynamic_slice_in_dim(gsum.reshape(d), lax.axis_index(AXES) * wr, wr, 0)
    return block_out, dx, gga, gwq, gwk, gwv, gwo, ggm, own(gwg, fg), own(gwu, fu), own(gwd, fd)


def solution(mesh):
    dp, seq = mesh.shape["dp"], mesh.shape["seq"]
    m6 = Mesh(mesh.devices.reshape(dp // 2, 2, seq // 8, 2, 2, 2), AXES)
    row = P(AXES, None)
    vec = P(AXES)
    col = P(None, AXES)
    inner = jax.shard_map(
        functools.partial(local, nz=seq // 4, ndp=dp), mesh=m6,
        in_specs=(row, vec, row, row, row, row, vec, row, row, row, P(DP, None), row),
        out_specs=(row, row, vec, row, row, row, row, vec, row, row, row),
        check_vma=False,
    )

    def run(tokens, gain_attn, w_query, w_key, w_value, w_out, gain_mlp, w_gate, w_up, w_down, doc_ids, cotangent):
        outs = inner(tokens, gain_attn, w_query, w_key, w_value, w_out, gain_mlp, w_gate.T, w_up.T, w_down, doc_ids, cotangent)
        return outs[:8] + (outs[8].T, outs[9].T, outs[10])

    return run
```
